512 devices in a mesh: dp: 64 (over x, y, core), proto: 8 (over z).
Axes of the slice: x: 4, y: 8, z: 8, core: 2. Of those that a mesh axis runs over, the one named last changes fastest.
Arguments:
- teacher_feats: bfloat16 [8192, 256], P('dp'), may hold values from -3 to 3
- student_feats: bfloat16 [8192, 256], P('dp'), may hold values from -0.375 to 0.375
- prototypes: bfloat16 [256, 32768], P(None, 'proto'), may hold values from -3 to 3
Outputs:
- grad_features: float32 [8192, 256], P('dp')
- grad_prototypes: float32 [256, 32768], P('dp', 'proto')
The draws below stay inside these ranges and needn't reach their ends.
All inputs are finite; a program needn't handle non-finite values.
Results may differ from the reference program's by a relative error of at most 0.0039.
Values sent between devices are 32-bit elements; how exact they have to be, the bound alone decides.
A program may use at most 64 MiB of HBM per device.

```python
import jax
import jax.numpy as jnp
from jax import lax

D = 256
PROTOS = 32768
CROP_DEV = 128
ITERS = 3
CROPS = 8192


def shared_axes(key):
    return jax.random.truncated_normal(key, -4.0, 4.0, (3, D), jnp.float32) * D ** (-0.5)


def combine_parts(weights, axes, noise):
    total = noise
    for index in range(3):
        total = total + weights[:, index:index + 1] * axes[index][None, :]
    return jnp.clip(total, -3.0, 3.0)


def crop_offsets(key):
    block_count = CROPS // CROP_DEV
    position = (jnp.arange(CROPS, dtype=jnp.float32) + 0.5) * (2.0 / CROPS) - 1.0
    direction = jnp.array([0.7, -0.5, 0.4], jnp.float32)
    block_shift = jax.random.uniform(key, (block_count, 3), jnp.float32, -0.5, 0.5)
    per_crop = jnp.repeat(block_shift, CROP_DEV, axis=0, total_repeat_length=CROPS)
    return position[:, None] * direction[None, :] + per_crop


def draw_teacher_feats(key, part):
    axes = shared_axes(key)
    key = jax.random.fold_in(key, 11)
    coef_key, noise_key, shift_key = jax.random.split(key, 3)
    weights = jax.random.uniform(coef_key, (CROPS, 3), jnp.float32, -1.0, 1.0)
    weights = weights + crop_offsets(shift_key)
    noise = 1.5 * jax.random.truncated_normal(noise_key, -4.0, 4.0, (CROPS, D), jnp.float32)
    noise = noise * D ** (-0.5)
    return combine_parts(weights, axes, noise).astype(jnp.bfloat16)


def draw_prototypes(key, part):
    axes = shared_axes(key)
    key = jax.random.fold_in(key, 12)
    coef_key, noise_key = jax.random.split(key)
    weights = jax.random.uniform(coef_key, (PROTOS, 3), jnp.float32, -1.0, 1.0)
    noise = 1.5 * jax.random.truncated_normal(noise_key, -4.0, 4.0, (PROTOS, D), jnp.float32)
    noise = noise * D ** (-0.5)
    return combine_parts(weights, axes, noise).T.astype(jnp.bfloat16)


def steps_of(rng, shape, cuts, least, high):
    gain, own = 1.0, jax.random.fold_in(rng, 6)
    for dim, blocks in cuts:
        draws = jnp.exp(jax.random.uniform(jax.random.fold_in(own, dim), (blocks,), jnp.float32, least / len(cuts), high / len(cuts)))
        gain = gain * jnp.repeat(draws, shape[dim] // blocks).reshape([-1 if axis == dim else 1 for axis in range(len(shape))])
    return gain


def gaussian(own_key, extent, deviation, bound, cuts=(), held_as=jnp.bfloat16):
    result = deviation * jax.random.normal(own_key, extent, jnp.float32)
    if cuts:
        result = result * steps_of(own_key, extent, cuts, -0.22, 0.18)
    return jnp.clip(result, -bound, bound).astype(held_as)


def setup_inputs(seed: int = 0) -> dict:
    key_of = jax.random.split(jax.random.key(seed), 4)
    return {
        "teacher_feats": draw_teacher_feats(jax.random.fold_in(key_of[3], 71), 0),
        "student_feats": gaussian(key_of[1], (CROPS, D), 0.0625, 0.375, ((0, 64),)),
        "prototypes": draw_prototypes(jax.random.fold_in(key_of[3], 71), 0),
    }


EPS = 1e-06
TEMP_T = 0.07
TEMP_S = 0.1

def unit_columns(weights):
    widened = weights.astype(jnp.float32)
    return (widened * lax.rsqrt(lax.optimization_barrier(jnp.sum(widened * widened, 0, keepdims=True)) + EPS)).astype(jnp.bfloat16)

def unit_rows(features):
    widened = features.astype(jnp.float32)
    inverse = lax.rsqrt(lax.optimization_barrier(jnp.sum(widened * widened, 1, keepdims=True)) + EPS)
    return ((widened * inverse).astype(jnp.bfloat16), inverse)

def reference(teacher_feats, student_feats, prototypes):
    unit_proto = unit_columns(prototypes)
    teacher_unit, _ = unit_rows(teacher_feats)
    student_unit, student_inv = unit_rows(student_feats)
    width = min(PROTOS, 4096)
    blocks = unit_proto.reshape(D, PROTOS // width, width).transpose(1, 0, 2)

    def teacher_block(block):
        return jnp.exp(jnp.dot(teacher_unit, block, preferred_element_type=jnp.float32) / TEMP_T)

    def student_block(block):
        return jnp.exp(jnp.dot(student_unit, block, preferred_element_type=jnp.float32) / TEMP_S)

    def student_sum(block):
        return lax.optimization_barrier(jnp.sum(student_block(block), 1))
    student_total = lax.optimization_barrier(jnp.sum(lax.map(student_sum, blocks), 0))
    row_scale = jnp.ones((CROPS,), jnp.float32)
    col_scale = jnp.ones((PROTOS // width, width), jnp.float32)
    for iteration in range(ITERS):

        def sweep(block):
            exp_block = teacher_block(block)
            inverse = 1.0 / jnp.dot(row_scale, exp_block, precision=lax.Precision.HIGHEST)
            return (inverse, jnp.dot(exp_block, inverse, precision=lax.Precision.HIGHEST))
        col_scale, partial_rows = lax.map(sweep, blocks)
        row_scale = 1.0 / lax.optimization_barrier(jnp.sum(partial_rows, 0))

    def finish(grad_feature, inputs):
        block, scales = inputs
        targets = teacher_block(block) * scales[None, :] * row_scale[:, None]
        probs = student_block(block) / student_total[:, None]
        grad_logit = (PROTOS / 64.0 * (probs - targets) / TEMP_S).astype(jnp.bfloat16)
        grad_block = lax.dot_general(student_unit, grad_logit, (((0,), (0,)), ((), ())), preferred_element_type=jnp.float32)
        grad_feature = grad_feature + lax.dot_general(grad_logit, block, (((1,), (1,)), ((), ())), preferred_element_type=jnp.float32)
        return (grad_feature, grad_block)
    grad_unit, grad_blocks = lax.scan(finish, jnp.zeros((CROPS, D), jnp.float32), (blocks, col_scale))
    grad_prototypes = grad_blocks.transpose(1, 0, 2).reshape(D, PROTOS)
    unit_wide = student_unit.astype(jnp.float32)
    projected = lax.optimization_barrier(jnp.sum(unit_wide * grad_unit, 1, keepdims=True))
    grad_features = (grad_unit - unit_wide * projected) * student_inv
    return (grad_features, grad_prototypes)
```

```python
import functools

import jax
import jax.numpy as jnp
from jax import lax
from jax.experimental import pallas as pl
from jax.experimental.pallas import tpu as pltpu
from jax.sharding import PartitionSpec as P

EPS = 1e-06
INV_T = 1.0 / 0.07
INV_S = 1.0 / 0.1
ITERS = 3
NX, NY, NC, NZ = 4, 8, 2, 8
B = 128
D = 256
K = 4096
CH = K // 256
TL = K // 128
KB = K // (NX * NC)
SCALE = 32768 / 64.0 / 0.1
MESH = pl.DeviceIdType.MESH

UP, XX, YY, DN, ZZ = (0, 3, 6, 9, 12)
G1, G2, TT, RR, GP, ZR, ZA = range(15, 22)
GROUPS = 22


def dot(a, b):
    return jnp.dot(a, b, preferred_element_type=jnp.float32)


def unit_rows(raw):
    wide = raw.astype(jnp.float32)
    inv = lax.rsqrt(jnp.sum(wide * wide, 1, keepdims=True) + EPS)
    return (wide * inv).astype(jnp.bfloat16), inv


def body(
    t_ref, s_ref, w_ref, gf_out, gp_out,
    WU, E, SE, F, ETB, ESB, SBT, GB, GPS, GPR, GFS, GFR, GFO, GFA,
    CS, CR, XS, XR, YS, YR, CF, ZS, ZRV, TS, RB, ITB, RW, ITW, ssem, rsem,
):
    dp = lax.axis_index("dp")
    z = lax.axis_index("proto")
    c = lax.rem(dp, 2)
    y = lax.rem(dp // 2, NY)
    x = dp // (2 * NY)

    def dev(dx, dy, dc, dz):
        return (
            (lax.rem(x + dx, NX) * NY + lax.rem(y + dy, NY)) * NC + lax.rem(c + dc, NC),
            lax.rem(z + dz, NZ),
        )

    mate = dev(0, 0, 1, 0)

    def send(src, dst, group, to):
        pltpu.make_async_remote_copy(
            src, dst, ssem.at[group], rsem.at[group], device_id=to, device_id_type=MESH
        ).start()

    def arrived(ref, group):
        pltpu.make_async_remote_copy(
            ref, ref, ssem.at[group], rsem.at[group], device_id=mate, device_id_type=MESH
        ).wait_recv()

    def sent(ref, group):
        pltpu.make_async_remote_copy(
            ref, ref, ssem.at[group], rsem.at[group], device_id=mate, device_id_type=MESH
        ).wait_send()

    barrier = pltpu.get_barrier_semaphore()

    def greet(i, carry):
        to = dev(i // (NY * NC), lax.rem(i // NC, NY), lax.rem(i, NC), 0)
        pl.semaphore_signal(barrier, inc=1, device_id=to, device_id_type=MESH)
        return carry

    lax.fori_loop(1, NX * NY * NC, greet, 0)
    for k in range(1, NZ):
        pl.semaphore_signal(barrier, inc=1, device_id=dev(0, 0, 0, k), device_id_type=MESH)

    t_unit, _ = unit_rows(t_ref[...])
    s_unit, _ = unit_rows(s_ref[...])
    F[0, :B, :] = t_unit.astype(jnp.float32)
    F[0, B:, :] = s_unit.astype(jnp.float32)

    def first(j, carry):
        w = w_ref[:, pl.ds(pl.multiple_of(j * 256, 256), 256)].astype(jnp.float32)
        w = (w * lax.rsqrt(jnp.sum(w * w, 0, keepdims=True) + EPS)).astype(jnp.bfloat16)
        WU[j] = w
        e = jnp.exp(dot(t_unit, w) * INV_T)
        E[2 * j] = e[:, :128]
        E[2 * j + 1] = e[:, 128:]
        CS[0, pl.ds(2 * j, 1), :] = jnp.sum(e[:, :128], 0, keepdims=True)
        CS[0, pl.ds(2 * j + 1, 1), :] = jnp.sum(e[:, 128:], 0, keepdims=True)
        return carry

    lax.fori_loop(0, CH, first, 0, unroll=2)
    pl.semaphore_wait(barrier, NX * NY * NC - 1 + NZ - 1)

    def student():
        def step(j, acc):
            e = jnp.exp(dot(s_unit, WU[j]) * INV_S)
            SE[2 * j] = e[:, :128]
            SE[2 * j + 1] = e[:, 128:]
            return acc + e[:, :128] + e[:, 128:]

        acc = lax.fori_loop(0, CH, step, jnp.zeros((B, 128), jnp.float32), unroll=2)
        return jnp.sum(acc.T, 0, keepdims=True)

    def gather_x():
        for k in range(1, NX):
            send(F.at[0], F.at[k], G1, dev(k, 0, 0, 0))

    def line_block(j, carry):
        tb = F[j, :B, :].astype(jnp.bfloat16)
        sw = F[j, B:, :]
        sb = sw.astype(jnp.bfloat16)
        SBT[j] = sw.T.astype(jnp.bfloat16)
        own = (x * NC + c) * (KB // 256)
        for h in range(KB // 256):
            w = WU[own + h]
            ETB[j, h] = jnp.exp(dot(tb, w) * INV_T)
            ESB[j, h] = jnp.exp(dot(sb, w) * INV_S)
        return carry

    def columns(i):
        @pl.when(c == 0)
        def _():
            send(CS.at[i], CR.at[i], UP + i, mate)

        if i == 0:
            total = student()
            ZS[0, 1:2, :] = total

        @pl.when(c == 1)
        def _():
            arrived(CR.at[i], UP + i)
            XS[i] = CS[i] + CR[i]
            for k in range(1, NX):
                send(XS.at[i], XR.at[i, k - 1], XX + i, dev(k, 0, 0, 0))
            arrived(XR.at[i], XX + i)
            YS[i] = (XS[i] + XR[i, 0]) + (XR[i, 1] + XR[i, 2])
            for k in range(1, NY):
                send(YS.at[i], YR.at[i, k - 1], YY + i, dev(0, k, 0, 0))
            if i == 0:
                gather_x()

        if i == 1:
            arrived(F.at[pl.ds(1, NX - 1)], G1)
            send(F.at[pl.ds(0, NX)], F.at[pl.ds(NX, NX)], G2, mate)
            lax.fori_loop(0, NX, line_block, 0)
        if i == 2:
            arrived(F.at[pl.ds(NX, NX)], G2)
            lax.fori_loop(NX, 2 * NX, line_block, 0)
            arrived(TS.at[pl.ds(1, 7)], TT)
            for j in range(2 * NX):
                ITB[j] = jnp.broadcast_to(TS[j] * SCALE, (128, B)).T

        @pl.when(c == 1)
        def _():
            arrived(YR.at[i], YY + i)
            total = YS[i]
            for k in range(NY - 1):
                total = total + YR[i, k]
            CF[i] = 1.0 / total
            send(CF.at[i], CF.at[i], DN + i, mate)

        @pl.when(c == 0)
        def _():
            arrived(CF.at[i], DN + i)
            if i == 0:
                gather_x()

    def rows(i):
        def step(t, acc):
            return acc + E[t] * CF[i, pl.ds(t, 1), :]

        acc = lax.fori_loop(0, TL, step, jnp.zeros((B, 128), jnp.float32), unroll=4)
        ZS[i, 0:1, :] = jnp.sum(acc.T, 0, keepdims=True)
        for k in range(1, NZ):
            send(ZS.at[i], ZRV.at[i, k - 1], ZZ + i, dev(0, 0, 0, k))
        arrived(ZRV.at[i], ZZ + i)
        total = ZS[i]
        for k in range(NZ - 1):
            total = total + ZRV[i, k]
        return 1.0 / total

    def spread(ref, group):
        for k in range(1, 2 * NX):
            send(ref.at[0], ref.at[k], group, dev(k % NX, 0, k // NX, 0))

    for i in range(ITERS):
        columns(i)
        if i == 0:
            ZS[1] = jnp.zeros((2, 128), jnp.float32)
            ZS[2] = jnp.zeros((2, 128), jnp.float32)
        inv = rows(i)
        if i == 0:
            TS[0] = inv[1:2, :]
            spread(TS, TT)
            ITW[...] = jnp.broadcast_to(inv[1:2, :] * SCALE, (128, B)).T
        if i < ITERS - 1:
            RW[...] = jnp.broadcast_to(inv[0:1, :], (128, B)).T

            def scaled(t, carry):
                CS[i + 1, pl.ds(t, 1), :] = jnp.sum(E[t] * RW[...], 0, keepdims=True)
                return carry

            lax.fori_loop(0, TL, scaled, 0, unroll=4)
        else:
            RB[0] = inv[0:1, :]
            spread(RB, RR)
            RW[...] = jnp.broadcast_to(inv[0:1, :] * SCALE, (128, B)).T

    last = ITERS - 1

    def feature(j, acc):
        g = [
            (SE[2 * j + h] * ITW[...] - (E[2 * j + h] * CF[last, pl.ds(2 * j + h, 1), :]) * RW[...]).astype(jnp.bfloat16)
            for h in range(2)
        ]
        return acc + lax.dot_general(
            jnp.concatenate(g, 1), WU[j], (((1,), (1,)), ((), ())), preferred_element_type=jnp.float32
        )

    GFA[...] = lax.fori_loop(0, CH, feature, jnp.zeros((B, D), jnp.float32), unroll=2)
    for k in range(NZ):
        GFS[k] = GFA[16 * k:16 * k + 16, :]
    for k in range(1, NZ):
        send(GFS.at[lax.rem(z + k, NZ)], GFR.at[k - 1], ZR, dev(0, 0, 0, k))

    arrived(RB.at[pl.ds(1, 7)], RR)
    first_tile = (x * NC + c) * (KB // 128)

    def line_grad(j, carry):
        rb = jnp.broadcast_to(RB[j] * SCALE, (128, B)).T
        for q in range(KB // 128):
            h, part = q // 2, pl.ds(128 * (q % 2), 128)
            col = CF[last, pl.ds(first_tile + q, 1), :]
            g = ESB[j, h, :, part] * ITB[j] - (ETB[j, h, :, part] * col) * rb
            GB[j, :, 128 * q:128 * q + 128] = g.astype(jnp.bfloat16)
        return carry

    lax.fori_loop(0, 2 * NX, line_grad, 0)
    for h in range(KB // 256):
        acc = jnp.zeros((D, 256), jnp.float32)
        for p in range(NX):
            lhs = jnp.concatenate([SBT[2 * p], SBT[2 * p + 1]], 1)
            rhs = jnp.concatenate(
                [GB[2 * p, :, 256 * h:256 * h + 256], GB[2 * p + 1, :, 256 * h:256 * h + 256]], 0
            )
            acc = acc + dot(lhs, rhs)
        GPS[:, :, 256 * h:256 * h + 256] = acc.reshape(D // 4, 4, 256)

    def scatter(i, carry):
        to = dev(i // (NY * NC), lax.rem(i // NC, NY), lax.rem(i, NC), 0)
        send(GPS.at[to[0]], GPR.at[i], GP, to)
        return carry

    lax.fori_loop(1, NX * NY * NC, scatter, 0)

    arrived(GFR, ZR)
    mine = pl.ds(pl.multiple_of(z * 16, 16), 16)
    u, inv = unit_rows(s_ref[mine, :])
    u = u.astype(jnp.float32)
    total = GFS[z]
    for k in range(NZ - 1):
        total = total + GFR[k]
    GFO[0] = (total - u * jnp.sum(u * total, 1, keepdims=True)) * inv
    for k in range(1, NZ):
        send(GFO.at[0], GFO.at[k], ZA, dev(0, 0, 0, k))
    gf_out[mine, :] = GFO[0]

    arrived(GPR.at[pl.ds(1, NX * NY * NC - 1)], GP)
    GPR[0] = GPS[dp]
    for dx in range(NX):
        for dc in range(NC):
            total = GPR[dx * NY * NC + dc]
            for dy in range(1, NY):
                total = total + GPR[(dx * NY + dy) * NC + dc]
            at = (lax.rem(x + NX - dx, NX) * NC + lax.rem(c + dc, NC)) * KB
            gp_out[:, pl.ds(pl.multiple_of(at, KB), KB)] = total

    arrived(GFO.at[pl.ds(1, NZ - 1)], ZA)
    for k in range(1, NZ):
        at = lax.rem(z + NZ - k, NZ) * 16
        gf_out[pl.ds(pl.multiple_of(at, 16), 16), :] = GFO[k]

    for i in range(ITERS):
        @pl.when(c == 0)
        def _():
            sent(CS.at[i], UP + i)

        @pl.when(c == 1)
        def _():
            sent(XR.at[i], XX + i)
            sent(YR.at[i], YY + i)
            sent(CF.at[i], DN + i)

        sent(ZRV.at[i], ZZ + i)
    sent(F.at[pl.ds(1, NX - 1)], G1)
    sent(F.at[pl.ds(0, NX)], G2)
    sent(TS.at[pl.ds(1, 7)], TT)
    sent(RB.at[pl.ds(1, 7)], RR)
    sent(GPR.at[pl.ds(1, NX * NY * NC - 1)], GP)
    sent(GFR, ZR)
    sent(GFO.at[pl.ds(1, NZ - 1)], ZA)


def shards(teacher, student, protos):
    f32, bf16 = jnp.float32, jnp.bfloat16
    vm = pltpu.VMEM
    scratch = [
        vm((CH, D, 256), bf16),
        vm((TL, B, 128), f32),
        vm((TL, B, 128), f32),
        vm((2 * NX, 2 * B, D), f32),
        vm((2 * NX, KB // 256, B, 256), f32),
        vm((2 * NX, KB // 256, B, 256), f32),
        vm((2 * NX, D, B), bf16),
        vm((2 * NX, B, KB), bf16),
        vm((64, 4, KB), f32),
        vm((64, 4, KB), f32),
        vm((NZ, 16, D), f32),
        vm((NZ - 1, 16, D), f32),
        vm((NZ, 16, D), f32),
        vm((B, D), f32),
        vm((ITERS, TL, 128), f32),
        vm((ITERS, TL, 128), f32),
        vm((ITERS, TL, 128), f32),
        vm((ITERS, NX - 1, TL, 128), f32),
        vm((ITERS, TL, 128), f32),
        vm((ITERS, NY - 1, TL, 128), f32),
        vm((ITERS, TL, 128), f32),
        vm((ITERS, 2, 128), f32),
        vm((ITERS, NZ - 1, 2, 128), f32),
        vm((2 * NX, 1, 128), f32),
        vm((2 * NX, 1, 128), f32),
        vm((2 * NX, B, 128), f32),
        vm((B, 128), f32),
        vm((B, 128), f32),
        pltpu.SemaphoreType.DMA((GROUPS,)),
        pltpu.SemaphoreType.DMA((GROUPS,)),
    ]
    whole = pl.BlockSpec(memory_space=pltpu.VMEM)
    return pl.pallas_call(
        body,
        out_shape=(jax.ShapeDtypeStruct((B, D), f32), jax.ShapeDtypeStruct((4, K), f32)),
        in_specs=[whole] * 3,
        out_specs=(whole, whole),
        scratch_shapes=scratch,
        compiler_params=pltpu.CompilerParams(
            collective_id=0, has_side_effects=True, vmem_limit_bytes=48 * 2**20
        ),
    )(teacher, student, protos)


def solution(mesh):
    placed = (P("dp", None), P("dp", None), P(None, "proto"))
    return jax.shard_map(
        shards,
        mesh=mesh,
        in_specs=placed,
        out_specs=(P("dp", None), P("dp", "proto")),
        check_vma=False,
    )
```

```python
import functools

import jax
import jax.numpy as jnp
from jax import lax
from jax.experimental import pallas as pl
from jax.experimental.pallas import tpu as pltpu
from jax.sharding import PartitionSpec as P

EPS = 1e-06
INV_T = 1.0 / 0.07
INV_S = 1.0 / 0.1
ITERS = 3
NX, NY, NC, NZ = 4, 8, 2, 8
B = 128
D = 256
K = 4096
CH = K // 256
TL = K // 128
KB = K // (NX * NC)
SCALE = 32768 / 64.0 / 0.1
MESH = pl.DeviceIdType.MESH

UP, DN, G0, G1, G2, TZ, T1, T2, RM, GP, ZR, ZA = range(12)
XX, YY, ZZ = (12, 15, 18)
GROUPS = 21
LOADS = 4


def dot(a, b):
    return jnp.dot(a, b, preferred_element_type=jnp.float32)


def unit_rows(raw):
    wide = raw.astype(jnp.float32)
    inv = lax.rsqrt(jnp.sum(wide * wide, 1, keepdims=True) + EPS)
    return (wide * inv).astype(jnp.bfloat16), inv


def across(row):
    return jnp.broadcast_to(row, (128, 128)).T


def body(
    t_hbm, s_hbm, w_hbm, gf_out, gp_out,
    t_ref, s_ref, w_ref, WU, E, SE, F, ETB, ESB, SBT, GB, GPS, GPR, GFS, GFR, GFO, GFA,
    CS, CR, XS, XR, YS, YR, CF, ZS, ZRV, ZL, TZS, TZR, TS, RB, RBM, ITB, RW, ITW, lsem, ssem, rsem,
):
    dp = lax.axis_index("dp")
    z = lax.axis_index("proto")
    c = lax.rem(dp, 2)
    y = lax.rem(dp // 2, NY)
    x = dp // (2 * NY)

    def dev(dx, dy, dc, dz):
        return (
            (lax.rem(x + dx, NX) * NY + lax.rem(y + dy, NY)) * NC + lax.rem(c + dc, NC),
            lax.rem(z + dz, NZ),
        )

    mate = dev(0, 0, 1, 0)

    def send(src, dst, group, to):
        pltpu.make_async_remote_copy(
            src, dst, ssem.at[group], rsem.at[group], device_id=to, device_id_type=MESH
        ).start()

    def arrived(ref, group):
        pltpu.make_async_remote_copy(
            ref, ref, ssem.at[group], rsem.at[group], device_id=mate, device_id_type=MESH
        ).wait_recv()

    def sent(ref, group):
        pltpu.make_async_remote_copy(
            ref, ref, ssem.at[group], rsem.at[group], device_id=mate, device_id_type=MESH
        ).wait_send()

    loads = [
        pltpu.make_async_copy(t_hbm, t_ref, lsem.at[0]),
        pltpu.make_async_copy(s_hbm, s_ref, lsem.at[1]),
    ]
    for piece in range(LOADS):
        cols = pl.ds(piece * (K // LOADS), K // LOADS)
        loads.append(pltpu.make_async_copy(w_hbm.at[:, cols], w_ref.at[:, cols], lsem.at[2 + piece]))
    for load in loads:
        load.start()

    peers = [dev(0, 0, 1, 0)]
    peers += [dev(k, 0, 0, 0) for k in range(1, NX)]
    peers += [dev(0, k, 0, 0) for k in range(1, NY)]
    peers += [dev(0, 0, 0, k) for k in range(1, NZ)]
    barrier = pltpu.get_barrier_semaphore()
    for to in peers:
        pl.semaphore_signal(barrier, inc=1, device_id=to, device_id_type=MESH)

    loads[0].wait()
    t_unit, _ = unit_rows(t_ref[...])
    F[0, :B, :] = t_unit.astype(jnp.float32)

    def first(j, carry):
        w = w_ref[:, pl.ds(pl.multiple_of(j * 256, 256), 256)].astype(jnp.float32)
        w = (w * lax.rsqrt(jnp.sum(w * w, 0, keepdims=True) + EPS)).astype(jnp.bfloat16)
        WU[j] = w
        e = jnp.exp(dot(t_unit, w) * INV_T)
        E[2 * j, :B] = e[:, :128]
        E[2 * j + 1, :B] = e[:, 128:]
        CS[pl.ds(2 * j, 1), :] = jnp.sum(e[:, :128], 0, keepdims=True)
        CS[pl.ds(2 * j + 1, 1), :] = jnp.sum(e[:, 128:], 0, keepdims=True)
        return carry

    per = CH // LOADS
    for piece in range(LOADS):
        loads[2 + piece].wait()
        lax.fori_loop(piece * per, piece * per + per, first, 0, unroll=True)
    loads[1].wait()
    s_unit, _ = unit_rows(s_ref[...])
    F[0, B:, :] = s_unit.astype(jnp.float32)
    pl.semaphore_wait(barrier, len(peers))

    def student():
        def step(j, acc):
            e = jnp.exp(dot(F[0, B:, :].astype(jnp.bfloat16), WU[j]) * INV_S)
            SE[2 * j] = e[:, :128]
            SE[2 * j + 1] = e[:, 128:]
            return acc + e[:, :128] + e[:, 128:]

        acc = lax.fori_loop(0, CH, step, jnp.zeros((B, 128), jnp.float32), unroll=4)
        TZS[...] = jnp.sum(acc.T, 0, keepdims=True)
        for k in range(1, NZ):
            send(TZS, TZR.at[k - 1], TZ, dev(0, 0, 0, k))

    def student_totals():
        arrived(TZR, TZ)
        total = TZS[...]
        for k in range(NZ - 1):
            total = total + TZR[k]
        TS[0] = SCALE / total
        ITW[...] = across(TS[0])
        for k in range(1, NX):
            send(TS.at[0], TS.at[k], T1, dev(k, 0, 0, 0))

    def hand_totals():
        arrived(TS.at[pl.ds(1, NX - 1)], T1)
        send(TS.at[pl.ds(0, NX)], TS.at[pl.ds(NX, NX)], T2, mate)

    def line_totals():
        arrived(TS.at[pl.ds(NX, NX)], T2)
        for j in range(2 * NX):
            ITB[j] = across(TS[j])

    def gather_x():
        for k in range(1, NX):
            send(F.at[0], F.at[k], G1, dev(k, 0, 0, 0))

    def hand_blocks():
        arrived(F.at[pl.ds(1, NX - 1)], G1)
        send(F.at[pl.ds(1, NX - 1)], F.at[pl.ds(NX + 1, NX - 1)], G2, mate)

    own = (x * NC + c) * (KB // 256)

    def line_block(j, carry):
        tb = F[j, :B, :].astype(jnp.bfloat16)
        sw = F[j, B:, :]
        sb = sw.astype(jnp.bfloat16)
        SBT[j] = sw.T.astype(jnp.bfloat16)
        for h in range(KB // 256):
            w = WU[own + h]
            ETB[j, h] = jnp.exp(dot(tb, w) * INV_T)
            ESB[j, h] = jnp.exp(dot(sb, w) * INV_S)
        return carry

    def blocks(lo, hi):
        lax.fori_loop(lo, hi, line_block, 0)

    last = ITERS - 1

    @pl.when(c == 0)
    def _():
        send(CS, CR, UP, mate)
        send(F.at[0], F.at[NX], G0, mate)
        student()
        blocks(0, 1)
        student_totals()
        gather_x()
        arrived(F.at[NX], G0)
        blocks(NX, NX + 1)
        hand_totals()
        hand_blocks()
        blocks(1, NX)
        arrived(F.at[pl.ds(NX + 1, NX - 1)], G2)
        blocks(NX + 1, 2 * NX)
        line_totals()
        arrived(CF.at[last], DN)
        arrived(RB, RM)

    @pl.when(c == 1)
    def _():
        def mate_exp(j, carry):
            e = jnp.exp(dot(F[NX, :B, :].astype(jnp.bfloat16), WU[j]) * INV_T)
            E[2 * j, B:] = e[:, :128]
            E[2 * j + 1, B:] = e[:, 128:]
            return carry

        for i in range(ITERS):
            if i == 0:
                send(F.at[0], F.at[NX], G0, mate)
                arrived(CR, UP)
                XS[0] = CS[...] + CR[...]
            for k in range(1, NX):
                send(XS.at[i], XR.at[i, k - 1], XX + i, dev(k, 0, 0, 0))
            if i == 0:
                arrived(F.at[NX], G0)
                lax.fori_loop(0, CH, mate_exp, 0, unroll=4)
            elif i == 1:
                blocks(0, 1)
                blocks(NX, NX + 1)
            else:
                arrived(F.at[pl.ds(NX + 1, NX - 1)], G2)
                blocks(NX + 1, 2 * NX)
            arrived(XR.at[i], XX + i)
            YS[i] = (XS[i] + XR[i, 0]) + (XR[i, 1] + XR[i, 2])
            for k in range(1, NY):
                send(YS.at[i], YR.at[i, k - 1], YY + i, dev(0, k, 0, 0))
            if i == 0:
                gather_x()
                student()
            elif i == 1:
                hand_totals()
                hand_blocks()
                blocks(1, NX)
            else:
                line_totals()
            arrived(YR.at[i], YY + i)
            total = YS[i]
            for k in range(NY - 1):
                total = total + YR[i, k]
            CF[i] = 1.0 / total
            if i == last:
                send(CF.at[last], CF.at[last], DN, mate)

            def step(t, acc):
                return acc + E[t] * CF[i, pl.ds(t, 1), :]

            acc = lax.fori_loop(0, TL, step, jnp.zeros((2 * B, 128), jnp.float32), unroll=4)
            ZS[i, 0:1, :] = jnp.sum(acc[:B].T, 0, keepdims=True)
            ZS[i, 1:2, :] = jnp.sum(acc[B:].T, 0, keepdims=True)
            if i < last:
                for k in range(1, NZ):
                    send(ZS.at[i], ZRV.at[i, k - 1], ZZ + i, dev(0, 0, 0, k))
                if i == 0:
                    student_totals()
                arrived(ZRV.at[i], ZZ + i)
                total = ZS[i]
                for k in range(NZ - 1):
                    total = total + ZRV[i, k]
                inv = 1.0 / total
                RW[:B] = across(inv[0:1])
                RW[B:] = across(inv[1:2])

                def scaled(t, carry):
                    e = E[t] * RW[...]
                    XS[i + 1, pl.ds(t, 1), :] = jnp.sum(e[:B] + e[B:], 0, keepdims=True)
                    return carry

                lax.fori_loop(0, TL, scaled, 0, unroll=4)
            else:
                for k in range(1, NX * NZ):
                    send(ZS.at[i], ZL.at[k], ZZ + i, dev(k // NZ, 0, 0, k % NZ))
                ZL[0] = ZS[i]
                arrived(ZL.at[pl.ds(1, NX * NZ - 1)], ZZ + i)
                for dx in range(NX):
                    total = ZL[dx * NZ]
                    for dz in range(1, NZ):
                        total = total + ZL[dx * NZ + dz]
                    inv = 1.0 / total
                    RB[dx] = inv[0:1]
                    RB[NX + dx] = inv[1:2]
                    RBM[dx] = inv[1:2]
                    RBM[NX + dx] = inv[0:1]
                send(RBM, RB, RM, mate)

    first_tile = (x * NC + c) * (KB // 128)

    def line_grad(j, carry):
        rb = across(RB[j] * SCALE)
        for q in range(KB // 128):
            h, part = q // 2, pl.ds(128 * (q % 2), 128)
            col = CF[last, pl.ds(first_tile + q, 1), :]
            g = ESB[j, h, :, part] * ITB[j] - (ETB[j, h, :, part] * col) * rb
            GB[j, :, 128 * q:128 * q + 128] = g.astype(jnp.bfloat16)
        return carry

    lax.fori_loop(0, 2 * NX, line_grad, 0, unroll=2)
    for h in range(KB // 256):
        acc = jnp.zeros((D, 256), jnp.float32)
        for p in range(NX):
            lhs = jnp.concatenate([SBT[2 * p], SBT[2 * p + 1]], 1)
            rhs = jnp.concatenate(
                [GB[2 * p, :, 256 * h:256 * h + 256], GB[2 * p + 1, :, 256 * h:256 * h + 256]], 0
            )
            acc = acc + dot(lhs, rhs)
        GPS[:, :, 256 * h:256 * h + 256] = acc.reshape(D // 4, 4, 256)

    def scatter(i, carry):
        to = dev(i // (NY * NC), lax.rem(i // NC, NY), lax.rem(i, NC), 0)
        send(GPS.at[to[0]], GPR.at[i], GP, to)
        return carry

    lax.fori_loop(1, NX * NY * NC, scatter, 0)

    RW[:B] = across(RB[0] * SCALE)

    def feature(j, acc):
        g = [
            (SE[2 * j + h] * ITW[...] - (E[2 * j + h, :B] * CF[last, pl.ds(2 * j + h, 1), :]) * RW[:B]).astype(jnp.bfloat16)
            for h in range(2)
        ]
        return acc + lax.dot_general(
            jnp.concatenate(g, 1), WU[j], (((1,), (1,)), ((), ())), preferred_element_type=jnp.float32
        )

    GFA[...] = lax.fori_loop(0, CH, feature, jnp.zeros((B, D), jnp.float32), unroll=4)
    for k in range(NZ):
        GFS[k] = GFA[16 * k:16 * k + 16, :]
    for k in range(1, NZ):
        send(GFS.at[lax.rem(z + k, NZ)], GFR.at[k - 1], ZR, dev(0, 0, 0, k))

    arrived(GFR, ZR)
    mine = pl.ds(pl.multiple_of(z * 16, 16), 16)
    u, inv = unit_rows(s_ref[mine, :])
    u = u.astype(jnp.float32)
    total = GFS[z]
    for k in range(NZ - 1):
        total = total + GFR[k]
    GFO[0] = (total - u * jnp.sum(u * total, 1, keepdims=True)) * inv
    for k in range(1, NZ):
        send(GFO.at[0], GFO.at[k], ZA, dev(0, 0, 0, k))
    gf_out[mine, :] = GFO[0]

    arrived(GPR.at[pl.ds(1, NX * NY * NC - 1)], GP)
    GPR[0] = GPS[dp]
    for dx in range(NX):
        for dc in range(NC):
            total = GPR[dx * NY * NC + dc]
            for dy in range(1, NY):
                total = total + GPR[(dx * NY + dy) * NC + dc]
            at = (lax.rem(x + NX - dx, NX) * NC + lax.rem(c + dc, NC)) * KB
            gp_out[:, pl.ds(pl.multiple_of(at, KB), KB)] = total

    arrived(GFO.at[pl.ds(1, NZ - 1)], ZA)
    for k in range(1, NZ):
        at = lax.rem(z + NZ - k, NZ) * 16
        gf_out[pl.ds(pl.multiple_of(at, 16), 16), :] = GFO[k]

    @pl.when(c == 0)
    def _():
        sent(CS, UP)

    @pl.when(c == 1)
    def _():
        for i in range(ITERS):
            sent(XR.at[i], XX + i)
            sent(YR.at[i], YY + i)
            if i < last:
                sent(ZRV.at[i], ZZ + i)
        sent(ZL.at[pl.ds(1, NX * NZ - 1)], ZZ + last)
        sent(CF.at[last], DN)
        sent(RBM, RM)

    sent(TZR, TZ)
    sent(F.at[0], G0)
    sent(F.at[pl.ds(1, NX - 1)], G1)
    sent(F.at[pl.ds(1, NX - 1)], G2)
    sent(TS.at[pl.ds(1, NX - 1)], T1)
    sent(TS.at[pl.ds(0, NX)], T2)
    sent(GPR.at[pl.ds(1, NX * NY * NC - 1)], GP)
    sent(GFR, ZR)
    sent(GFO.at[pl.ds(1, NZ - 1)], ZA)


def shards(teacher, student, protos):
    f32, bf16 = jnp.float32, jnp.bfloat16
    vm = pltpu.VMEM
    scratch = [
        vm((B, D), bf16),
        vm((B, D), bf16),
        vm((D, K), bf16),
        vm((CH, D, 256), bf16),
        vm((TL, 2 * B, 128), f32),
        vm((TL, B, 128), f32),
        vm((2 * NX, 2 * B, D), f32),
        vm((2 * NX, KB // 256, B, 256), f32),
        vm((2 * NX, KB // 256, B, 256), f32),
        vm((2 * NX, D, B), bf16),
        vm((2 * NX, B, KB), bf16),
        vm((64, 4, KB), f32),
        vm((64, 4, KB), f32),
        vm((NZ, 16, D), f32),
        vm((NZ - 1, 16, D), f32),
        vm((NZ, 16, D), f32),
        vm((B, D), f32),
        vm((TL, 128), f32),
        vm((TL, 128), f32),
        vm((ITERS, TL, 128), f32),
        vm((ITERS, NX - 1, TL, 128), f32),
        vm((ITERS, TL, 128), f32),
        vm((ITERS, NY - 1, TL, 128), f32),
        vm((ITERS, TL, 128), f32),
        vm((ITERS, 2, 128), f32),
        vm((ITERS - 1, NZ - 1, 2, 128), f32),
        vm((NX * NZ, 2, 128), f32),
        vm((1, 128), f32),
        vm((NZ - 1, 1, 128), f32),
        vm((2 * NX, 1, 128), f32),
        vm((2 * NX, 1, 128), f32),
        vm((2 * NX, 1, 128), f32),
        vm((2 * NX, B, 128), f32),
        vm((2 * B, 128), f32),
        vm((B, 128), f32),
        pltpu.SemaphoreType.DMA((2 + LOADS,)),
        pltpu.SemaphoreType.DMA((GROUPS,)),
        pltpu.SemaphoreType.DMA((GROUPS,)),
    ]
    whole = pl.BlockSpec(memory_space=pltpu.VMEM)
    anywhere = pl.BlockSpec(memory_space=pl.ANY)
    return pl.pallas_call(
        body,
        out_shape=(jax.ShapeDtypeStruct((B, D), f32), jax.ShapeDtypeStruct((4, K), f32)),
        in_specs=[anywhere] * 3,
        out_specs=(whole, whole),
        scratch_shapes=scratch,
        compiler_params=pltpu.CompilerParams(
            collective_id=0, has_side_effects=True, vmem_limit_bytes=60 * 2**20
        ),
    )(teacher, student, protos)


def solution(mesh):
    placed = (P("dp", None), P("dp", None), P(None, "proto"))
    return jax.shard_map(
        shards,
        mesh=mesh,
        in_specs=placed,
        out_specs=(P("dp", None), P("dp", "proto")),
        check_vma=False,
    )
```

```python
import functools

import jax
import jax.numpy as jnp
from jax import lax
from jax.experimental import pallas as pl
from jax.experimental.pallas import tpu as pltpu
from jax.sharding import PartitionSpec as P

EPS = 1e-06
INV_T = 1.0 / 0.07
INV_S = 1.0 / 0.1
ITERS = 3
NX, NY, NC, NZ = 4, 8, 2, 8
B = 128
D = 256
K = 4096
CH = K // 256
TL = K // 128
NB = 2 * NX
KB = K // (NB * NC)
SCALE = 32768 / 64.0 / 0.1
MESH = pl.DeviceIdType.MESH

UP, DN, G0, GY, G1, G2, TZ, T1, T2, RM, GP, AR, TR, ZA = range(14)
XX, YY, ZZ = (14, 17, 20)
GROUPS = 23
XO = (2, 1, 3)
YO = ZO = (4, 3, 5, 2, 6, 1, 7)
LOADS = 4


def dot(a, b):
    return jnp.dot(a, b, preferred_element_type=jnp.float32)


def unit_rows(raw):
    wide = raw.astype(jnp.float32)
    inv = lax.rsqrt(jnp.sum(wide * wide, 1, keepdims=True) + EPS)
    return (wide * inv).astype(jnp.bfloat16), inv


def across(row):
    return jnp.broadcast_to(row, (128, 128)).T


def body(
    t_hbm, s_hbm, w_hbm, gf_out, gp_out,
    t_ref, s_ref, w_ref, WU, E, SE, F, ETB, ESB, SBT, GB, GPS, GPR, GAS, GAR, GTS, GTR, GFO, GFA,
    CS, CR, XS, XR, YS, YR, CF, ZS, ZRV, ZL, TZS, TZR, TS, RB, RBM, ITB, RW, ITW, lsem, ssem, rsem,
):
    dp = lax.axis_index("dp")
    z = lax.axis_index("proto")
    c = lax.rem(dp, 2)
    y = lax.rem(dp // 2, NY)
    x = dp // (2 * NY)

    def dev(dx, dy, dc, dz):
        return (
            (lax.rem(x + dx, NX) * NY + lax.rem(y + dy, NY)) * NC + lax.rem(c + dc, NC),
            lax.rem(z + dz, NZ),
        )

    mate = dev(0, 0, 1, 0)
    flip = NY + 1 - 2 * lax.rem(y, 2)

    def send(src, dst, group, to):
        pltpu.make_async_remote_copy(
            src, dst, ssem.at[group], rsem.at[group], device_id=to, device_id_type=MESH
        ).start()

    def arrived(ref, group):
        pltpu.make_async_remote_copy(
            ref, ref, ssem.at[group], rsem.at[group], device_id=mate, device_id_type=MESH
        ).wait_recv()

    def sent(ref, group):
        pltpu.make_async_remote_copy(
            ref, ref, ssem.at[group], rsem.at[group], device_id=mate, device_id_type=MESH
        ).wait_send()

    loads = [
        pltpu.make_async_copy(t_hbm, t_ref, lsem.at[0]),
        pltpu.make_async_copy(s_hbm, s_ref, lsem.at[1]),
    ]
    for piece in range(LOADS):
        cols = pl.ds(piece * (K // LOADS), K // LOADS)
        loads.append(pltpu.make_async_copy(w_hbm.at[:, cols], w_ref.at[:, cols], lsem.at[2 + piece]))
    for load in loads:
        load.start()

    peers = [dev(0, 0, 1, 0)]
    peers += [dev(k, 0, 0, 0) for k in range(1, NX)]
    peers += [dev(0, k, 0, 0) for k in range(1, NY)]
    peers += [dev(0, 0, 0, k) for k in range(1, NZ)]
    peers += [dev(k, flip, 0, 0) for k in range(1, NX)]
    barrier = pltpu.get_barrier_semaphore()
    for to in peers:
        pl.semaphore_signal(barrier, inc=1, device_id=to, device_id_type=MESH)

    loads[0].wait()
    t_unit, _ = unit_rows(t_ref[...])
    F[0, :B, :] = t_unit.astype(jnp.float32)

    def first(j, carry):
        w = w_ref[:, pl.ds(pl.multiple_of(j * 256, 256), 256)].astype(jnp.float32)
        w = (w * lax.rsqrt(jnp.sum(w * w, 0, keepdims=True) + EPS)).astype(jnp.bfloat16)
        WU[j] = w
        e = jnp.exp(dot(t_unit, w) * INV_T)
        E[2 * j, :B] = e[:, :128]
        E[2 * j + 1, :B] = e[:, 128:]
        CS[pl.ds(2 * j, 1), :] = jnp.sum(e[:, :128], 0, keepdims=True)
        CS[pl.ds(2 * j + 1, 1), :] = jnp.sum(e[:, 128:], 0, keepdims=True)
        return carry

    per = CH // LOADS
    for piece in range(LOADS):
        loads[2 + piece].wait()
        lax.fori_loop(piece * per, piece * per + per, first, 0, unroll=True)
    loads[1].wait()
    s_unit, _ = unit_rows(s_ref[...])
    F[0, B:, :] = s_unit.astype(jnp.float32)
    pl.semaphore_wait(barrier, len(peers))

    def student():
        def step(j, acc):
            e = jnp.exp(dot(F[0, B:, :].astype(jnp.bfloat16), WU[j]) * INV_S)
            SE[2 * j] = e[:, :128]
            SE[2 * j + 1] = e[:, 128:]
            return acc + e[:, :128] + e[:, 128:]

        acc = lax.fori_loop(0, CH, step, jnp.zeros((B, 128), jnp.float32), unroll=4)
        TZS[...] = jnp.sum(acc.T, 0, keepdims=True)
        for k in ZO:
            send(TZS, TZR.at[k - 1], TZ, dev(0, 0, 0, k))

    def product(tile, kept, got, group):
        def step(j, acc):
            g = jnp.concatenate([tile(2 * j), tile(2 * j + 1)], 1)
            high = g.astype(jnp.bfloat16)
            low = (g - high.astype(jnp.float32)).astype(jnp.bfloat16)
            return acc + lax.dot_general(
                jnp.concatenate([high, low], 0), WU[j], (((1,), (1,)), ((), ())), preferred_element_type=jnp.float32
            )

        acc = lax.fori_loop(0, CH, step, jnp.zeros((2 * B, D), jnp.float32), unroll=2)
        GFA[...] = acc[:B] + acc[B:]
        for k in range(NZ):
            kept[k] = GFA[16 * k:16 * k + 16, :]
        for k in ZO:
            send(kept.at[lax.rem(z + k, NZ)], got.at[k - 1], group, dev(0, 0, 0, k))

    def student_product():
        product(lambda t: SE[t] * ITW[...], GAS, GAR, AR)

    def teacher_product():
        product(lambda t: E[t, :B] * CF[ITERS - 1, pl.ds(t, 1), :], GTS, GTR, TR)

    def student_totals():
        arrived(TZR, TZ)
        total = TZS[...]
        for k in range(NZ - 1):
            total = total + TZR[k]
        TS[0] = SCALE / total
        ITW[...] = across(TS[0])
        for k in XO:
            for p in (1, 0):
                send(TS.at[0], TS.at[2 * k + p], T1, dev(k, flip * p, 0, 0))
        send(TS.at[0], TS.at[1], T1, dev(0, flip, 0, 0))

    def hand_totals():
        arrived(TS.at[pl.ds(1, NB - 1)], T1)
        send(TS.at[pl.ds(0, NB)], TS.at[pl.ds(NB, NB)], T2, mate)

    def line_totals():
        arrived(TS.at[pl.ds(NB, NB)], T2)
        for j in range(2 * NB):
            ITB[j] = across(TS[j])

    def gather_y():
        send(F.at[0], F.at[1], GY, dev(0, flip, 0, 0))

    def gather_x():
        arrived(F.at[1], GY)
        for k in XO:
            send(F.at[pl.ds(0, 2)], F.at[pl.ds(2 * k, 2)], G1, dev(k, 0, 0, 0))

    def hand_blocks():
        arrived(F.at[pl.ds(2, NB - 2)], G1)
        send(F.at[pl.ds(1, NB - 1)], F.at[pl.ds(NB + 1, NB - 1)], G2, mate)

    own = (x * 2 + lax.rem(y, 2)) * NC + c

    def line_block(j, carry):
        tb = F[j, :B, :].astype(jnp.bfloat16)
        sw = F[j, B:, :]
        SBT[j] = sw.T.astype(jnp.bfloat16)
        ETB[j] = jnp.exp(dot(tb, WU[own]) * INV_T)
        ESB[j] = jnp.exp(dot(sw.astype(jnp.bfloat16), WU[own]) * INV_S)
        return carry

    def blocks(lo, hi):
        lax.fori_loop(lo, hi, line_block, 0)

    last = ITERS - 1

    @pl.when(c == 0)
    def _():
        send(CS, CR, UP, mate)
        send(F.at[0], F.at[NB], G0, mate)
        gather_y()
        student()
        blocks(0, 1)
        student_totals()
        arrived(F.at[NB], G0)
        gather_x()
        blocks(NB, NB + 1)
        student_product()
        blocks(1, 2)
        hand_totals()
        line_totals()
        hand_blocks()
        blocks(2, NB)
        arrived(F.at[pl.ds(NB + 1, NB - 1)], G2)
        blocks(NB + 1, 2 * NB)
        arrived(CF.at[last], DN)
        teacher_product()
        arrived(RB, RM)

    @pl.when(c == 1)
    def _():
        def mate_exp(j, carry):
            e = jnp.exp(dot(F[NB, :B, :].astype(jnp.bfloat16), WU[j]) * INV_T)
            E[2 * j, B:] = e[:, :128]
            E[2 * j + 1, B:] = e[:, 128:]
            return carry

        for i in range(ITERS):
            if i == 0:
                send(F.at[0], F.at[NB], G0, mate)
                arrived(CR, UP)
                XS[0] = CS[...] + CR[...]
            for k in XO:
                send(XS.at[i], XR.at[i, k - 1], XX + i, dev(k, 0, 0, 0))
            if i == 0:
                gather_y()
                arrived(F.at[NB], G0)
                lax.fori_loop(0, CH, mate_exp, 0, unroll=4)
            elif i == 1:
                blocks(0, 2)
                blocks(NB, NB + 1)
                hand_totals()
            arrived(XR.at[i], XX + i)
            YS[i] = (XS[i] + XR[i, 0]) + (XR[i, 1] + XR[i, 2])
            for k in YO:
                send(YS.at[i], YR.at[i, k - 1], YY + i, dev(0, k, 0, 0))
            if i == 0:
                student()
            elif i == 1:
                student_product()
            else:
                hand_blocks()
                blocks(2, NB)
            arrived(YR.at[i], YY + i)
            total = YS[i]
            for k in range(NY - 1):
                total = total + YR[i, k]
            CF[i] = 1.0 / total
            if i == last:
                send(CF.at[last], CF.at[last], DN, mate)

            def step(t, acc):
                return acc + E[t] * CF[i, pl.ds(t, 1), :]

            acc = lax.fori_loop(0, TL, step, jnp.zeros((2 * B, 128), jnp.float32), unroll=4)
            ZS[i, 0:1, :] = jnp.sum(acc[:B].T, 0, keepdims=True)
            ZS[i, 1:2, :] = jnp.sum(acc[B:].T, 0, keepdims=True)
            if i < last:
                for k in ZO:
                    send(ZS.at[i], ZRV.at[i, k - 1], ZZ + i, dev(0, 0, 0, k))
                if i == 0:
                    student_totals()
                    gather_x()
                else:
                    line_totals()
                arrived(ZRV.at[i], ZZ + i)
                total = ZS[i]
                for k in range(NZ - 1):
                    total = total + ZRV[i, k]
                inv = 1.0 / total
                RW[:B] = across(inv[0:1])
                RW[B:] = across(inv[1:2])

                def scaled(t, carry):
                    e = E[t] * RW[...]
                    XS[i + 1, pl.ds(t, 1), :] = jnp.sum(e[:B] + e[B:], 0, keepdims=True)
                    return carry

                lax.fori_loop(0, TL, scaled, 0, unroll=4)
            else:
                far = lambda k: -(min(k // (2 * NZ), NX - k // (2 * NZ)) + k // NZ % 2 + min(k % NZ, NZ - k % NZ))
                for k in sorted(range(1, NB * NZ), key=far):
                    to = dev(k // (2 * NZ), flip * (k // NZ % 2), 0, k % NZ)
                    send(ZS.at[i], ZL.at[k], ZZ + i, to)
                ZL[0] = ZS[i]
                teacher_product()
                arrived(F.at[pl.ds(NB + 1, NB - 1)], G2)
                blocks(NB + 1, 2 * NB)
                arrived(ZL.at[pl.ds(1, NB * NZ - 1)], ZZ + i)
                for j in range(NB):
                    total = ZL[j * NZ]
                    for dz in range(1, NZ):
                        total = total + ZL[j * NZ + dz]
                    inv = 1.0 / total
                    RB[j] = inv[0:1]
                    RB[NB + j] = inv[1:2]
                    RBM[j] = inv[1:2]
                    RBM[NB + j] = inv[0:1]
                send(RBM, RB, RM, mate)

    def line_grad(j, carry):
        rb = across(RB[j] * SCALE)
        for q in range(KB // 128):
            part = pl.ds(128 * q, 128)
            col = CF[last, pl.ds(own * (KB // 128) + q, 1), :]
            g = ESB[j, :, part] * ITB[j] - (ETB[j, :, part] * col) * rb
            GB[j, :, 128 * q:128 * q + 128] = g.astype(jnp.bfloat16)
        return carry

    lax.fori_loop(0, 2 * NB, line_grad, 0, unroll=4)
    acc = jnp.zeros((D, KB), jnp.float32)
    for p in range(NB):
        lhs = jnp.concatenate([SBT[2 * p], SBT[2 * p + 1]], 1)
        acc = acc + dot(lhs, jnp.concatenate([GB[2 * p], GB[2 * p + 1]], 0))
    GPS[...] = acc.reshape(D // 4, 4, KB)

    for dy in YO + (0,):
        def scatter(i, carry):
            to = dev(i // NC, dy, lax.rem(i, NC), 0)
            send(GPS.at[to[0]], GPR.at[i // NC * (NY * NC) + dy * NC + lax.rem(i, NC)], GP, to)
            return carry

        lax.fori_loop(0 if dy else 1, NX * NC, scatter, 0)

    RW[:B] = across(RB[0] * SCALE)
    mine = pl.ds(pl.multiple_of(z * 16, 16), 16)
    u, inv = unit_rows(s_ref[mine, :])
    u = u.astype(jnp.float32)
    arrived(GAR, AR)
    arrived(GTR, TR)
    total, teach = GAS[z], GTS[z]
    for k in range(NZ - 1):
        total = total + GAR[k]
        teach = teach + GTR[k]
    total = total - teach * RW[mine, 0:1]
    GFO[0] = (total - u * jnp.sum(u * total, 1, keepdims=True)) * inv
    for k in ZO:
        send(GFO.at[0], GFO.at[k], ZA, dev(0, 0, 0, k))
    gf_out[mine, :] = GFO[0]
    arrived(GFO.at[pl.ds(1, NZ - 1)], ZA)
    for k in range(1, NZ):
        at = lax.rem(z + NZ - k, NZ) * 16
        gf_out[pl.ds(pl.multiple_of(at, 16), 16), :] = GFO[k]

    arrived(GPR.at[pl.ds(1, NX * NY * NC - 1)], GP)
    GPR[0] = GPS[dp]
    for dx in range(NX):
        for dc in range(NC):
            for p in range(2):
                total = GPR[(dx * NY + p) * NC + dc]
                for dy in range(p + 2, NY, 2):
                    total = total + GPR[(dx * NY + dy) * NC + dc]
                at = (lax.rem(x + NX - dx, NX) * 2 + lax.rem(y + p, 2)) * NC + lax.rem(c + dc, NC)
                gp_out[:, pl.ds(pl.multiple_of(at * KB, KB), KB)] = total

    @pl.when(c == 0)
    def _():
        sent(CS, UP)

    @pl.when(c == 1)
    def _():
        for i in range(ITERS):
            sent(XR.at[i], XX + i)
            sent(YR.at[i], YY + i)
            if i < last:
                sent(ZRV.at[i], ZZ + i)
        sent(ZL.at[pl.ds(1, NB * NZ - 1)], ZZ + last)
        sent(CF.at[last], DN)
        sent(RBM, RM)

    sent(TZR, TZ)
    sent(F.at[0], G0)
    sent(F.at[0], GY)
    sent(F.at[pl.ds(2, NB - 2)], G1)
    sent(F.at[pl.ds(1, NB - 1)], G2)
    sent(TS.at[pl.ds(1, NB - 1)], T1)
    sent(TS.at[pl.ds(0, NB)], T2)
    sent(GPR.at[pl.ds(1, NX * NY * NC - 1)], GP)
    sent(GAR, AR)
    sent(GTR, TR)
    sent(GFO.at[pl.ds(1, NZ - 1)], ZA)


def place(features, protos, features_out, protos_out, sem):
    copies = [
        pltpu.make_async_copy(features, features_out, sem.at[0]),
        pltpu.make_async_copy(protos, protos_out, sem.at[1]),
    ]
    for copy in copies:
        copy.start()
    for copy in copies:
        copy.wait()


def shards(teacher, student, protos):
    f32, bf16 = jnp.float32, jnp.bfloat16
    vm = pltpu.VMEM
    scratch = [
        vm((B, D), bf16),
        vm((B, D), bf16),
        vm((D, K), bf16),
        vm((CH, D, 256), bf16),
        vm((TL, 2 * B, 128), f32),
        vm((TL, B, 128), f32),
        vm((2 * NB, 2 * B, D), f32),
        vm((2 * NB, B, KB), f32),
        vm((2 * NB, B, KB), f32),
        vm((2 * NB, D, B), bf16),
        vm((2 * NB, B, KB), bf16),
        vm((64, 4, KB), f32),
        vm((64, 4, KB), f32),
        vm((NZ, 16, D), f32),
        vm((NZ - 1, 16, D), f32),
        vm((NZ, 16, D), f32),
        vm((NZ - 1, 16, D), f32),
        vm((NZ, 16, D), f32),
        vm((B, D), f32),
        vm((TL, 128), f32),
        vm((TL, 128), f32),
        vm((ITERS, TL, 128), f32),
        vm((ITERS, NX - 1, TL, 128), f32),
        vm((ITERS, TL, 128), f32),
        vm((ITERS, NY - 1, TL, 128), f32),
        vm((ITERS, TL, 128), f32),
        vm((ITERS, 2, 128), f32),
        vm((ITERS - 1, NZ - 1, 2, 128), f32),
        vm((NB * NZ, 2, 128), f32),
        vm((1, 128), f32),
        vm((NZ - 1, 1, 128), f32),
        vm((2 * NB, 1, 128), f32),
        vm((2 * NB, 1, 128), f32),
        vm((2 * NB, 1, 128), f32),
        vm((2 * NB, B, 128), f32),
        vm((2 * B, 128), f32),
        vm((B, 128), f32),
        pltpu.SemaphoreType.DMA((2 + LOADS,)),
        pltpu.SemaphoreType.DMA((GROUPS,)),
        pltpu.SemaphoreType.DMA((GROUPS,)),
    ]
    whole = pl.BlockSpec(memory_space=pltpu.VMEM)
    anywhere = pl.BlockSpec(memory_space=pl.ANY)
    grads = pl.pallas_call(
        body,
        out_shape=(jax.ShapeDtypeStruct((B, D), f32), jax.ShapeDtypeStruct((4, K), f32)),
        in_specs=[anywhere] * 3,
        out_specs=(whole, whole),
        scratch_shapes=scratch,
        compiler_params=pltpu.CompilerParams(
            collective_id=0, has_side_effects=True, vmem_limit_bytes=60 * 2**20
        ),
    )(teacher, student, protos)
    return pl.pallas_call(
        place,
        out_shape=tuple(jax.ShapeDtypeStruct(g.shape, g.dtype) for g in grads),
        in_specs=[anywhere] * 2,
        out_specs=(anywhere,) * 2,
        scratch_shapes=[pltpu.SemaphoreType.DMA((2,))],
        compiler_params=pltpu.CompilerParams(vmem_limit_bytes=60 * 2**20),
    )(*grads)


def solution(mesh):
    placed = (P("dp", None), P("dp", None), P(None, "proto"))
    return jax.shard_map(
        shards,
        mesh=mesh,
        in_specs=placed,
        out_specs=(P("dp", None), P("dp", "proto")),
        check_vma=False,
    )
```

```python
import functools

import jax
import jax.numpy as jnp
from jax import lax
from jax.experimental import pallas as pl
from jax.experimental.pallas import tpu as pltpu
from jax.sharding import PartitionSpec as P

EPS = 1e-06
INV_T = 1.0 / 0.07
INV_S = 1.0 / 0.1
ITERS = 3
NX, NY, NC, NZ = 4, 8, 2, 8
B = 128
D = 256
K = 4096
CH = K // 256
TL = K // 128
NB = 2 * NX
KB = K // (NB * NC)
SCALE = 32768 / 64.0 / 0.1
MESH = pl.DeviceIdType.MESH

UP, DN, G0, GY, G2, TZ, T1, T2, RM, GP, AR, TR, ZA = range(13)
XX, YY, ZZ = (13, 16, 19)
GL, GR, GF = (22, 24, 26)
GROUPS = 28
XO = (2, 1, 3)
YO = ZO = (4, 3, 5, 2, 6, 1, 7)
LOADS = 4


def dot(a, b):
    return jnp.dot(a, b, preferred_element_type=jnp.float32)


def unit_rows(raw):
    wide = raw.astype(jnp.float32)
    inv = lax.rsqrt(jnp.sum(wide * wide, 1, keepdims=True) + EPS)
    return (wide * inv).astype(jnp.bfloat16), inv


def across(row):
    return jnp.broadcast_to(row, (128, 128)).T


def body(
    t_hbm, s_hbm, w_hbm, gf_out, gp_out,
    t_ref, s_ref, w_ref, WU, E, SE, F, ETB, ESB, SBT, GB, GPS, GPR, GAS, GAR, GTS, GTR, GFO, GFA,
    CS, CR, XS, XR, YS, YR, CF, ZS, ZRV, ZL, TZS, TZR, TS, RB, RBM, ITB, RW, ITW, lsem, ssem, rsem,
):
    dp = lax.axis_index("dp")
    z = lax.axis_index("proto")
    c = lax.rem(dp, 2)
    y = lax.rem(dp // 2, NY)
    x = dp // (2 * NY)

    def dev(dx, dy, dc, dz):
        return (
            (lax.rem(x + dx, NX) * NY + lax.rem(y + dy, NY)) * NC + lax.rem(c + dc, NC),
            lax.rem(z + dz, NZ),
        )

    mate = dev(0, 0, 1, 0)
    flip = NY + 1 - 2 * lax.rem(y, 2)

    def send(src, dst, group, to):
        pltpu.make_async_remote_copy(
            src, dst, ssem.at[group], rsem.at[group], device_id=to, device_id_type=MESH
        ).start()

    def arrived(ref, group):
        pltpu.make_async_remote_copy(
            ref, ref, ssem.at[group], rsem.at[group], device_id=mate, device_id_type=MESH
        ).wait_recv()

    def sent(ref, group):
        pltpu.make_async_remote_copy(
            ref, ref, ssem.at[group], rsem.at[group], device_id=mate, device_id_type=MESH
        ).wait_send()

    loads = [
        pltpu.make_async_copy(t_hbm, t_ref, lsem.at[0]),
        pltpu.make_async_copy(s_hbm, s_ref, lsem.at[1]),
    ]
    for piece in range(LOADS):
        cols = pl.ds(piece * (K // LOADS), K // LOADS)
        loads.append(pltpu.make_async_copy(w_hbm.at[:, cols], w_ref.at[:, cols], lsem.at[2 + piece]))
    for load in loads:
        load.start()

    peers = [dev(0, 0, 1, 0)]
    peers += [dev(k, 0, 0, 0) for k in range(1, NX)]
    peers += [dev(0, k, 0, 0) for k in range(1, NY)]
    peers += [dev(0, 0, 0, k) for k in range(1, NZ)]
    peers += [dev(k, flip, 0, 0) for k in range(1, NX)]
    barrier = pltpu.get_barrier_semaphore()
    for to in peers:
        pl.semaphore_signal(barrier, inc=1, device_id=to, device_id_type=MESH)

    loads[0].wait()
    t_unit, _ = unit_rows(t_ref[...])
    F[0, :B, :] = t_unit.astype(jnp.float32)

    def first(j, carry):
        w = w_ref[:, pl.ds(pl.multiple_of(j * 256, 256), 256)].astype(jnp.float32)
        w = (w * lax.rsqrt(jnp.sum(w * w, 0, keepdims=True) + EPS)).astype(jnp.bfloat16)
        WU[j] = w
        e = jnp.exp(dot(t_unit, w) * INV_T)
        E[2 * j, :B] = e[:, :128]
        E[2 * j + 1, :B] = e[:, 128:]
        CS[pl.ds(2 * j, 1), :] = jnp.sum(e[:, :128], 0, keepdims=True)
        CS[pl.ds(2 * j + 1, 1), :] = jnp.sum(e[:, 128:], 0, keepdims=True)
        return carry

    per = CH // LOADS
    for piece in range(LOADS):
        loads[2 + piece].wait()
        lax.fori_loop(piece * per, piece * per + per, first, 0, unroll=True)
    loads[1].wait()
    s_unit, _ = unit_rows(s_ref[...])
    F[0, B:, :] = s_unit.astype(jnp.float32)
    pl.semaphore_wait(barrier, len(peers))

    def student():
        def step(j, acc):
            e = jnp.exp(dot(F[0, B:, :].astype(jnp.bfloat16), WU[j]) * INV_S)
            SE[2 * j] = e[:, :128]
            SE[2 * j + 1] = e[:, 128:]
            return acc + e[:, :128] + e[:, 128:]

        acc = lax.fori_loop(0, CH, step, jnp.zeros((B, 128), jnp.float32), unroll=4)
        TZS[...] = jnp.sum(acc.T, 0, keepdims=True)
        for k in ZO:
            send(TZS, TZR.at[k - 1], TZ, dev(0, 0, 0, k))

    def product(tile, kept, got, group):
        def step(j, acc):
            g = jnp.concatenate([tile(2 * j), tile(2 * j + 1)], 1)
            high = g.astype(jnp.bfloat16)
            low = (g - high.astype(jnp.float32)).astype(jnp.bfloat16)
            return acc + lax.dot_general(
                jnp.concatenate([high, low], 0), WU[j], (((1,), (1,)), ((), ())), preferred_element_type=jnp.float32
            )

        acc = lax.fori_loop(0, CH, step, jnp.zeros((2 * B, D), jnp.float32), unroll=2)
        GFA[...] = acc[:B] + acc[B:]
        for k in range(NZ):
            kept[k] = GFA[16 * k:16 * k + 16, :]
        for k in ZO:
            send(kept.at[lax.rem(z + k, NZ)], got.at[k - 1], group, dev(0, 0, 0, k))

    def student_product():
        product(lambda t: SE[t] * ITW[...], GAS, GAR, AR)

    def teacher_product():
        product(lambda t: E[t, :B] * CF[ITERS - 1, pl.ds(t, 1), :], GTS, GTR, TR)

    def student_totals():
        arrived(TZR, TZ)
        total = TZS[...]
        for k in range(NZ - 1):
            total = total + TZR[k]
        TS[0] = SCALE / total
        ITW[...] = across(TS[0])
        for k in XO:
            for p in (1, 0):
                send(TS.at[0], TS.at[2 * k + p], T1, dev(k, flip * p, 0, 0))
        send(TS.at[0], TS.at[1], T1, dev(0, flip, 0, 0))

    def hand_totals():
        arrived(TS.at[pl.ds(1, NB - 1)], T1)
        send(TS.at[pl.ds(0, NB)], TS.at[pl.ds(NB, NB)], T2, mate)

    def line_totals():
        arrived(TS.at[pl.ds(NB, NB)], T2)
        for j in range(2 * NB):
            ITB[j] = across(TS[j])

    def to_sides(p):
        send(F.at[p], F.at[2 + p], GL + p, dev(1, 0, 0, 0))
        send(F.at[p], F.at[6 + p], GR + p, dev(3, 0, 0, 0))

    def relay(p):
        arrived(F.at[2 + p], GL + p)
        arrived(F.at[6 + p], GR + p)
        send(F.at[2 + p, pl.ds(0, B)], F.at[4 + p, pl.ds(0, B)], GF + p, dev(1, 0, 0, 0))
        send(F.at[6 + p, pl.ds(B, B)], F.at[4 + p, pl.ds(B, B)], GF + p, dev(3, 0, 0, 0))

    def gather_1():
        send(F.at[0], F.at[1], GY, dev(0, flip, 0, 0))
        to_sides(0)

    def gather_2():
        arrived(F.at[1], GY)
        to_sides(1)
        relay(0)

    def gather_3():
        relay(1)

    def gather_4():
        for p in range(2):
            arrived(F.at[4 + p], GF + p)
        send(F.at[pl.ds(1, NB - 1)], F.at[pl.ds(NB + 1, NB - 1)], G2, mate)

    own = (x * 2 + lax.rem(y, 2)) * NC + c

    def line_block(j, carry):
        tb = F[j, :B, :].astype(jnp.bfloat16)
        sw = F[j, B:, :]
        SBT[j] = sw.T.astype(jnp.bfloat16)
        ETB[j] = jnp.exp(dot(tb, WU[own]) * INV_T)
        ESB[j] = jnp.exp(dot(sw.astype(jnp.bfloat16), WU[own]) * INV_S)
        return carry

    def blocks(lo, hi):
        lax.fori_loop(lo, hi, line_block, 0)

    last = ITERS - 1

    @pl.when(c == 0)
    def _():
        send(CS, CR, UP, mate)
        send(F.at[0], F.at[NB], G0, mate)
        gather_1()
        student()
        blocks(0, 1)
        student_totals()
        arrived(F.at[NB], G0)
        gather_2()
        blocks(NB, NB + 1)
        blocks(1, 2)
        gather_3()
        hand_totals()
        student_product()
        line_totals()
        gather_4()
        blocks(2, NB)
        arrived(F.at[pl.ds(NB + 1, NB - 1)], G2)
        blocks(NB + 1, 2 * NB)
        arrived(CF.at[last], DN)
        teacher_product()
        arrived(RB, RM)

    @pl.when(c == 1)
    def _():
        def mate_exp(j, carry):
            e = jnp.exp(dot(F[NB, :B, :].astype(jnp.bfloat16), WU[j]) * INV_T)
            E[2 * j, B:] = e[:, :128]
            E[2 * j + 1, B:] = e[:, 128:]
            return carry

        for i in range(ITERS):
            if i == 0:
                send(F.at[0], F.at[NB], G0, mate)
                arrived(CR, UP)
                XS[0] = CS[...] + CR[...]
            for k in XO:
                send(XS.at[i], XR.at[i, k - 1], XX + i, dev(k, 0, 0, 0))
            if i == 0:
                gather_1()
                arrived(F.at[NB], G0)
                lax.fori_loop(0, CH, mate_exp, 0, unroll=4)
            elif i == 1:
                blocks(0, 2)
                blocks(NB, NB + 1)
                hand_totals()
            else:
                blocks(2, NB)
            arrived(XR.at[i], XX + i)
            YS[i] = (XS[i] + XR[i, 0]) + (XR[i, 1] + XR[i, 2])
            for k in YO:
                send(YS.at[i], YR.at[i, k - 1], YY + i, dev(0, k, 0, 0))
            if i == 0:
                student()
            elif i == 1:
                gather_3()
                student_product()
            else:
                arrived(F.at[pl.ds(NB + 1, NB - 1)], G2)
                blocks(NB + 1, 2 * NB)
            arrived(YR.at[i], YY + i)
            total = YS[i]
            for k in range(NY - 1):
                total = total + YR[i, k]
            CF[i] = 1.0 / total
            if i == last:
                send(CF.at[last], CF.at[last], DN, mate)

            def step(t, acc):
                return acc + E[t] * CF[i, pl.ds(t, 1), :]

            acc = lax.fori_loop(0, TL, step, jnp.zeros((2 * B, 128), jnp.float32), unroll=4)
            ZS[i, 0:1, :] = jnp.sum(acc[:B].T, 0, keepdims=True)
            ZS[i, 1:2, :] = jnp.sum(acc[B:].T, 0, keepdims=True)
            if i < last:
                for k in ZO:
                    send(ZS.at[i], ZRV.at[i, k - 1], ZZ + i, dev(0, 0, 0, k))
                if i == 0:
                    student_totals()
                    gather_2()
                else:
                    gather_4()
                    line_totals()
                arrived(ZRV.at[i], ZZ + i)
                total = ZS[i]
                for k in range(NZ - 1):
                    total = total + ZRV[i, k]
                inv = 1.0 / total
                RW[:B] = across(inv[0:1])
                RW[B:] = across(inv[1:2])

                def scaled(t, carry):
                    e = E[t] * RW[...]
                    XS[i + 1, pl.ds(t, 1), :] = jnp.sum(e[:B] + e[B:], 0, keepdims=True)
                    return carry

                lax.fori_loop(0, TL, scaled, 0, unroll=4)
            else:
                far = lambda k: -(min(k // (2 * NZ), NX - k // (2 * NZ)) + k // NZ % 2 + min(k % NZ, NZ - k % NZ))
                for k in sorted(range(1, NB * NZ), key=far):
                    to = dev(k // (2 * NZ), flip * (k // NZ % 2), 0, k % NZ)
                    send(ZS.at[i], ZL.at[k], ZZ + i, to)
                ZL[0] = ZS[i]
                teacher_product()
                arrived(ZL.at[pl.ds(1, NB * NZ - 1)], ZZ + i)
                for j in range(NB):
                    total = ZL[j * NZ]
                    for dz in range(1, NZ):
                        total = total + ZL[j * NZ + dz]
                    inv = 1.0 / total
                    RB[j] = inv[0:1]
                    RB[NB + j] = inv[1:2]
                    RBM[j] = inv[1:2]
                    RBM[NB + j] = inv[0:1]
                send(RBM, RB, RM, mate)

    def line_grad(j, carry):
        rb = across(RB[j] * SCALE)
        for q in range(KB // 128):
            part = pl.ds(128 * q, 128)
            col = CF[last, pl.ds(own * (KB // 128) + q, 1), :]
            g = ESB[j, :, part] * ITB[j] - (ETB[j, :, part] * col) * rb
            GB[j, :, 128 * q:128 * q + 128] = g.astype(jnp.bfloat16)
        return carry

    lax.fori_loop(0, 2 * NB, line_grad, 0, unroll=4)
    acc = jnp.zeros((D, KB), jnp.float32)
    for p in range(NB):
        lhs = jnp.concatenate([SBT[2 * p], SBT[2 * p + 1]], 1)
        acc = acc + dot(lhs, jnp.concatenate([GB[2 * p], GB[2 * p + 1]], 0))
    GPS[...] = acc.reshape(D // 4, 4, KB)

    for dy in YO + (0,):
        def scatter(i, carry):
            to = dev(i // NC, dy, lax.rem(i, NC), 0)
            send(GPS.at[to[0]], GPR.at[i // NC * (NY * NC) + dy * NC + lax.rem(i, NC)], GP, to)
            return carry

        lax.fori_loop(0 if dy else 1, NX * NC, scatter, 0)

    RW[:B] = across(RB[0] * SCALE)
    mine = pl.ds(pl.multiple_of(z * 16, 16), 16)
    u, inv = unit_rows(s_ref[mine, :])
    u = u.astype(jnp.float32)
    arrived(GAR, AR)
    arrived(GTR, TR)
    total, teach = GAS[z], GTS[z]
    for k in range(NZ - 1):
        total = total + GAR[k]
        teach = teach + GTR[k]
    total = total - teach * RW[mine, 0:1]
    GFO[0] = (total - u * jnp.sum(u * total, 1, keepdims=True)) * inv
    for k in ZO:
        send(GFO.at[0], GFO.at[k], ZA, dev(0, 0, 0, k))
    gf_out[mine, :] = GFO[0]
    arrived(GFO.at[pl.ds(1, NZ - 1)], ZA)
    for k in range(1, NZ):
        at = lax.rem(z + NZ - k, NZ) * 16
        gf_out[pl.ds(pl.multiple_of(at, 16), 16), :] = GFO[k]

    arrived(GPR.at[pl.ds(1, NX * NY * NC - 1)], GP)
    GPR[0] = GPS[dp]
    for dx in range(NX):
        for dc in range(NC):
            for p in range(2):
                total = GPR[(dx * NY + p) * NC + dc]
                for dy in range(p + 2, NY, 2):
                    total = total + GPR[(dx * NY + dy) * NC + dc]
                at = (lax.rem(x + NX - dx, NX) * 2 + lax.rem(y + p, 2)) * NC + lax.rem(c + dc, NC)
                gp_out[:, pl.ds(pl.multiple_of(at * KB, KB), KB)] = total

    @pl.when(c == 0)
    def _():
        sent(CS, UP)

    @pl.when(c == 1)
    def _():
        for i in range(ITERS):
            sent(XR.at[i], XX + i)
            sent(YR.at[i], YY + i)
            if i < last:
                sent(ZRV.at[i], ZZ + i)
        sent(ZL.at[pl.ds(1, NB * NZ - 1)], ZZ + last)
        sent(CF.at[last], DN)
        sent(RBM, RM)

    sent(TZR, TZ)
    sent(F.at[0], G0)
    sent(F.at[0], GY)
    for p in range(2):
        sent(F.at[p], GL + p)
        sent(F.at[p], GR + p)
        sent(F.at[4 + p], GF + p)
    sent(F.at[pl.ds(1, NB - 1)], G2)
    sent(TS.at[pl.ds(1, NB - 1)], T1)
    sent(TS.at[pl.ds(0, NB)], T2)
    sent(GPR.at[pl.ds(1, NX * NY * NC - 1)], GP)
    sent(GAR, AR)
    sent(GTR, TR)
    sent(GFO.at[pl.ds(1, NZ - 1)], ZA)


def place(features, protos, features_out, protos_out):
    features_out[...] = features[...]
    protos_out[...] = protos[...]


def shards(teacher, student, protos):
    f32, bf16 = jnp.float32, jnp.bfloat16
    vm = pltpu.VMEM
    scratch = [
        vm((B, D), bf16),
        vm((B, D), bf16),
        vm((D, K), bf16),
        vm((CH, D, 256), bf16),
        vm((TL, 2 * B, 128), f32),
        vm((TL, B, 128), f32),
        vm((2 * NB, 2 * B, D), f32),
        vm((2 * NB, B, KB), f32),
        vm((2 * NB, B, KB), f32),
        vm((2 * NB, D, B), bf16),
        vm((2 * NB, B, KB), bf16),
        vm((64, 4, KB), f32),
        vm((64, 4, KB), f32),
        vm((NZ, 16, D), f32),
        vm((NZ - 1, 16, D), f32),
        vm((NZ, 16, D), f32),
        vm((NZ - 1, 16, D), f32),
        vm((NZ, 16, D), f32),
        vm((B, D), f32),
        vm((TL, 128), f32),
        vm((TL, 128), f32),
        vm((ITERS, TL, 128), f32),
        vm((ITERS, NX - 1, TL, 128), f32),
        vm((ITERS, TL, 128), f32),
        vm((ITERS, NY - 1, TL, 128), f32),
        vm((ITERS, TL, 128), f32),
        vm((ITERS, 2, 128), f32),
        vm((ITERS - 1, NZ - 1, 2, 128), f32),
        vm((NB * NZ, 2, 128), f32),
        vm((1, 128), f32),
        vm((NZ - 1, 1, 128), f32),
        vm((2 * NB, 1, 128), f32),
        vm((2 * NB, 1, 128), f32),
        vm((2 * NB, 1, 128), f32),
        vm((2 * NB, B, 128), f32),
        vm((2 * B, 128), f32),
        vm((B, 128), f32),
        pltpu.SemaphoreType.DMA((2 + LOADS,)),
        pltpu.SemaphoreType.DMA((GROUPS,)),
        pltpu.SemaphoreType.DMA((GROUPS,)),
    ]
    whole = pl.BlockSpec(memory_space=pltpu.VMEM)
    anywhere = pl.BlockSpec(memory_space=pl.ANY)
    grads = pl.pallas_call(
        body,
        out_shape=(jax.ShapeDtypeStruct((B, D), f32), jax.ShapeDtypeStruct((4, K), f32)),
        in_specs=[anywhere] * 3,
        out_specs=(whole, whole),
        scratch_shapes=scratch,
        compiler_params=pltpu.CompilerParams(
            collective_id=0, has_side_effects=True, vmem_limit_bytes=60 * 2**20
        ),
    )(teacher, student, protos)
    return pl.pallas_call(
        place,
        out_shape=tuple(jax.ShapeDtypeStruct(g.shape, g.dtype) for g in grads),
        in_specs=[whole] * 2,
        out_specs=(whole,) * 2,
        compiler_params=pltpu.CompilerParams(vmem_limit_bytes=60 * 2**20),
    )(*grads)


def solution(mesh):
    placed = (P("dp", None), P("dp", None), P(None, "proto"))
    return jax.shard_map(
        shards,
        mesh=mesh,
        in_specs=placed,
        out_specs=(P("dp", None), P("dp", "proto")),
        check_vma=False,
    )
```

```python
import functools

import jax
import jax.numpy as jnp
from jax import lax
from jax.experimental import pallas as pl
from jax.experimental.pallas import tpu as pltpu
from jax.sharding import PartitionSpec as P

EPS = 1e-06
INV_T = 1.0 / 0.07
INV_S = 1.0 / 0.1
ITERS = 3
NX, NY, NC, NZ = 4, 8, 2, 8
B = 128
D = 256
K = 4096
CH = K // 256
TL = K // 128
NB = 2 * NX
KB = K // (NB * NC)
SCALE = 32768 / 64.0 / 0.1
MESH = pl.DeviceIdType.MESH

UP, DN, G0, GY, NO, TZ, T1, T2, RM, GP, AR, TR, ZA = range(13)
XX, YY, ZZ = (13, 16, 19)
GL, GR, GF, GH = (22, 24, 26, 28)
GROUPS = 31
PARTS = ((1, 2), (3, 2), (5, 3))
XO = (2, 1, 3)
YO = ZO = (4, 3, 5, 2, 6, 1, 7)
LOADS = 4


def dot(a, b):
    return jnp.dot(a, b, preferred_element_type=jnp.float32)


def unit_rows(raw):
    wide = raw.astype(jnp.float32)
    inv = lax.rsqrt(jnp.sum(wide * wide, 1, keepdims=True) + EPS)
    return (wide * inv).astype(jnp.bfloat16), inv


def across(row):
    return jnp.broadcast_to(row, (128, 128)).T


def body(
    t_hbm, s_hbm, w_hbm, gf_out, gp_out,
    t_ref, s_ref, w_ref, WU, E, SE, F, ETB, ESB, SBT, GB, GPS, GPR, GAS, GAR, GTS, GTR, GFO, GFA,
    CS, CR, XS, XR, YS, YR, CF, ZS, ZRV, ZL, TZS, TZR, TS, RB, RBM, ITB, RW, ITW, lsem, ssem, rsem, phase,
):
    dp = lax.axis_index("dp")
    z = lax.axis_index("proto")
    c = lax.rem(dp, 2)
    y = lax.rem(dp // 2, NY)
    x = dp // (2 * NY)

    def dev(dx, dy, dc, dz):
        return (
            (lax.rem(x + dx, NX) * NY + lax.rem(y + dy, NY)) * NC + lax.rem(c + dc, NC),
            lax.rem(z + dz, NZ),
        )

    mate = dev(0, 0, 1, 0)
    flip = NY + 1 - 2 * lax.rem(y, 2)

    def send(src, dst, group, to):
        pltpu.make_async_remote_copy(
            src, dst, ssem.at[group], rsem.at[group], device_id=to, device_id_type=MESH
        ).start()

    def arrived(ref, group):
        pltpu.make_async_remote_copy(
            ref, ref, ssem.at[group], rsem.at[group], device_id=mate, device_id_type=MESH
        ).wait_recv()

    def sent(ref, group):
        pltpu.make_async_remote_copy(
            ref, ref, ssem.at[group], rsem.at[group], device_id=mate, device_id_type=MESH
        ).wait_send()

    loads = [
        pltpu.make_async_copy(t_hbm, t_ref, lsem.at[0]),
        pltpu.make_async_copy(s_hbm, s_ref, lsem.at[1]),
    ]
    for piece in range(LOADS):
        cols = pl.ds(piece * (K // LOADS), K // LOADS)
        loads.append(pltpu.make_async_copy(w_hbm.at[:, cols], w_ref.at[:, cols], lsem.at[2 + piece]))
    for load in loads:
        load.start()

    peers = [dev(0, 0, 1, 0)]
    peers += [dev(k, 0, 0, 0) for k in range(1, NX)]
    peers += [dev(0, k, 0, 0) for k in range(1, NY)]
    peers += [dev(0, 0, 0, k) for k in range(1, NZ)]
    peers += [dev(k, flip, 0, 0) for k in range(1, NX)]
    barrier = pltpu.get_barrier_semaphore()
    for to in peers:
        pl.semaphore_signal(barrier, inc=1, device_id=to, device_id_type=MESH)

    loads[0].wait()
    t_unit, _ = unit_rows(t_ref[...])
    F[0, :B, :] = t_unit.astype(jnp.float32)

    def first(j, carry):
        w = w_ref[:, pl.ds(pl.multiple_of(j * 256, 256), 256)].astype(jnp.float32)
        w = (w * lax.rsqrt(jnp.sum(w * w, 0, keepdims=True) + EPS)).astype(jnp.bfloat16)
        WU[j] = w
        e = jnp.exp(dot(t_unit, w) * INV_T)
        E[2 * j, :B] = e[:, :128]
        E[2 * j + 1, :B] = e[:, 128:]
        CS[pl.ds(2 * j, 1), :] = jnp.sum(e[:, :128], 0, keepdims=True)
        CS[pl.ds(2 * j + 1, 1), :] = jnp.sum(e[:, 128:], 0, keepdims=True)
        return carry

    per = CH // LOADS
    for piece in range(LOADS):
        loads[2 + piece].wait()
        lax.fori_loop(piece * per, piece * per + per, first, 0, unroll=True)
    loads[1].wait()
    s_unit, _ = unit_rows(s_ref[...])
    F[0, B:, :] = s_unit.astype(jnp.float32)
    pl.semaphore_wait(barrier, len(peers))

    def student():
        def step(j, acc):
            e = jnp.exp(dot(F[0, B:, :].astype(jnp.bfloat16), WU[j]) * INV_S)
            SE[2 * j] = e[:, :128]
            SE[2 * j + 1] = e[:, 128:]
            return acc + e[:, :128] + e[:, 128:]

        acc = lax.fori_loop(0, CH, step, jnp.zeros((B, 128), jnp.float32), unroll=4)
        TZS[...] = jnp.sum(acc.T, 0, keepdims=True)
        for k in ZO:
            send(TZS, TZR.at[k - 1], TZ, dev(0, 0, 0, k))

    def product(tile, kept, got, group):
        def step(j, acc):
            g = jnp.concatenate([tile(2 * j), tile(2 * j + 1)], 1)
            high = g.astype(jnp.bfloat16)
            low = (g - high.astype(jnp.float32)).astype(jnp.bfloat16)
            return acc + lax.dot_general(
                jnp.concatenate([high, low], 0), WU[j], (((1,), (1,)), ((), ())), preferred_element_type=jnp.float32
            )

        acc = lax.fori_loop(0, CH, step, jnp.zeros((2 * B, D), jnp.float32), unroll=2)
        GFA[...] = acc[:B] + acc[B:]
        for k in range(NZ):
            kept[k] = GFA[16 * k:16 * k + 16, :]
        for k in ZO:
            send(kept.at[lax.rem(z + k, NZ)], got.at[k - 1], group, dev(0, 0, 0, k))

    def student_product():
        product(lambda t: SE[t] * ITW[...], GAS, GAR, AR)

    def teacher_product():
        product(lambda t: E[t, :B] * CF[ITERS - 1, pl.ds(t, 1), :], GTS, GTR, TR)

    def student_totals():
        arrived(TZR, TZ)
        total = TZS[...]
        for k in range(NZ - 1):
            total = total + TZR[k]
        TS[0] = SCALE / total
        ITW[...] = across(TS[0])
        for k in XO:
            for p in (1, 0):
                send(TS.at[0], TS.at[2 * k + p], T1, dev(k, flip * p, 0, 0))
        send(TS.at[0], TS.at[1], T1, dev(0, flip, 0, 0))

    def hand_totals():
        arrived(TS.at[pl.ds(1, NB - 1)], T1)
        send(TS.at[pl.ds(0, NB)], TS.at[pl.ds(NB, NB)], T2, mate)

    def line_totals():
        arrived(TS.at[pl.ds(NB, NB)], T2)
        for j in range(2 * NB):
            ITB[j] = across(TS[j])

    def to_sides(p):
        send(F.at[p], F.at[2 + p], GL + p, dev(1, 0, 0, 0))
        send(F.at[p], F.at[6 + p], GR + p, dev(3, 0, 0, 0))

    def relay(p):
        arrived(F.at[2 + p], GL + p)
        arrived(F.at[6 + p], GR + p)
        send(F.at[2 + p, pl.ds(0, B)], F.at[4 + p, pl.ds(0, B)], GF + p, dev(1, 0, 0, 0))
        send(F.at[6 + p, pl.ds(B, B)], F.at[4 + p, pl.ds(B, B)], GF + p, dev(3, 0, 0, 0))

    def to_pair():
        send(F.at[0], F.at[1], GY, dev(0, flip, 0, 0))

    def second_row():
        arrived(F.at[1], GY)
        to_sides(1)
        relay(0)

    def hand(part):
        lo, count = PARTS[part]
        send(F.at[pl.ds(lo, count)], F.at[pl.ds(NB + lo, count)], GH + part, mate)

    def handed(part):
        lo, count = PARTS[part]
        arrived(F.at[pl.ds(NB + lo, count)], GH + part)
        blocks(NB + lo, NB + lo + count)

    def idle(point):
        pl.semaphore_signal(phase.at[point], inc=1, device_id=mate, device_id_type=MESH)

    def when_idle(point):
        pl.semaphore_wait(phase.at[point], 1)

    own = (x * 2 + lax.rem(y, 2)) * NC + c

    def line_block(j, carry):
        tb = F[j, :B, :].astype(jnp.bfloat16)
        sw = F[j, B:, :]
        SBT[j] = sw.T.astype(jnp.bfloat16)
        ETB[j] = jnp.exp(dot(tb, WU[own]) * INV_T)
        ESB[j] = jnp.exp(dot(sw.astype(jnp.bfloat16), WU[own]) * INV_S)
        return carry

    def blocks(lo, hi):
        lax.fori_loop(lo, hi, line_block, 0)

    last = ITERS - 1

    @pl.when(c == 0)
    def _():
        send(CS, CR, UP, mate)
        send(F.at[0], F.at[NB], G0, mate)
        student()
        when_idle(0)
        to_sides(0)
        student_totals()
        when_idle(1)
        to_pair()
        arrived(F.at[NB], G0)
        blocks(NB, NB + 1)
        blocks(0, 1)
        hand_totals()
        when_idle(2)
        second_row()
        student_product()
        hand(0)
        blocks(1, 3)
        line_totals()
        arrived(F.at[4], GF)
        blocks(4, 5)
        when_idle(3)
        relay(1)
        hand(1)
        blocks(3, 4)
        blocks(6, 8)
        arrived(F.at[5], GF + 1)
        hand(2)
        blocks(5, 6)
        for part in range(3):
            handed(part)
        arrived(CF.at[last], DN)
        teacher_product()
        arrived(RB, RM)

    @pl.when(c == 1)
    def _():
        def mate_exp(j, carry):
            e = jnp.exp(dot(F[NB, :B, :].astype(jnp.bfloat16), WU[j]) * INV_T)
            E[2 * j, B:] = e[:, :128]
            E[2 * j + 1, B:] = e[:, 128:]
            return carry

        for i in range(ITERS):
            if i == 0:
                send(F.at[0], F.at[NB], G0, mate)
                arrived(CR, UP)
                XS[0] = CS[...] + CR[...]
            for k in XO:
                send(XS.at[i], XR.at[i, k - 1], XX + i, dev(k, 0, 0, 0))
            if i == 0:
                arrived(F.at[NB], G0)
                lax.fori_loop(0, CH, mate_exp, 0, unroll=4)
            elif i == 1:
                blocks(0, 1)
                blocks(NB, NB + 1)
                hand_totals()
            else:
                hand(0)
                blocks(1, 3)
            arrived(XR.at[i], XX + i)
            YS[i] = (XS[i] + XR[i, 0]) + (XR[i, 1] + XR[i, 2])
            for k in YO:
                send(YS.at[i], YR.at[i, k - 1], YY + i, dev(0, k, 0, 0))
            if i == 0:
                idle(0)
                to_sides(0)
                student()
            elif i == 1:
                idle(2)
                second_row()
                student_product()
            else:
                idle(3)
                relay(1)
                arrived(F.at[4], GF)
                hand(1)
                blocks(3, 5)
                blocks(6, 8)
                handed(0)
            arrived(YR.at[i], YY + i)
            total = YS[i]
            for k in range(NY - 1):
                total = total + YR[i, k]
            CF[i] = 1.0 / total
            if i == last:
                send(CF.at[last], CF.at[last], DN, mate)

            def step(t, acc):
                return acc + E[t] * CF[i, pl.ds(t, 1), :]

            acc = lax.fori_loop(0, TL, step, jnp.zeros((2 * B, 128), jnp.float32), unroll=4)
            ZS[i, 0:1, :] = jnp.sum(acc[:B].T, 0, keepdims=True)
            ZS[i, 1:2, :] = jnp.sum(acc[B:].T, 0, keepdims=True)
            if i < last:
                for k in ZO:
                    send(ZS.at[i], ZRV.at[i, k - 1], ZZ + i, dev(0, 0, 0, k))
                if i == 0:
                    idle(1)
                    to_pair()
                    student_totals()
                else:
                    line_totals()
                arrived(ZRV.at[i], ZZ + i)
                total = ZS[i]
                for k in range(NZ - 1):
                    total = total + ZRV[i, k]
                inv = 1.0 / total
                RW[:B] = across(inv[0:1])
                RW[B:] = across(inv[1:2])

                def scaled(t, carry):
                    e = E[t] * RW[...]
                    XS[i + 1, pl.ds(t, 1), :] = jnp.sum(e[:B] + e[B:], 0, keepdims=True)
                    return carry

                lax.fori_loop(0, TL, scaled, 0, unroll=4)
            else:
                far = lambda k: -(min(k // (2 * NZ), NX - k // (2 * NZ)) + k // NZ % 2 + min(k % NZ, NZ - k % NZ))
                for k in sorted(range(1, NB * NZ), key=far):
                    to = dev(k // (2 * NZ), flip * (k // NZ % 2), 0, k % NZ)
                    send(ZS.at[i], ZL.at[k], ZZ + i, to)
                ZL[0] = ZS[i]
                teacher_product()
                arrived(F.at[5], GF + 1)
                hand(2)
                blocks(5, 6)
                handed(1)
                handed(2)
                arrived(ZL.at[pl.ds(1, NB * NZ - 1)], ZZ + i)
                for j in range(NB):
                    total = ZL[j * NZ]
                    for dz in range(1, NZ):
                        total = total + ZL[j * NZ + dz]
                    inv = 1.0 / total
                    RB[j] = inv[0:1]
                    RB[NB + j] = inv[1:2]
                    RBM[j] = inv[1:2]
                    RBM[NB + j] = inv[0:1]
                send(RBM, RB, RM, mate)

    def line_grad(j, carry):
        rb = across(RB[j] * SCALE)
        for q in range(KB // 128):
            part = pl.ds(128 * q, 128)
            col = CF[last, pl.ds(own * (KB // 128) + q, 1), :]
            g = ESB[j, :, part] * ITB[j] - (ETB[j, :, part] * col) * rb
            GB[j, :, 128 * q:128 * q + 128] = g.astype(jnp.bfloat16)
        return carry

    lax.fori_loop(0, 2 * NB, line_grad, 0, unroll=4)
    acc = jnp.zeros((D, KB), jnp.float32)
    for p in range(NB):
        lhs = jnp.concatenate([SBT[2 * p], SBT[2 * p + 1]], 1)
        acc = acc + dot(lhs, jnp.concatenate([GB[2 * p], GB[2 * p + 1]], 0))
    GPS[...] = acc.reshape(D // 4, 4, KB)

    for dy in YO + (0,):
        def scatter(i, carry):
            to = dev(i // NC, dy, lax.rem(i, NC), 0)
            send(GPS.at[to[0]], GPR.at[i // NC * (NY * NC) + dy * NC + lax.rem(i, NC)], GP, to)
            return carry

        lax.fori_loop(0 if dy else 1, NX * NC, scatter, 0)

    RW[:B] = across(RB[0] * SCALE)
    mine = pl.ds(pl.multiple_of(z * 16, 16), 16)
    u, inv = unit_rows(s_ref[mine, :])
    u = u.astype(jnp.float32)
    arrived(GAR, AR)
    arrived(GTR, TR)
    total, teach = GAS[z], GTS[z]
    for k in range(NZ - 1):
        total = total + GAR[k]
        teach = teach + GTR[k]
    total = total - teach * RW[mine, 0:1]
    GFO[0] = (total - u * jnp.sum(u * total, 1, keepdims=True)) * inv
    for k in ZO:
        send(GFO.at[0], GFO.at[k], ZA, dev(0, 0, 0, k))
    gf_out[mine, :] = GFO[0]
    arrived(GFO.at[pl.ds(1, NZ - 1)], ZA)
    for k in range(1, NZ):
        at = lax.rem(z + NZ - k, NZ) * 16
        gf_out[pl.ds(pl.multiple_of(at, 16), 16), :] = GFO[k]

    arrived(GPR.at[pl.ds(1, NX * NY * NC - 1)], GP)
    GPR[0] = GPS[dp]
    for dx in range(NX):
        for dc in range(NC):
            for p in range(2):
                total = GPR[(dx * NY + p) * NC + dc]
                for dy in range(p + 2, NY, 2):
                    total = total + GPR[(dx * NY + dy) * NC + dc]
                at = (lax.rem(x + NX - dx, NX) * 2 + lax.rem(y + p, 2)) * NC + lax.rem(c + dc, NC)
                gp_out[:, pl.ds(pl.multiple_of(at * KB, KB), KB)] = total

    @pl.when(c == 0)
    def _():
        sent(CS, UP)

    @pl.when(c == 1)
    def _():
        for i in range(ITERS):
            sent(XR.at[i], XX + i)
            sent(YR.at[i], YY + i)
            if i < last:
                sent(ZRV.at[i], ZZ + i)
        sent(ZL.at[pl.ds(1, NB * NZ - 1)], ZZ + last)
        sent(CF.at[last], DN)
        sent(RBM, RM)

    sent(TZR, TZ)
    sent(F.at[0], G0)
    sent(F.at[0], GY)
    for p in range(2):
        sent(F.at[p], GL + p)
        sent(F.at[p], GR + p)
        sent(F.at[4 + p], GF + p)
    for part, (lo, count) in enumerate(PARTS):
        sent(F.at[pl.ds(lo, count)], GH + part)
    sent(TS.at[pl.ds(1, NB - 1)], T1)
    sent(TS.at[pl.ds(0, NB)], T2)
    sent(GPR.at[pl.ds(1, NX * NY * NC - 1)], GP)
    sent(GAR, AR)
    sent(GTR, TR)
    sent(GFO.at[pl.ds(1, NZ - 1)], ZA)


def place(features, protos, features_out, protos_out):
    features_out[...] = features[...]
    protos_out[...] = protos[...]


def shards(teacher, student, protos):
    f32, bf16 = jnp.float32, jnp.bfloat16
    vm = pltpu.VMEM
    scratch = [
        vm((B, D), bf16),
        vm((B, D), bf16),
        vm((D, K), bf16),
        vm((CH, D, 256), bf16),
        vm((TL, 2 * B, 128), f32),
        vm((TL, B, 128), f32),
        vm((2 * NB, 2 * B, D), f32),
        vm((2 * NB, B, KB), f32),
        vm((2 * NB, B, KB), f32),
        vm((2 * NB, D, B), bf16),
        vm((2 * NB, B, KB), bf16),
        vm((64, 4, KB), f32),
        vm((64, 4, KB), f32),
        vm((NZ, 16, D), f32),
        vm((NZ - 1, 16, D), f32),
        vm((NZ, 16, D), f32),
        vm((NZ - 1, 16, D), f32),
        vm((NZ, 16, D), f32),
        vm((B, D), f32),
        vm((TL, 128), f32),
        vm((TL, 128), f32),
        vm((ITERS, TL, 128), f32),
        vm((ITERS, NX - 1, TL, 128), f32),
        vm((ITERS, TL, 128), f32),
        vm((ITERS, NY - 1, TL, 128), f32),
        vm((ITERS, TL, 128), f32),
        vm((ITERS, 2, 128), f32),
        vm((ITERS - 1, NZ - 1, 2, 128), f32),
        vm((NB * NZ, 2, 128), f32),
        vm((1, 128), f32),
        vm((NZ - 1, 1, 128), f32),
        vm((2 * NB, 1, 128), f32),
        vm((2 * NB, 1, 128), f32),
        vm((2 * NB, 1, 128), f32),
        vm((2 * NB, B, 128), f32),
        vm((2 * B, 128), f32),
        vm((B, 128), f32),
        pltpu.SemaphoreType.DMA((2 + LOADS,)),
        pltpu.SemaphoreType.DMA((GROUPS,)),
        pltpu.SemaphoreType.DMA((GROUPS,)),
        pltpu.SemaphoreType.REGULAR((4,)),
    ]
    whole = pl.BlockSpec(memory_space=pltpu.VMEM)
    anywhere = pl.BlockSpec(memory_space=pl.ANY)
    grads = pl.pallas_call(
        body,
        out_shape=(jax.ShapeDtypeStruct((B, D), f32), jax.ShapeDtypeStruct((4, K), f32)),
        in_specs=[anywhere] * 3,
        out_specs=(whole, whole),
        scratch_shapes=scratch,
        compiler_params=pltpu.CompilerParams(
            collective_id=0, has_side_effects=True, vmem_limit_bytes=60 * 2**20
        ),
    )(teacher, student, protos)
    return pl.pallas_call(
        place,
        out_shape=tuple(jax.ShapeDtypeStruct(g.shape, g.dtype) for g in grads),
        in_specs=[whole] * 2,
        out_specs=(whole,) * 2,
        compiler_params=pltpu.CompilerParams(vmem_limit_bytes=60 * 2**20),
    )(*grads)


def solution(mesh):
    placed = (P("dp", None), P("dp", None), P(None, "proto"))
    return jax.shard_map(
        shards,
        mesh=mesh,
        in_specs=placed,
        out_specs=(P("dp", None), P("dp", "proto")),
        check_vma=False,
    )
```

```python
import functools

import jax
import jax.numpy as jnp
from jax import lax
from jax.experimental import pallas as pl
from jax.experimental.pallas import tpu as pltpu
from jax.sharding import PartitionSpec as P

EPS = 1e-06
INV_T = 1.0 / 0.07
INV_S = 1.0 / 0.1
ITERS = 3
NX, NY, NC, NZ = 4, 8, 2, 8
B = 128
D = 256
K = 4096
CH = K // 256
TL = K // 128
NB = 2 * NX
KB = K // (NB * NC)
SCALE = 32768 / 64.0 / 0.1
MESH = pl.DeviceIdType.MESH

UP, DN, G0, GY, NO, TZ, T1, T2, RM, GP, AR, TR, ZA = range(13)
XX, YY, ZZ = (13, 16, 19)
GL, GR, GF, GH = (22, 24, 26, 28)
GROUPS = 31
PARTS = ((1, 2), (3, 2), (5, 3))
XO = (2, 1, 3)
YO = ZO = (4, 3, 5, 2, 6, 1, 7)
LOADS = 4


def dot(a, b):
    return jnp.dot(a, b, preferred_element_type=jnp.float32)


def unit_rows(raw):
    wide = raw.astype(jnp.float32)
    inv = lax.rsqrt(jnp.sum(wide * wide, 1, keepdims=True) + EPS)
    return (wide * inv).astype(jnp.bfloat16), inv


def across(row):
    return jnp.broadcast_to(row, (128, 128)).T


def body(
    t_hbm, s_hbm, w_hbm, gf_out, gp_out,
    t_ref, s_ref, w_ref, WU, E, SE, F, ETB, ESB, SBT, GB, GPS, GPR, GAS, GAR, GTS, GTR, GFO, GFA,
    CS, CR, XS, XR, YS, YR, CF, ZS, ZRV, ZL, TZS, TZR, TS, RB, RBM, ITB, RW, ITW, lsem, ssem, rsem, phase,
):
    dp = lax.axis_index("dp")
    z = lax.axis_index("proto")
    c = lax.rem(dp, 2)
    y = lax.rem(dp // 2, NY)
    x = dp // (2 * NY)

    def dev(dx, dy, dc, dz):
        return (
            (lax.rem(x + dx, NX) * NY + lax.rem(y + dy, NY)) * NC + lax.rem(c + dc, NC),
            lax.rem(z + dz, NZ),
        )

    mate = dev(0, 0, 1, 0)
    flip = NY + 1 - 2 * lax.rem(y, 2)

    def send(src, dst, group, to):
        pltpu.make_async_remote_copy(
            src, dst, ssem.at[group], rsem.at[group], device_id=to, device_id_type=MESH
        ).start()

    def arrived(ref, group):
        pltpu.make_async_remote_copy(
            ref, ref, ssem.at[group], rsem.at[group], device_id=mate, device_id_type=MESH
        ).wait_recv()

    def sent(ref, group):
        pltpu.make_async_remote_copy(
            ref, ref, ssem.at[group], rsem.at[group], device_id=mate, device_id_type=MESH
        ).wait_send()

    loads = [pltpu.make_async_copy(t_hbm, t_ref, lsem.at[0])]
    for piece in range(LOADS):
        cols = pl.ds(piece * (K // LOADS), K // LOADS)
        loads.append(pltpu.make_async_copy(w_hbm.at[:, cols], w_ref.at[:, cols], lsem.at[1 + piece]))
    loads.append(pltpu.make_async_copy(s_hbm, s_ref, lsem.at[1 + LOADS]))
    for load in loads:
        load.start()

    peers = [dev(0, 0, 1, 0)]
    peers += [dev(k, 0, 0, 0) for k in range(1, NX)]
    peers += [dev(0, k, 0, 0) for k in range(1, NY)]
    peers += [dev(0, 0, 0, k) for k in range(1, NZ)]
    peers += [dev(k, flip, 0, 0) for k in range(1, NX)]
    barrier = pltpu.get_barrier_semaphore()
    for to in peers:
        pl.semaphore_signal(barrier, inc=1, device_id=to, device_id_type=MESH)

    loads[0].wait()
    t_unit, _ = unit_rows(t_ref[...])
    F[0, :B, :] = t_unit.astype(jnp.float32)

    def first(j, carry):
        w = w_ref[:, pl.ds(pl.multiple_of(j * 256, 256), 256)].astype(jnp.float32)
        w = (w * lax.rsqrt(jnp.sum(w * w, 0, keepdims=True) + EPS)).astype(jnp.bfloat16)
        WU[j] = w
        e = jnp.exp(dot(t_unit, w) * INV_T)
        E[2 * j, :B] = e[:, :128]
        E[2 * j + 1, :B] = e[:, 128:]
        CS[pl.ds(2 * j, 1), :] = jnp.sum(e[:, :128], 0, keepdims=True)
        CS[pl.ds(2 * j + 1, 1), :] = jnp.sum(e[:, 128:], 0, keepdims=True)
        return carry

    per = CH // LOADS
    for piece in range(LOADS):
        loads[1 + piece].wait()
        lax.fori_loop(piece * per, piece * per + per, first, 0, unroll=True)
    loads[1 + LOADS].wait()
    s_unit, _ = unit_rows(s_ref[...])
    F[0, B:, :] = s_unit.astype(jnp.float32)
    pl.semaphore_wait(barrier, len(peers))

    def student():
        def step(j, acc):
            e = jnp.exp(dot(F[0, B:, :].astype(jnp.bfloat16), WU[j]) * INV_S)
            SE[2 * j] = e[:, :128]
            SE[2 * j + 1] = e[:, 128:]
            return acc + e[:, :128] + e[:, 128:]

        acc = lax.fori_loop(0, CH, step, jnp.zeros((B, 128), jnp.float32), unroll=4)
        TZS[...] = jnp.sum(acc.T, 0, keepdims=True)
        for k in ZO:
            send(TZS, TZR.at[k - 1], TZ, dev(0, 0, 0, k))

    def product(tile, kept, got, group):
        def step(j, acc):
            g = jnp.concatenate([tile(2 * j), tile(2 * j + 1)], 1)
            high = g.astype(jnp.bfloat16)
            low = (g - high.astype(jnp.float32)).astype(jnp.bfloat16)
            return acc + lax.dot_general(
                jnp.concatenate([high, low], 0), WU[j], (((1,), (1,)), ((), ())), preferred_element_type=jnp.float32
            )

        acc = lax.fori_loop(0, CH, step, jnp.zeros((2 * B, D), jnp.float32), unroll=4)
        GFA[...] = acc[:B] + acc[B:]
        for k in range(NZ):
            kept[k] = GFA[16 * k:16 * k + 16, :]
        for k in ZO:
            send(kept.at[lax.rem(z + k, NZ)], got.at[k - 1], group, dev(0, 0, 0, k))

    def student_product():
        product(lambda t: SE[t] * ITW[...], GAS, GAR, AR)

    def teacher_product():
        product(lambda t: E[t, :B] * CF[ITERS - 1, pl.ds(t, 1), :], GTS, GTR, TR)

    def student_totals():
        arrived(TZR, TZ)
        total = TZS[...]
        for k in range(NZ - 1):
            total = total + TZR[k]
        TS[0] = SCALE / total
        ITW[...] = across(TS[0])
        for k in XO:
            for p in (1, 0):
                send(TS.at[0], TS.at[2 * k + p], T1, dev(k, flip * p, 0, 0))
        send(TS.at[0], TS.at[1], T1, dev(0, flip, 0, 0))

    def hand_totals():
        arrived(TS.at[pl.ds(1, NB - 1)], T1)
        send(TS.at[pl.ds(0, NB)], TS.at[pl.ds(NB, NB)], T2, mate)

    def line_totals():
        arrived(TS.at[pl.ds(NB, NB)], T2)
        for j in range(2 * NB):
            ITB[j] = across(TS[j])

    def to_sides(p):
        send(F.at[p], F.at[2 + p], GL + p, dev(1, 0, 0, 0))
        send(F.at[p], F.at[6 + p], GR + p, dev(3, 0, 0, 0))

    def relay(p):
        arrived(F.at[2 + p], GL + p)
        arrived(F.at[6 + p], GR + p)
        send(F.at[2 + p, pl.ds(0, B)], F.at[4 + p, pl.ds(0, B)], GF + p, dev(1, 0, 0, 0))
        send(F.at[6 + p, pl.ds(B, B)], F.at[4 + p, pl.ds(B, B)], GF + p, dev(3, 0, 0, 0))

    def to_pair():
        send(F.at[0], F.at[1], GY, dev(0, flip, 0, 0))

    def second_row():
        arrived(F.at[1], GY)
        to_sides(1)
        relay(0)

    def hand(part):
        lo, count = PARTS[part]
        send(F.at[pl.ds(lo, count)], F.at[pl.ds(NB + lo, count)], GH + part, mate)

    def handed(part):
        lo, count = PARTS[part]
        arrived(F.at[pl.ds(NB + lo, count)], GH + part)
        blocks(NB + lo, NB + lo + count)

    def idle(point):
        pl.semaphore_signal(phase.at[point], inc=1, device_id=mate, device_id_type=MESH)

    def when_idle(point):
        pl.semaphore_wait(phase.at[point], 1)

    own = (x * 2 + lax.rem(y, 2)) * NC + c

    def line_block(j, carry):
        tb = F[j, :B, :].astype(jnp.bfloat16)
        sw = F[j, B:, :]
        SBT[j] = sw.T.astype(jnp.bfloat16)
        ETB[j] = jnp.exp(dot(tb, WU[own]) * INV_T)
        ESB[j] = jnp.exp(dot(sw.astype(jnp.bfloat16), WU[own]) * INV_S)
        return carry

    def blocks(lo, hi):
        lax.fori_loop(lo, hi, line_block, 0)

    last = ITERS - 1

    @pl.when(c == 0)
    def _():
        send(CS, CR, UP, mate)
        send(F.at[0], F.at[NB], G0, mate)
        student()
        when_idle(0)
        to_sides(0)
        student_totals()
        when_idle(1)
        to_pair()
        arrived(F.at[NB], G0)
        blocks(NB, NB + 1)
        blocks(0, 1)
        hand_totals()
        when_idle(2)
        second_row()
        student_product()
        hand(0)
        blocks(1, 3)
        line_totals()
        arrived(F.at[4], GF)
        blocks(4, 5)
        when_idle(3)
        relay(1)
        hand(1)
        blocks(3, 4)
        blocks(6, 8)
        arrived(F.at[5], GF + 1)
        hand(2)
        blocks(5, 6)
        handed(0)
        arrived(CF.at[last], DN)
        teacher_product()
        handed(1)
        handed(2)
        arrived(RB, RM)

    @pl.when(c == 1)
    def _():
        def mate_exp(j, carry):
            e = jnp.exp(dot(F[NB, :B, :].astype(jnp.bfloat16), WU[j]) * INV_T)
            E[2 * j, B:] = e[:, :128]
            E[2 * j + 1, B:] = e[:, 128:]
            return carry

        for i in range(ITERS):
            if i == 0:
                send(F.at[0], F.at[NB], G0, mate)
                arrived(CR, UP)
                XS[0] = CS[...] + CR[...]
            for k in XO:
                send(XS.at[i], XR.at[i, k - 1], XX + i, dev(k, 0, 0, 0))
            if i == 0:
                arrived(F.at[NB], G0)
                lax.fori_loop(0, CH, mate_exp, 0, unroll=4)
            elif i == 1:
                blocks(0, 1)
                blocks(NB, NB + 1)
                hand_totals()
            else:
                hand(0)
                blocks(1, 3)
            arrived(XR.at[i], XX + i)
            YS[i] = (XS[i] + XR[i, 0]) + (XR[i, 1] + XR[i, 2])
            for k in YO:
                send(YS.at[i], YR.at[i, k - 1], YY + i, dev(0, k, 0, 0))
            if i == 0:
                idle(0)
                to_sides(0)
                student()
            elif i == 1:
                idle(2)
                second_row()
                student_product()
            else:
                idle(3)
                relay(1)
                arrived(F.at[4], GF)
                hand(1)
                blocks(3, 5)
                blocks(6, 8)
                handed(0)
            arrived(YR.at[i], YY + i)
            total = YS[i]
            for k in range(NY - 1):
                total = total + YR[i, k]
            CF[i] = 1.0 / total
            if i == last:
                send(CF.at[last], CF.at[last], DN, mate)

            def step(t, acc):
                return acc + E[t] * CF[i, pl.ds(t, 1), :]

            acc = lax.fori_loop(0, TL, step, jnp.zeros((2 * B, 128), jnp.float32), unroll=8)
            ZS[i, 0:1, :] = jnp.sum(acc[:B].T, 0, keepdims=True)
            ZS[i, 1:2, :] = jnp.sum(acc[B:].T, 0, keepdims=True)
            if i < last:
                for k in ZO:
                    send(ZS.at[i], ZRV.at[i, k - 1], ZZ + i, dev(0, 0, 0, k))
                if i == 0:
                    idle(1)
                    to_pair()
                    student_totals()
                else:
                    line_totals()
                arrived(ZRV.at[i], ZZ + i)
                total = ZS[i]
                for k in range(NZ - 1):
                    total = total + ZRV[i, k]
                inv = 1.0 / total
                RW[:B] = across(inv[0:1])
                RW[B:] = across(inv[1:2])

                def scaled(t, carry):
                    e = E[t] * RW[...]
                    XS[i + 1, pl.ds(t, 1), :] = jnp.sum(e[:B] + e[B:], 0, keepdims=True)
                    return carry

                lax.fori_loop(0, TL, scaled, 0, unroll=8)
            else:
                far = lambda k: -(min(k // (2 * NZ), NX - k // (2 * NZ)) + k // NZ % 2 + min(k % NZ, NZ - k % NZ))
                for k in sorted(range(1, NB * NZ), key=far):
                    to = dev(k // (2 * NZ), flip * (k // NZ % 2), 0, k % NZ)
                    send(ZS.at[i], ZL.at[k], ZZ + i, to)
                ZL[0] = ZS[i]
                arrived(F.at[5], GF + 1)
                hand(2)
                teacher_product()
                blocks(5, 6)
                handed(1)
                handed(2)
                arrived(ZL.at[pl.ds(1, NB * NZ - 1)], ZZ + i)
                for j in range(NB):
                    total = ZL[j * NZ]
                    for dz in range(1, NZ):
                        total = total + ZL[j * NZ + dz]
                    inv = 1.0 / total
                    RB[j] = inv[0:1]
                    RB[NB + j] = inv[1:2]
                    RBM[j] = inv[1:2]
                    RBM[NB + j] = inv[0:1]
                send(RBM, RB, RM, mate)

    def line_grad(j, carry):
        rb = across(RB[j] * SCALE)
        for q in range(KB // 128):
            part = pl.ds(128 * q, 128)
            col = CF[last, pl.ds(own * (KB // 128) + q, 1), :]
            g = ESB[j, :, part] * ITB[j] - (ETB[j, :, part] * col) * rb
            GB[j, :, 128 * q:128 * q + 128] = g.astype(jnp.bfloat16)
        return carry

    lax.fori_loop(0, 2 * NB, line_grad, 0, unroll=True)
    acc = jnp.zeros((D, KB), jnp.float32)
    for p in range(NB):
        lhs = jnp.concatenate([SBT[2 * p], SBT[2 * p + 1]], 1)
        acc = acc + dot(lhs, jnp.concatenate([GB[2 * p], GB[2 * p + 1]], 0))
    GPS[...] = acc.reshape(D // 4, 4, KB)

    for dy in YO + (0,):
        def scatter(i, carry):
            to = dev(i // NC, dy, lax.rem(i, NC), 0)
            send(GPS.at[to[0]], GPR.at[i // NC * (NY * NC) + dy * NC + lax.rem(i, NC)], GP, to)
            return carry

        lax.fori_loop(0 if dy else 1, NX * NC, scatter, 0)

    RW[:B] = across(RB[0] * SCALE)
    mine = pl.ds(pl.multiple_of(z * 16, 16), 16)
    u, inv = unit_rows(s_ref[mine, :])
    u = u.astype(jnp.float32)
    arrived(GAR, AR)
    arrived(GTR, TR)
    total, teach = GAS[z], GTS[z]
    for k in range(NZ - 1):
        total = total + GAR[k]
        teach = teach + GTR[k]
    total = total - teach * RW[mine, 0:1]
    GFO[0] = (total - u * jnp.sum(u * total, 1, keepdims=True)) * inv
    for k in ZO:
        send(GFO.at[0], GFO.at[k], ZA, dev(0, 0, 0, k))
    gf_out[mine, :] = GFO[0]
    arrived(GFO.at[pl.ds(1, NZ - 1)], ZA)
    for k in range(1, NZ):
        at = lax.rem(z + NZ - k, NZ) * 16
        gf_out[pl.ds(pl.multiple_of(at, 16), 16), :] = GFO[k]

    arrived(GPR.at[pl.ds(1, NX * NY * NC - 1)], GP)
    GPR[0] = GPS[dp]
    for dx in range(NX):
        for dc in range(NC):
            for p in range(2):
                total = GPR[(dx * NY + p) * NC + dc]
                for dy in range(p + 2, NY, 2):
                    total = total + GPR[(dx * NY + dy) * NC + dc]
                at = (lax.rem(x + NX - dx, NX) * 2 + lax.rem(y + p, 2)) * NC + lax.rem(c + dc, NC)
                gp_out[:, pl.ds(pl.multiple_of(at * KB, KB), KB)] = total

    @pl.when(c == 0)
    def _():
        sent(CS, UP)

    @pl.when(c == 1)
    def _():
        for i in range(ITERS):
            sent(XR.at[i], XX + i)
            sent(YR.at[i], YY + i)
            if i < last:
                sent(ZRV.at[i], ZZ + i)
        sent(ZL.at[pl.ds(1, NB * NZ - 1)], ZZ + last)
        sent(CF.at[last], DN)
        sent(RBM, RM)

    sent(TZR, TZ)
    sent(F.at[0], G0)
    sent(F.at[0], GY)
    for p in range(2):
        sent(F.at[p], GL + p)
        sent(F.at[p], GR + p)
        sent(F.at[4 + p], GF + p)
    for part, (lo, count) in enumerate(PARTS):
        sent(F.at[pl.ds(lo, count)], GH + part)
    sent(TS.at[pl.ds(1, NB - 1)], T1)
    sent(TS.at[pl.ds(0, NB)], T2)
    sent(GPR.at[pl.ds(1, NX * NY * NC - 1)], GP)
    sent(GAR, AR)
    sent(GTR, TR)
    sent(GFO.at[pl.ds(1, NZ - 1)], ZA)


def place(features, protos, features_out, protos_out):
    features_out[...] = features[...]
    protos_out[...] = protos[...]


def shards(teacher, student, protos):
    f32, bf16 = jnp.float32, jnp.bfloat16
    vm = pltpu.VMEM
    scratch = [
        vm((B, D), bf16),
        vm((B, D), bf16),
        vm((D, K), bf16),
        vm((CH, D, 256), bf16),
        vm((TL, 2 * B, 128), f32),
        vm((TL, B, 128), f32),
        vm((2 * NB, 2 * B, D), f32),
        vm((2 * NB, B, KB), f32),
        vm((2 * NB, B, KB), f32),
        vm((2 * NB, D, B), bf16),
        vm((2 * NB, B, KB), bf16),
        vm((64, 4, KB), f32),
        vm((64, 4, KB), f32),
        vm((NZ, 16, D), f32),
        vm((NZ - 1, 16, D), f32),
        vm((NZ, 16, D), f32),
        vm((NZ - 1, 16, D), f32),
        vm((NZ, 16, D), f32),
        vm((B, D), f32),
        vm((TL, 128), f32),
        vm((TL, 128), f32),
        vm((ITERS, TL, 128), f32),
        vm((ITERS, NX - 1, TL, 128), f32),
        vm((ITERS, TL, 128), f32),
        vm((ITERS, NY - 1, TL, 128), f32),
        vm((ITERS, TL, 128), f32),
        vm((ITERS, 2, 128), f32),
        vm((ITERS - 1, NZ - 1, 2, 128), f32),
        vm((NB * NZ, 2, 128), f32),
        vm((1, 128), f32),
        vm((NZ - 1, 1, 128), f32),
        vm((2 * NB, 1, 128), f32),
        vm((2 * NB, 1, 128), f32),
        vm((2 * NB, 1, 128), f32),
        vm((2 * NB, B, 128), f32),
        vm((2 * B, 128), f32),
        vm((B, 128), f32),
        pltpu.SemaphoreType.DMA((2 + LOADS,)),
        pltpu.SemaphoreType.DMA((GROUPS,)),
        pltpu.SemaphoreType.DMA((GROUPS,)),
        pltpu.SemaphoreType.REGULAR((4,)),
    ]
    whole = pl.BlockSpec(memory_space=pltpu.VMEM)
    anywhere = pl.BlockSpec(memory_space=pl.ANY)
    grads = pl.pallas_call(
        body,
        out_shape=(jax.ShapeDtypeStruct((B, D), f32), jax.ShapeDtypeStruct((4, K), f32)),
        in_specs=[anywhere] * 3,
        out_specs=(whole, whole),
        scratch_shapes=scratch,
        compiler_params=pltpu.CompilerParams(
            collective_id=0, has_side_effects=True, vmem_limit_bytes=60 * 2**20
        ),
    )(teacher, student, protos)
    return pl.pallas_call(
        place,
        out_shape=tuple(jax.ShapeDtypeStruct(g.shape, g.dtype) for g in grads),
        in_specs=[whole] * 2,
        out_specs=(whole,) * 2,
        compiler_params=pltpu.CompilerParams(vmem_limit_bytes=60 * 2**20),
    )(*grads)


def solution(mesh):
    placed = (P("dp", None), P("dp", None), P(None, "proto"))
    return jax.shard_map(
        shards,
        mesh=mesh,
        in_specs=placed,
        out_specs=(P("dp", None), P("dp", "proto")),
        check_vma=False,
    )
```

```python
import functools

import jax
import jax.numpy as jnp
from jax import lax
from jax.experimental import pallas as pl
from jax.experimental.pallas import tpu as pltpu
from jax.sharding import PartitionSpec as P

EPS = 1e-06
INV_T = 1.0 / 0.07
INV_S = 1.0 / 0.1
ITERS = 3
NX, NY, NC, NZ = 4, 8, 2, 8
B = 128
D = 256
K = 4096
CH = K // 256
TL = K // 128
NB = 2 * NX
KB = K // (NB * NC)
SCALE = 32768 / 64.0 / 0.1
MESH = pl.DeviceIdType.MESH

UP, DN, G0, GY, NO, TZ, T1, T2, RM, GP, AR, TR, ZA = range(13)
XX, YY, ZZ = (13, 16, 19)
GL, GR, GF, GH = (22, 24, 26, 28)
GROUPS = 31
PARTS = ((1, 2), (3, 2), (5, 3))
XO = (2, 1, 3)
YO = ZO = (4, 3, 5, 2, 6, 1, 7)
LOADS = 4


def dot(a, b):
    return jnp.dot(a, b, preferred_element_type=jnp.float32)


def unit_rows(raw):
    wide = raw.astype(jnp.float32)
    inv = lax.rsqrt(jnp.sum(wide * wide, 1, keepdims=True) + EPS)
    return (wide * inv).astype(jnp.bfloat16), inv


def across(row):
    return jnp.broadcast_to(row, (128, 128)).T


def body(
    t_hbm, s_hbm, w_hbm, gf_out, gp_out,
    t_ref, s_ref, w_ref, WU, E, SE, F, ETB, ESB, SBT, GB, GPS, GPR, GAS, GAR, GTS, GTR, GFO, GFA,
    CS, CR, XS, XR, YS, YR, CF, ZS, ZRV, ZL, TZS, TZR, TS, RB, RBM, ITB, RW, ITW, lsem, ssem, rsem, phase,
):
    dp = lax.axis_index("dp")
    z = lax.axis_index("proto")
    c = lax.rem(dp, 2)
    y = lax.rem(dp // 2, NY)
    x = dp // (2 * NY)

    def dev(dx, dy, dc, dz):
        return (
            (lax.rem(x + dx, NX) * NY + lax.rem(y + dy, NY)) * NC + lax.rem(c + dc, NC),
            lax.rem(z + dz, NZ),
        )

    mate = dev(0, 0, 1, 0)
    flip = NY + 1 - 2 * lax.rem(y, 2)

    def send(src, dst, group, to):
        pltpu.make_async_remote_copy(
            src, dst, ssem.at[group], rsem.at[group], device_id=to, device_id_type=MESH
        ).start()

    def arrived(ref, group):
        pltpu.make_async_remote_copy(
            ref, ref, ssem.at[group], rsem.at[group], device_id=mate, device_id_type=MESH
        ).wait_recv()

    def sent(ref, group):
        pltpu.make_async_remote_copy(
            ref, ref, ssem.at[group], rsem.at[group], device_id=mate, device_id_type=MESH
        ).wait_send()

    barrier = pltpu.get_barrier_semaphore()
    peers = [(0, k, 0, 0) for k in YO] + [(0, 0, 0, k) for k in ZO] + [(k, 0, 0, 0) for k in XO]
    peers = sorted(peers, key=lambda o: -(min(o[0], NX - o[0]) + min(o[1], NY - o[1]) + min(o[3], NZ - o[3])))
    pl.semaphore_signal(barrier, inc=1, device_id=mate, device_id_type=MESH)

    @pl.when(c == 1)
    def _():
        for offset in peers:
            pl.semaphore_signal(barrier, inc=1, device_id=dev(*offset), device_id_type=MESH)

    loads = [pltpu.make_async_copy(t_hbm, t_ref, lsem.at[0])]
    for piece in range(LOADS):
        cols = pl.ds(piece * (K // LOADS), K // LOADS)
        loads.append(pltpu.make_async_copy(w_hbm.at[:, cols], w_ref.at[:, cols], lsem.at[1 + piece]))
    loads.append(pltpu.make_async_copy(s_hbm, s_ref, lsem.at[1 + LOADS]))
    for load in loads:
        load.start()

    loads[0].wait()
    t_unit, _ = unit_rows(t_ref[...])
    F[0, :B, :] = t_unit.astype(jnp.float32)

    def first(j, carry):
        w = w_ref[:, pl.ds(pl.multiple_of(j * 256, 256), 256)].astype(jnp.float32)
        w = (w * lax.rsqrt(jnp.sum(w * w, 0, keepdims=True) + EPS)).astype(jnp.bfloat16)
        WU[j] = w
        e = jnp.exp(dot(t_unit, w) * INV_T)
        E[2 * j, :B] = e[:, :128]
        E[2 * j + 1, :B] = e[:, 128:]
        CS[pl.ds(2 * j, 1), :] = jnp.sum(e[:, :128], 0, keepdims=True)
        CS[pl.ds(2 * j + 1, 1), :] = jnp.sum(e[:, 128:], 0, keepdims=True)
        return carry

    per = CH // LOADS
    for piece in range(LOADS):
        loads[1 + piece].wait()
        lax.fori_loop(piece * per, piece * per + per, first, 0, unroll=True)
    loads[1 + LOADS].wait()
    s_unit, _ = unit_rows(s_ref[...])
    F[0, B:, :] = s_unit.astype(jnp.float32)

    @pl.when(c == 0)
    def _():
        pl.semaphore_wait(barrier, 1)

    @pl.when(c == 1)
    def _():
        pl.semaphore_wait(barrier, 1 + len(peers))

    def student():
        def step(j, acc):
            e = jnp.exp(dot(F[0, B:, :].astype(jnp.bfloat16), WU[j]) * INV_S)
            SE[2 * j] = e[:, :128]
            SE[2 * j + 1] = e[:, 128:]
            return acc + e[:, :128] + e[:, 128:]

        acc = lax.fori_loop(0, CH, step, jnp.zeros((B, 128), jnp.float32), unroll=4)
        TZS[...] = jnp.sum(acc.T, 0, keepdims=True)

    def exchange_totals():
        for k in ZO:
            send(TZS, TZR.at[k - 1], TZ, dev(0, 0, 0, k))

    def product(tile, kept, got, group):
        def step(j, acc):
            g = jnp.concatenate([tile(2 * j), tile(2 * j + 1)], 1)
            high = g.astype(jnp.bfloat16)
            low = (g - high.astype(jnp.float32)).astype(jnp.bfloat16)
            return acc + lax.dot_general(
                jnp.concatenate([high, low], 0), WU[j], (((1,), (1,)), ((), ())), preferred_element_type=jnp.float32
            )

        acc = lax.fori_loop(0, CH, step, jnp.zeros((2 * B, D), jnp.float32), unroll=4)
        GFA[...] = acc[:B] + acc[B:]
        for k in range(NZ):
            kept[k] = GFA[16 * k:16 * k + 16, :]
        for k in ZO:
            send(kept.at[lax.rem(z + k, NZ)], got.at[k - 1], group, dev(0, 0, 0, k))

    def student_product():
        product(lambda t: SE[t] * ITW[...], GAS, GAR, AR)

    def teacher_product():
        product(lambda t: E[t, :B] * CF[ITERS - 1, pl.ds(t, 1), :], GTS, GTR, TR)

    def student_totals():
        arrived(TZR, TZ)
        total = TZS[...]
        for k in range(NZ - 1):
            total = total + TZR[k]
        TS[0] = SCALE / total
        ITW[...] = across(TS[0])
        for k in XO:
            for p in (1, 0):
                send(TS.at[0], TS.at[2 * k + p], T1, dev(k, flip * p, 0, 0))
        send(TS.at[0], TS.at[1], T1, dev(0, flip, 0, 0))

    def hand_totals():
        arrived(TS.at[pl.ds(1, NB - 1)], T1)
        send(TS.at[pl.ds(0, NB)], TS.at[pl.ds(NB, NB)], T2, mate)

    def line_totals():
        arrived(TS.at[pl.ds(NB, NB)], T2)
        for j in range(2 * NB):
            ITB[j] = across(TS[j])

    def to_sides(p):
        send(F.at[p], F.at[2 + p], GL + p, dev(1, 0, 0, 0))
        send(F.at[p], F.at[6 + p], GR + p, dev(3, 0, 0, 0))

    def relay(p):
        arrived(F.at[2 + p], GL + p)
        arrived(F.at[6 + p], GR + p)
        send(F.at[2 + p, pl.ds(0, B)], F.at[4 + p, pl.ds(0, B)], GF + p, dev(1, 0, 0, 0))
        send(F.at[6 + p, pl.ds(B, B)], F.at[4 + p, pl.ds(B, B)], GF + p, dev(3, 0, 0, 0))

    def to_pair():
        send(F.at[0], F.at[1], GY, dev(0, flip, 0, 0))

    def second_row():
        arrived(F.at[1], GY)
        to_sides(1)
        relay(0)

    def hand(part):
        lo, count = PARTS[part]
        send(F.at[pl.ds(lo, count)], F.at[pl.ds(NB + lo, count)], GH + part, mate)

    def handed(part):
        lo, count = PARTS[part]
        arrived(F.at[pl.ds(NB + lo, count)], GH + part)
        blocks(NB + lo, NB + lo + count)

    def idle(point):
        pl.semaphore_signal(phase.at[point], inc=1, device_id=mate, device_id_type=MESH)

    def when_idle(point):
        pl.semaphore_wait(phase.at[point], 1)

    own = (x * 2 + lax.rem(y, 2)) * NC + c

    def line_block(j, carry):
        tb = F[j, :B, :].astype(jnp.bfloat16)
        sw = F[j, B:, :]
        SBT[j] = sw.T.astype(jnp.bfloat16)
        ETB[j] = jnp.exp(dot(tb, WU[own]) * INV_T)
        ESB[j] = jnp.exp(dot(sw.astype(jnp.bfloat16), WU[own]) * INV_S)
        return carry

    def blocks(lo, hi):
        lax.fori_loop(lo, hi, line_block, 0)

    last = ITERS - 1

    @pl.when(c == 0)
    def _():
        send(CS, CR, UP, mate)
        send(F.at[0], F.at[NB], G0, mate)
        student()
        when_idle(0)
        to_sides(0)
        when_idle(1)
        to_pair()
        arrived(F.at[NB], G0)
        blocks(NB, NB + 1)
        blocks(0, 1)
        when_idle(4)
        exchange_totals()
        when_idle(2)
        second_row()
        student_totals()
        student_product()
        hand_totals()
        hand(0)
        blocks(1, 3)
        line_totals()
        arrived(F.at[4], GF)
        blocks(4, 5)
        when_idle(3)
        relay(1)
        hand(1)
        blocks(3, 4)
        blocks(6, 8)
        arrived(F.at[5], GF + 1)
        hand(2)
        blocks(5, 6)
        handed(0)
        arrived(CF.at[last], DN)
        teacher_product()
        handed(1)
        handed(2)
        arrived(RB, RM)

    @pl.when(c == 1)
    def _():
        def mate_exp(j, carry):
            e = jnp.exp(dot(F[NB, :B, :].astype(jnp.bfloat16), WU[j]) * INV_T)
            E[2 * j, B:] = e[:, :128]
            E[2 * j + 1, B:] = e[:, 128:]
            return carry

        for i in range(ITERS):
            if i == 0:
                send(F.at[0], F.at[NB], G0, mate)
                arrived(CR, UP)
                XS[0] = CS[...] + CR[...]
            for k in XO:
                send(XS.at[i], XR.at[i, k - 1], XX + i, dev(k, 0, 0, 0))
            if i == 0:
                arrived(F.at[NB], G0)
                lax.fori_loop(0, CH, mate_exp, 0, unroll=4)
            elif i == 1:
                blocks(0, 1)
                blocks(NB, NB + 1)
                hand_totals()
            else:
                hand(0)
                line_totals()
                blocks(1, 3)
            arrived(XR.at[i], XX + i)
            YS[i] = (XS[i] + XR[i, 0]) + (XR[i, 1] + XR[i, 2])
            for k in YO:
                send(YS.at[i], YR.at[i, k - 1], YY + i, dev(0, k, 0, 0))
            if i == 0:
                idle(0)
                to_sides(0)
                student()
                exchange_totals()
            elif i == 1:
                idle(2)
                second_row()
                student_product()
            else:
                idle(3)
                relay(1)
                arrived(F.at[4], GF)
                hand(1)
                blocks(3, 5)
                blocks(6, 8)
                handed(0)
            arrived(YR.at[i], YY + i)
            total = YS[i]
            for k in range(NY - 1):
                total = total + YR[i, k]
            CF[i] = 1.0 / total
            if i == last:
                send(CF.at[last], CF.at[last], DN, mate)

            def step(t, acc):
                return acc + E[t] * CF[i, pl.ds(t, 1), :]

            acc = lax.fori_loop(0, TL, step, jnp.zeros((2 * B, 128), jnp.float32), unroll=8)
            ZS[i, 0:1, :] = jnp.sum(acc[:B].T, 0, keepdims=True)
            ZS[i, 1:2, :] = jnp.sum(acc[B:].T, 0, keepdims=True)
            if i < last:
                for k in ZO:
                    send(ZS.at[i], ZRV.at[i, k - 1], ZZ + i, dev(0, 0, 0, k))
                if i == 0:
                    idle(1)
                    to_pair()
                    student_totals()
                arrived(ZRV.at[i], ZZ + i)
                if i == 0:
                    idle(4)
                total = ZS[i]
                for k in range(NZ - 1):
                    total = total + ZRV[i, k]
                inv = 1.0 / total
                RW[:B] = across(inv[0:1])
                RW[B:] = across(inv[1:2])

                def scaled(t, carry):
                    e = E[t] * RW[...]
                    XS[i + 1, pl.ds(t, 1), :] = jnp.sum(e[:B] + e[B:], 0, keepdims=True)
                    return carry

                lax.fori_loop(0, TL, scaled, 0, unroll=8)
            else:
                far = lambda k: -(min(k // (2 * NZ), NX - k // (2 * NZ)) + k // NZ % 2 + min(k % NZ, NZ - k % NZ))
                for k in sorted(range(1, NB * NZ), key=far):
                    to = dev(k // (2 * NZ), flip * (k // NZ % 2), 0, k % NZ)
                    send(ZS.at[i], ZL.at[k], ZZ + i, to)
                ZL[0] = ZS[i]
                arrived(F.at[5], GF + 1)
                hand(2)
                teacher_product()
                blocks(5, 6)
                handed(1)
                handed(2)
                arrived(ZL.at[pl.ds(1, NB * NZ - 1)], ZZ + i)
                for j in range(NB):
                    total = ZL[j * NZ]
                    for dz in range(1, NZ):
                        total = total + ZL[j * NZ + dz]
                    inv = 1.0 / total
                    RB[j] = inv[0:1]
                    RB[NB + j] = inv[1:2]
                    RBM[j] = inv[1:2]
                    RBM[NB + j] = inv[0:1]
                send(RBM, RB, RM, mate)

    def line_grad(j, carry):
        rb = across(RB[j] * SCALE)
        for q in range(KB // 128):
            part = pl.ds(128 * q, 128)
            col = CF[last, pl.ds(own * (KB // 128) + q, 1), :]
            g = ESB[j, :, part] * ITB[j] - (ETB[j, :, part] * col) * rb
            GB[j, :, 128 * q:128 * q + 128] = g.astype(jnp.bfloat16)
        return carry

    lax.fori_loop(0, 2 * NB, line_grad, 0, unroll=True)
    acc = jnp.zeros((D, KB), jnp.float32)
    for p in range(NB):
        lhs = jnp.concatenate([SBT[2 * p], SBT[2 * p + 1]], 1)
        acc = acc + dot(lhs, jnp.concatenate([GB[2 * p], GB[2 * p + 1]], 0))
    GPS[...] = acc.reshape(D // 4, 4, KB)

    for dy in YO + (0,):
        def scatter(i, carry):
            to = dev(i // NC, dy, lax.rem(i, NC), 0)
            send(GPS.at[to[0]], GPR.at[i // NC * (NY * NC) + dy * NC + lax.rem(i, NC)], GP, to)
            return carry

        lax.fori_loop(0 if dy else 1, NX * NC, scatter, 0)

    RW[:B] = across(RB[0] * SCALE)
    mine = pl.ds(pl.multiple_of(z * 16, 16), 16)
    u, inv = unit_rows(s_ref[mine, :])
    u = u.astype(jnp.float32)
    arrived(GAR, AR)
    arrived(GTR, TR)
    total, teach = GAS[z], GTS[z]
    for k in range(NZ - 1):
        total = total + GAR[k]
        teach = teach + GTR[k]
    total = total - teach * RW[mine, 0:1]
    GFO[0] = (total - u * jnp.sum(u * total, 1, keepdims=True)) * inv
    for k in ZO:
        send(GFO.at[0], GFO.at[k], ZA, dev(0, 0, 0, k))
    gf_out[mine, :] = GFO[0]
    arrived(GFO.at[pl.ds(1, NZ - 1)], ZA)
    for k in range(1, NZ):
        at = lax.rem(z + NZ - k, NZ) * 16
        gf_out[pl.ds(pl.multiple_of(at, 16), 16), :] = GFO[k]

    arrived(GPR.at[pl.ds(1, NX * NY * NC - 1)], GP)
    GPR[0] = GPS[dp]
    for dx in range(NX):
        for dc in range(NC):
            for p in range(2):
                total = GPR[(dx * NY + p) * NC + dc]
                for dy in range(p + 2, NY, 2):
                    total = total + GPR[(dx * NY + dy) * NC + dc]
                at = (lax.rem(x + NX - dx, NX) * 2 + lax.rem(y + p, 2)) * NC + lax.rem(c + dc, NC)
                gp_out[:, pl.ds(pl.multiple_of(at * KB, KB), KB)] = total

    @pl.when(c == 0)
    def _():
        sent(CS, UP)

    @pl.when(c == 1)
    def _():
        for i in range(ITERS):
            sent(XR.at[i], XX + i)
            sent(YR.at[i], YY + i)
            if i < last:
                sent(ZRV.at[i], ZZ + i)
        sent(ZL.at[pl.ds(1, NB * NZ - 1)], ZZ + last)
        sent(CF.at[last], DN)
        sent(RBM, RM)

    sent(TZR, TZ)
    sent(F.at[0], G0)
    sent(F.at[0], GY)
    for p in range(2):
        sent(F.at[p], GL + p)
        sent(F.at[p], GR + p)
        sent(F.at[4 + p], GF + p)
    for part, (lo, count) in enumerate(PARTS):
        sent(F.at[pl.ds(lo, count)], GH + part)
    sent(TS.at[pl.ds(1, NB - 1)], T1)
    sent(TS.at[pl.ds(0, NB)], T2)
    sent(GPR.at[pl.ds(1, NX * NY * NC - 1)], GP)
    sent(GAR, AR)
    sent(GTR, TR)
    sent(GFO.at[pl.ds(1, NZ - 1)], ZA)


def place(features, protos, features_out, protos_out):
    features_out[...] = features[...]
    protos_out[...] = protos[...]


def shards(teacher, student, protos):
    f32, bf16 = jnp.float32, jnp.bfloat16
    vm = pltpu.VMEM
    scratch = [
        vm((B, D), bf16),
        vm((B, D), bf16),
        vm((D, K), bf16),
        vm((CH, D, 256), bf16),
        vm((TL, 2 * B, 128), f32),
        vm((TL, B, 128), f32),
        vm((2 * NB, 2 * B, D), f32),
        vm((2 * NB, B, KB), f32),
        vm((2 * NB, B, KB), f32),
        vm((2 * NB, D, B), bf16),
        vm((2 * NB, B, KB), bf16),
        vm((64, 4, KB), f32),
        vm((64, 4, KB), f32),
        vm((NZ, 16, D), f32),
        vm((NZ - 1, 16, D), f32),
        vm((NZ, 16, D), f32),
        vm((NZ - 1, 16, D), f32),
        vm((NZ, 16, D), f32),
        vm((B, D), f32),
        vm((TL, 128), f32),
        vm((TL, 128), f32),
        vm((ITERS, TL, 128), f32),
        vm((ITERS, NX - 1, TL, 128), f32),
        vm((ITERS, TL, 128), f32),
        vm((ITERS, NY - 1, TL, 128), f32),
        vm((ITERS, TL, 128), f32),
        vm((ITERS, 2, 128), f32),
        vm((ITERS - 1, NZ - 1, 2, 128), f32),
        vm((NB * NZ, 2, 128), f32),
        vm((1, 128), f32),
        vm((NZ - 1, 1, 128), f32),
        vm((2 * NB, 1, 128), f32),
        vm((2 * NB, 1, 128), f32),
        vm((2 * NB, 1, 128), f32),
        vm((2 * NB, B, 128), f32),
        vm((2 * B, 128), f32),
        vm((B, 128), f32),
        pltpu.SemaphoreType.DMA((2 + LOADS,)),
        pltpu.SemaphoreType.DMA((GROUPS,)),
        pltpu.SemaphoreType.DMA((GROUPS,)),
        pltpu.SemaphoreType.REGULAR((5,)),
    ]
    whole = pl.BlockSpec(memory_space=pltpu.VMEM)
    anywhere = pl.BlockSpec(memory_space=pl.ANY)
    grads = pl.pallas_call(
        body,
        out_shape=(jax.ShapeDtypeStruct((B, D), f32), jax.ShapeDtypeStruct((4, K), f32)),
        in_specs=[anywhere] * 3,
        out_specs=(whole, whole),
        scratch_shapes=scratch,
        compiler_params=pltpu.CompilerParams(
            collective_id=0, has_side_effects=True, vmem_limit_bytes=60 * 2**20
        ),
    )(teacher, student, protos)
    return pl.pallas_call(
        place,
        out_shape=tuple(jax.ShapeDtypeStruct(g.shape, g.dtype) for g in grads),
        in_specs=[whole] * 2,
        out_specs=(whole,) * 2,
        compiler_params=pltpu.CompilerParams(vmem_limit_bytes=60 * 2**20),
    )(*grads)


def solution(mesh):
    placed = (P("dp", None), P("dp", None), P(None, "proto"))
    return jax.shard_map(
        shards,
        mesh=mesh,
        in_specs=placed,
        out_specs=(P("dp", None), P("dp", "proto")),
        check_vma=False,
    )
```

```python
import functools

import jax
import jax.numpy as jnp
from jax import lax
from jax.experimental import pallas as pl
from jax.experimental.pallas import tpu as pltpu
from jax.sharding import PartitionSpec as P

EPS = 1e-06
INV_T = 1.0 / 0.07
INV_S = 1.0 / 0.1
ITERS = 3
NX, NY, NC, NZ = 4, 8, 2, 8
B = 128
D = 256
K = 4096
CH = K // 256
TL = K // 128
NB = 2 * NX
KB = K // (NB * NC)
SCALE = 32768 / 64.0 / 0.1
MESH = pl.DeviceIdType.MESH

UP, DN, G0, GY, NO, TZ, T1, T2, RM, GP, AR, TR, ZA = range(13)
XX, YY, ZZ = (13, 16, 19)
GL, GR, GF, GH = (22, 24, 26, 28)
GROUPS = 31
PARTS = ((1, 2), (3, 2), (5, 3))
XO = (2, 1, 3)
YO = ZO = (4, 3, 5, 2, 6, 1, 7)
LOADS = 4


def dot(a, b):
    return jnp.dot(a, b, preferred_element_type=jnp.float32)


def unit_rows(raw):
    wide = raw.astype(jnp.float32)
    inv = lax.rsqrt(jnp.sum(wide * wide, 1, keepdims=True) + EPS)
    return (wide * inv).astype(jnp.bfloat16), inv


def across(row):
    return jnp.broadcast_to(row, (128, 128)).T


def body(
    t_hbm, s_hbm, w_hbm, gf_out, gp_out,
    t_ref, s_ref, w_ref, WU, E, SE, F, ETB, ESB, SBT, GB, GPS, GPR, GAS, GAR, GTS, GTR, GFO, GFA,
    CS, CR, XS, XR, YS, YR, CF, ZS, ZRV, ZL, TZS, TZR, TS, RB, RBM, ITB, RW, ITW, lsem, ssem, rsem, phase,
):
    dp = lax.axis_index("dp")
    z = lax.axis_index("proto")
    c = lax.rem(dp, 2)
    y = lax.rem(dp // 2, NY)
    x = dp // (2 * NY)

    def dev(dx, dy, dc, dz):
        return (
            (lax.rem(x + dx, NX) * NY + lax.rem(y + dy, NY)) * NC + lax.rem(c + dc, NC),
            lax.rem(z + dz, NZ),
        )

    mate = dev(0, 0, 1, 0)
    flip = NY + 1 - 2 * lax.rem(y, 2)

    def send(src, dst, group, to):
        pltpu.make_async_remote_copy(
            src, dst, ssem.at[group], rsem.at[group], device_id=to, device_id_type=MESH
        ).start()

    def arrived(ref, group):
        pltpu.make_async_remote_copy(
            ref, ref, ssem.at[group], rsem.at[group], device_id=mate, device_id_type=MESH
        ).wait_recv()

    def sent(ref, group):
        pltpu.make_async_remote_copy(
            ref, ref, ssem.at[group], rsem.at[group], device_id=mate, device_id_type=MESH
        ).wait_send()

    offsets = [(0, k, 0, 0) for k in YO] + [(0, 0, 0, k) for k in ZO] + [(k, 0, 0, 0) for k in XO]
    offsets = sorted(offsets, key=lambda o: -(min(o[0], NX - o[0]) + min(o[1], NY - o[1]) + min(o[3], NZ - o[3])))
    peers = [dev(k, flip, 0, 0) for k in XO] + [dev(*o) for o in offsets] + [mate]
    barrier = pltpu.get_barrier_semaphore()
    for to in peers:
        pl.semaphore_signal(barrier, inc=1, device_id=to, device_id_type=MESH)

    loads = [pltpu.make_async_copy(t_hbm, t_ref, lsem.at[0])]
    for piece in range(LOADS):
        cols = pl.ds(piece * (K // LOADS), K // LOADS)
        loads.append(pltpu.make_async_copy(w_hbm.at[:, cols], w_ref.at[:, cols], lsem.at[1 + piece]))
    loads.append(pltpu.make_async_copy(s_hbm, s_ref, lsem.at[1 + LOADS]))
    for load in loads:
        load.start()

    loads[0].wait()
    t_unit, _ = unit_rows(t_ref[...])
    F[0, :B, :] = t_unit.astype(jnp.float32)

    def first(j, carry):
        w = w_ref[:, pl.ds(pl.multiple_of(j * 256, 256), 256)].astype(jnp.float32)
        w = (w * lax.rsqrt(jnp.sum(w * w, 0, keepdims=True) + EPS)).astype(jnp.bfloat16)
        WU[j] = w
        e = jnp.exp(dot(t_unit, w) * INV_T)
        E[2 * j, :B] = e[:, :128]
        E[2 * j + 1, :B] = e[:, 128:]
        CS[pl.ds(2 * j, 1), :] = jnp.sum(e[:, :128], 0, keepdims=True)
        CS[pl.ds(2 * j + 1, 1), :] = jnp.sum(e[:, 128:], 0, keepdims=True)
        return carry

    per = CH // LOADS
    for piece in range(LOADS):
        loads[1 + piece].wait()
        lax.fori_loop(piece * per, piece * per + per, first, 0, unroll=True)
    loads[1 + LOADS].wait()
    s_unit, _ = unit_rows(s_ref[...])
    F[0, B:, :] = s_unit.astype(jnp.float32)
    pl.semaphore_wait(barrier, len(peers))

    def student():
        def step(j, acc):
            e = jnp.exp(dot(F[0, B:, :].astype(jnp.bfloat16), WU[j]) * INV_S)
            SE[2 * j] = e[:, :128]
            SE[2 * j + 1] = e[:, 128:]
            return acc + e[:, :128] + e[:, 128:]

        acc = lax.fori_loop(0, CH, step, jnp.zeros((B, 128), jnp.float32), unroll=4)
        TZS[...] = jnp.sum(acc.T, 0, keepdims=True)
        for k in ZO:
            send(TZS, TZR.at[k - 1], TZ, dev(0, 0, 0, k))

    def product(tile, kept, got, group):
        def step(j, acc):
            g = jnp.concatenate([tile(2 * j), tile(2 * j + 1)], 1)
            high = g.astype(jnp.bfloat16)
            low = (g - high.astype(jnp.float32)).astype(jnp.bfloat16)
            return acc + lax.dot_general(
                jnp.concatenate([high, low], 0), WU[j], (((1,), (1,)), ((), ())), preferred_element_type=jnp.float32
            )

        acc = lax.fori_loop(0, CH, step, jnp.zeros((2 * B, D), jnp.float32), unroll=4)
        GFA[...] = acc[:B] + acc[B:]
        for k in range(NZ):
            kept[k] = GFA[16 * k:16 * k + 16, :]
        for k in ZO:
            send(kept.at[lax.rem(z + k, NZ)], got.at[k - 1], group, dev(0, 0, 0, k))

    def student_product():
        product(lambda t: SE[t] * ITW[...], GAS, GAR, AR)

    def teacher_product():
        product(lambda t: E[t, :B] * CF[ITERS - 1, pl.ds(t, 1), :], GTS, GTR, TR)

    def student_totals():
        arrived(TZR, TZ)
        total = TZS[...]
        for k in range(NZ - 1):
            total = total + TZR[k]
        TS[0] = SCALE / total
        ITW[...] = across(TS[0])
        for k in XO:
            for p in (1, 0):
                send(TS.at[0], TS.at[2 * k + p], T1, dev(k, flip * p, 0, 0))
        send(TS.at[0], TS.at[1], T1, dev(0, flip, 0, 0))

    def hand_totals():
        arrived(TS.at[pl.ds(1, NB - 1)], T1)
        send(TS.at[pl.ds(0, NB)], TS.at[pl.ds(NB, NB)], T2, mate)

    def line_totals():
        arrived(TS.at[pl.ds(NB, NB)], T2)
        for j in range(2 * NB):
            ITB[j] = across(TS[j])

    def to_sides(p):
        send(F.at[p], F.at[2 + p], GL + p, dev(1, 0, 0, 0))
        send(F.at[p], F.at[6 + p], GR + p, dev(3, 0, 0, 0))

    def relay(p):
        arrived(F.at[2 + p], GL + p)
        arrived(F.at[6 + p], GR + p)
        send(F.at[2 + p, pl.ds(0, B)], F.at[4 + p, pl.ds(0, B)], GF + p, dev(1, 0, 0, 0))
        send(F.at[6 + p, pl.ds(B, B)], F.at[4 + p, pl.ds(B, B)], GF + p, dev(3, 0, 0, 0))

    def to_pair():
        send(F.at[0], F.at[1], GY, dev(0, flip, 0, 0))

    def second_row():
        arrived(F.at[1], GY)
        to_sides(1)
        relay(0)

    def hand(part):
        lo, count = PARTS[part]
        send(F.at[pl.ds(lo, count)], F.at[pl.ds(NB + lo, count)], GH + part, mate)

    def handed(part):
        lo, count = PARTS[part]
        arrived(F.at[pl.ds(NB + lo, count)], GH + part)
        blocks(NB + lo, NB + lo + count)

    def idle(point):
        pl.semaphore_signal(phase.at[point], inc=1, device_id=mate, device_id_type=MESH)

    def when_idle(point):
        pl.semaphore_wait(phase.at[point], 1)

    own = (x * 2 + lax.rem(y, 2)) * NC + c

    def line_block(j, carry):
        tb = F[j, :B, :].astype(jnp.bfloat16)
        sw = F[j, B:, :]
        SBT[j] = sw.T.astype(jnp.bfloat16)
        ETB[j] = jnp.exp(dot(tb, WU[own]) * INV_T)
        ESB[j] = jnp.exp(dot(sw.astype(jnp.bfloat16), WU[own]) * INV_S)
        return carry

    def blocks(lo, hi):
        lax.fori_loop(lo, hi, line_block, 0)

    last = ITERS - 1

    @pl.when(c == 0)
    def _():
        send(CS, CR, UP, mate)
        send(F.at[0], F.at[NB], G0, mate)
        student()
        when_idle(0)
        to_sides(0)
        student_totals()
        when_idle(1)
        to_pair()
        arrived(F.at[NB], G0)
        blocks(NB, NB + 1)
        blocks(0, 1)
        hand_totals()
        when_idle(2)
        second_row()
        student_product()
        hand(0)
        blocks(1, 3)
        line_totals()
        arrived(F.at[4], GF)
        blocks(4, 5)
        when_idle(3)
        relay(1)
        hand(1)
        blocks(3, 4)
        blocks(6, 8)
        arrived(F.at[5], GF + 1)
        hand(2)
        blocks(5, 6)
        handed(0)
        arrived(CF.at[last], DN)
        teacher_product()
        handed(1)
        handed(2)
        arrived(RB, RM)

    @pl.when(c == 1)
    def _():
        def mate_exp(j, carry):
            e = jnp.exp(dot(F[NB, :B, :].astype(jnp.bfloat16), WU[j]) * INV_T)
            E[2 * j, B:] = e[:, :128]
            E[2 * j + 1, B:] = e[:, 128:]
            return carry

        for i in range(ITERS):
            if i == 0:
                send(F.at[0], F.at[NB], G0, mate)
                arrived(CR, UP)
                XS[0] = CS[...] + CR[...]
            for k in XO:
                send(XS.at[i], XR.at[i, k - 1], XX + i, dev(k, 0, 0, 0))
            if i == 0:
                arrived(F.at[NB], G0)
                lax.fori_loop(0, CH, mate_exp, 0, unroll=4)
            elif i == 1:
                blocks(0, 1)
                blocks(NB, NB + 1)
                hand_totals()
            else:
                hand(0)
                blocks(1, 3)
            arrived(XR.at[i], XX + i)
            YS[i] = (XS[i] + XR[i, 0]) + (XR[i, 1] + XR[i, 2])
            for k in YO:
                send(YS.at[i], YR.at[i, k - 1], YY + i, dev(0, k, 0, 0))
            if i == 0:
                idle(0)
                to_sides(0)
                student()
            elif i == 1:
                idle(2)
                second_row()
                student_product()
            else:
                idle(3)
                relay(1)
                arrived(F.at[4], GF)
                hand(1)
            arrived(YR.at[i], YY + i)
            total = YS[i]
            for k in range(NY - 1):
                total = total + YR[i, k]
            CF[i] = 1.0 / total
            if i == last:
                send(CF.at[last], CF.at[last], DN, mate)

            def step(t, acc):
                return acc + E[t] * CF[i, pl.ds(t, 1), :]

            acc = lax.fori_loop(0, TL, step, jnp.zeros((2 * B, 128), jnp.float32), unroll=8)
            ZS[i, 0:1, :] = jnp.sum(acc[:B].T, 0, keepdims=True)
            ZS[i, 1:2, :] = jnp.sum(acc[B:].T, 0, keepdims=True)
            if i < last:
                for k in ZO:
                    send(ZS.at[i], ZRV.at[i, k - 1], ZZ + i, dev(0, 0, 0, k))
                if i == 0:
                    idle(1)
                    to_pair()
                    student_totals()
                else:
                    line_totals()
                arrived(ZRV.at[i], ZZ + i)
                total = ZS[i]
                for k in range(NZ - 1):
                    total = total + ZRV[i, k]
                inv = 1.0 / total
                RW[:B] = across(inv[0:1])
                RW[B:] = across(inv[1:2])

                def scaled(t, carry):
                    e = E[t] * RW[...]
                    XS[i + 1, pl.ds(t, 1), :] = jnp.sum(e[:B] + e[B:], 0, keepdims=True)
                    return carry

                lax.fori_loop(0, TL, scaled, 0, unroll=8)
            else:
                far = lambda k: -(min(k // (2 * NZ), NX - k // (2 * NZ)) + k // NZ % 2 + min(k % NZ, NZ - k % NZ))
                for k in sorted(range(1, NB * NZ), key=far):
                    to = dev(k // (2 * NZ), flip * (k // NZ % 2), 0, k % NZ)
                    send(ZS.at[i], ZL.at[k], ZZ + i, to)
                ZL[0] = ZS[i]
                arrived(F.at[5], GF + 1)
                hand(2)
                teacher_product()
                blocks(3, NB)
                handed(0)
                handed(1)
                handed(2)
                arrived(ZL.at[pl.ds(1, NB * NZ - 1)], ZZ + i)
                for j in range(NB):
                    total = ZL[j * NZ]
                    for dz in range(1, NZ):
                        total = total + ZL[j * NZ + dz]
                    inv = 1.0 / total
                    RB[j] = inv[0:1]
                    RB[NB + j] = inv[1:2]
                    RBM[j] = inv[1:2]
                    RBM[NB + j] = inv[0:1]
                send(RBM, RB, RM, mate)

    def line_grad(j, carry):
        rb = across(RB[j] * SCALE)
        for q in range(KB // 128):
            part = pl.ds(128 * q, 128)
            col = CF[last, pl.ds(own * (KB // 128) + q, 1), :]
            g = ESB[j, :, part] * ITB[j] - (ETB[j, :, part] * col) * rb
            GB[j, :, 128 * q:128 * q + 128] = g.astype(jnp.bfloat16)
        return carry

    lax.fori_loop(0, 2 * NB, line_grad, 0, unroll=True)
    acc = jnp.zeros((D, KB), jnp.float32)
    for p in range(NB):
        lhs = jnp.concatenate([SBT[2 * p], SBT[2 * p + 1]], 1)
        acc = acc + dot(lhs, jnp.concatenate([GB[2 * p], GB[2 * p + 1]], 0))
    GPS[...] = acc.reshape(D // 4, 4, KB)

    for dy in YO + (0,):
        def scatter(i, carry):
            to = dev(i // NC, dy, lax.rem(i, NC), 0)
            send(GPS.at[to[0]], GPR.at[i // NC * (NY * NC) + dy * NC + lax.rem(i, NC)], GP, to)
            return carry

        lax.fori_loop(0 if dy else 1, NX * NC, scatter, 0)

    RW[:B] = across(RB[0] * SCALE)
    mine = pl.ds(pl.multiple_of(z * 16, 16), 16)
    u, inv = unit_rows(s_ref[mine, :])
    u = u.astype(jnp.float32)
    arrived(GAR, AR)
    arrived(GTR, TR)
    total, teach = GAS[z], GTS[z]
    for k in range(NZ - 1):
        total = total + GAR[k]
        teach = teach + GTR[k]
    total = total - teach * RW[mine, 0:1]
    GFO[0] = (total - u * jnp.sum(u * total, 1, keepdims=True)) * inv
    for k in ZO:
        send(GFO.at[0], GFO.at[k], ZA, dev(0, 0, 0, k))
    gf_out[mine, :] = GFO[0]
    arrived(GFO.at[pl.ds(1, NZ - 1)], ZA)
    for k in range(1, NZ):
        at = lax.rem(z + NZ - k, NZ) * 16
        gf_out[pl.ds(pl.multiple_of(at, 16), 16), :] = GFO[k]

    arrived(GPR.at[pl.ds(1, NX * NY * NC - 1)], GP)
    GPR[0] = GPS[dp]
    for dx in range(NX):
        for dc in range(NC):
            for p in range(2):
                total = GPR[(dx * NY + p) * NC + dc]
                for dy in range(p + 2, NY, 2):
                    total = total + GPR[(dx * NY + dy) * NC + dc]
                at = (lax.rem(x + NX - dx, NX) * 2 + lax.rem(y + p, 2)) * NC + lax.rem(c + dc, NC)
                gp_out[:, pl.ds(pl.multiple_of(at * KB, KB), KB)] = total

    @pl.when(c == 0)
    def _():
        sent(CS, UP)

    @pl.when(c == 1)
    def _():
        for i in range(ITERS):
            sent(XR.at[i], XX + i)
            sent(YR.at[i], YY + i)
            if i < last:
                sent(ZRV.at[i], ZZ + i)
        sent(ZL.at[pl.ds(1, NB * NZ - 1)], ZZ + last)
        sent(CF.at[last], DN)
        sent(RBM, RM)

    sent(TZR, TZ)
    sent(F.at[0], G0)
    sent(F.at[0], GY)
    for p in range(2):
        sent(F.at[p], GL + p)
        sent(F.at[p], GR + p)
        sent(F.at[4 + p], GF + p)
    for part, (lo, count) in enumerate(PARTS):
        sent(F.at[pl.ds(lo, count)], GH + part)
    sent(TS.at[pl.ds(1, NB - 1)], T1)
    sent(TS.at[pl.ds(0, NB)], T2)
    sent(GPR.at[pl.ds(1, NX * NY * NC - 1)], GP)
    sent(GAR, AR)
    sent(GTR, TR)
    sent(GFO.at[pl.ds(1, NZ - 1)], ZA)


def place(features, protos, features_out, protos_out):
    features_out[...] = features[...]
    protos_out[...] = protos[...]


def shards(teacher, student, protos):
    f32, bf16 = jnp.float32, jnp.bfloat16
    vm = pltpu.VMEM
    scratch = [
        vm((B, D), bf16),
        vm((B, D), bf16),
        vm((D, K), bf16),
        vm((CH, D, 256), bf16),
        vm((TL, 2 * B, 128), f32),
        vm((TL, B, 128), f32),
        vm((2 * NB, 2 * B, D), f32),
        vm((2 * NB, B, KB), f32),
        vm((2 * NB, B, KB), f32),
        vm((2 * NB, D, B), bf16),
        vm((2 * NB, B, KB), bf16),
        vm((64, 4, KB), f32),
        vm((64, 4, KB), f32),
        vm((NZ, 16, D), f32),
        vm((NZ - 1, 16, D), f32),
        vm((NZ, 16, D), f32),
        vm((NZ - 1, 16, D), f32),
        vm((NZ, 16, D), f32),
        vm((B, D), f32),
        vm((TL, 128), f32),
        vm((TL, 128), f32),
        vm((ITERS, TL, 128), f32),
        vm((ITERS, NX - 1, TL, 128), f32),
        vm((ITERS, TL, 128), f32),
        vm((ITERS, NY - 1, TL, 128), f32),
        vm((ITERS, TL, 128), f32),
        vm((ITERS, 2, 128), f32),
        vm((ITERS - 1, NZ - 1, 2, 128), f32),
        vm((NB * NZ, 2, 128), f32),
        vm((1, 128), f32),
        vm((NZ - 1, 1, 128), f32),
        vm((2 * NB, 1, 128), f32),
        vm((2 * NB, 1, 128), f32),
        vm((2 * NB, 1, 128), f32),
        vm((2 * NB, B, 128), f32),
        vm((2 * B, 128), f32),
        vm((B, 128), f32),
        pltpu.SemaphoreType.DMA((2 + LOADS,)),
        pltpu.SemaphoreType.DMA((GROUPS,)),
        pltpu.SemaphoreType.DMA((GROUPS,)),
        pltpu.SemaphoreType.REGULAR((4,)),
    ]
    whole = pl.BlockSpec(memory_space=pltpu.VMEM)
    anywhere = pl.BlockSpec(memory_space=pl.ANY)
    grads = pl.pallas_call(
        body,
        out_shape=(jax.ShapeDtypeStruct((B, D), f32), jax.ShapeDtypeStruct((4, K), f32)),
        in_specs=[anywhere] * 3,
        out_specs=(whole, whole),
        scratch_shapes=scratch,
        compiler_params=pltpu.CompilerParams(
            collective_id=0, has_side_effects=True, vmem_limit_bytes=60 * 2**20
        ),
    )(teacher, student, protos)
    return pl.pallas_call(
        place,
        out_shape=tuple(jax.ShapeDtypeStruct(g.shape, g.dtype) for g in grads),
        in_specs=[whole] * 2,
        out_specs=(whole,) * 2,
        compiler_params=pltpu.CompilerParams(vmem_limit_bytes=60 * 2**20),
    )(*grads)


def solution(mesh):
    placed = (P("dp", None), P("dp", None), P(None, "proto"))
    return jax.shard_map(
        shards,
        mesh=mesh,
        in_specs=placed,
        out_specs=(P("dp", None), P("dp", "proto")),
        check_vma=False,
    )
```

```python
import functools

import jax
import jax.numpy as jnp
from jax import lax
from jax.experimental import pallas as pl
from jax.experimental.pallas import tpu as pltpu
from jax.sharding import PartitionSpec as P

EPS = 1e-06
INV_T = 1.0 / 0.07
INV_S = 1.0 / 0.1
ITERS = 3
NX, NY, NC, NZ = 4, 8, 2, 8
B = 128
D = 256
K = 4096
CH = K // 256
TL = K // 128
NB = 2 * NX
KB = K // (NB * NC)
SCALE = 32768 / 64.0 / 0.1
MESH = pl.DeviceIdType.MESH

UP, DN, G0, GY, NO, TZ, T1, T2, RM, GP, AR, TR, ZA = range(13)
XX, YY, ZZ = (13, 16, 19)
GL, GR, GF, GH = (22, 24, 26, 28)
GROUPS = 31
PARTS = ((1, 2), (3, 2), (5, 3))
XO = (2, 1, 3)
YO = ZO = (4, 3, 5, 2, 6, 1, 7)
LOADS = 4


def dot(a, b):
    return jnp.dot(a, b, preferred_element_type=jnp.float32)


def unit_rows(raw):
    wide = raw.astype(jnp.float32)
    inv = lax.rsqrt(jnp.sum(wide * wide, 1, keepdims=True) + EPS)
    return (wide * inv).astype(jnp.bfloat16), inv


def across(row):
    return jnp.broadcast_to(row, (128, 128)).T


def body(
    t_hbm, s_hbm, w_hbm, gf_out, gp_out,
    t_ref, s_ref, w_ref, WU, E, SE, F, ETB, ESB, SBT, GB, GPS, GPR, GAS, GAR, GTS, GTR, GFO, GFA,
    CS, CR, XS, XR, YS, YR, CF, ZS, ZRV, ZL, TZS, TZR, TS, RB, RBM, ITB, RW, ITW, lsem, ssem, rsem, phase,
):
    dp = lax.axis_index("dp")
    z = lax.axis_index("proto")
    c = lax.rem(dp, 2)
    y = lax.rem(dp // 2, NY)
    x = dp // (2 * NY)

    def dev(dx, dy, dc, dz):
        return (
            (lax.rem(x + dx, NX) * NY + lax.rem(y + dy, NY)) * NC + lax.rem(c + dc, NC),
            lax.rem(z + dz, NZ),
        )

    mate = dev(0, 0, 1, 0)
    flip = NY + 1 - 2 * lax.rem(y, 2)

    def send(src, dst, group, to):
        pltpu.make_async_remote_copy(
            src, dst, ssem.at[group], rsem.at[group], device_id=to, device_id_type=MESH
        ).start()

    def arrived(ref, group):
        pltpu.make_async_remote_copy(
            ref, ref, ssem.at[group], rsem.at[group], device_id=mate, device_id_type=MESH
        ).wait_recv()

    def sent(ref, group):
        pltpu.make_async_remote_copy(
            ref, ref, ssem.at[group], rsem.at[group], device_id=mate, device_id_type=MESH
        ).wait_send()

    offsets = [(0, k, 0, 0) for k in YO] + [(0, 0, 0, k) for k in ZO] + [(k, 0, 0, 0) for k in XO]
    offsets = sorted(offsets, key=lambda o: -(min(o[0], NX - o[0]) + min(o[1], NY - o[1]) + min(o[3], NZ - o[3])))
    peers = [dev(k, flip, 0, 0) for k in XO] + [dev(*o) for o in offsets] + [mate]
    barrier = pltpu.get_barrier_semaphore()
    for to in peers:
        pl.semaphore_signal(barrier, inc=1, device_id=to, device_id_type=MESH)

    loads = [pltpu.make_async_copy(t_hbm, t_ref, lsem.at[0])]
    for piece in range(LOADS):
        cols = pl.ds(piece * (K // LOADS), K // LOADS)
        loads.append(pltpu.make_async_copy(w_hbm.at[:, cols], w_ref.at[:, cols], lsem.at[1 + piece]))
    loads.append(pltpu.make_async_copy(s_hbm, s_ref, lsem.at[1 + LOADS]))
    for load in loads:
        load.start()

    loads[0].wait()
    t_unit, _ = unit_rows(t_ref[...])
    F[0, :B, :] = t_unit.astype(jnp.float32)

    def first(j, carry):
        w = w_ref[:, pl.ds(pl.multiple_of(j * 256, 256), 256)].astype(jnp.float32)
        w = (w * lax.rsqrt(jnp.sum(w * w, 0, keepdims=True) + EPS)).astype(jnp.bfloat16)
        WU[j] = w
        e = jnp.exp(dot(t_unit, w) * INV_T)
        E[2 * j, :B] = e[:, :128]
        E[2 * j + 1, :B] = e[:, 128:]
        CS[pl.ds(2 * j, 1), :] = jnp.sum(e[:, :128], 0, keepdims=True)
        CS[pl.ds(2 * j + 1, 1), :] = jnp.sum(e[:, 128:], 0, keepdims=True)
        return carry

    per = CH // LOADS
    for piece in range(LOADS):
        loads[1 + piece].wait()
        lax.fori_loop(piece * per, piece * per + per, first, 0, unroll=True)
    loads[1 + LOADS].wait()
    s_unit, _ = unit_rows(s_ref[...])
    F[0, B:, :] = s_unit.astype(jnp.float32)
    pl.semaphore_wait(barrier, len(peers))

    def student():
        def step(j, acc):
            e = jnp.exp(dot(F[0, B:, :].astype(jnp.bfloat16), WU[j]) * INV_S)
            SE[2 * j] = e[:, :128]
            SE[2 * j + 1] = e[:, 128:]
            return acc + e[:, :128] + e[:, 128:]

        acc = lax.fori_loop(0, CH, step, jnp.zeros((B, 128), jnp.float32), unroll=4)
        TZS[...] = jnp.sum(acc.T, 0, keepdims=True)
        for k in ZO:
            send(TZS, TZR.at[k - 1], TZ, dev(0, 0, 0, k))

    def product(tile, kept, got, group):
        def step(j, acc):
            g = jnp.concatenate([tile(2 * j), tile(2 * j + 1)], 1)
            high = g.astype(jnp.bfloat16)
            low = (g - high.astype(jnp.float32)).astype(jnp.bfloat16)
            return acc + lax.dot_general(
                jnp.concatenate([high, low], 0), WU[j], (((1,), (1,)), ((), ())), preferred_element_type=jnp.float32
            )

        acc = lax.fori_loop(0, CH, step, jnp.zeros((2 * B, D), jnp.float32), unroll=4)
        GFA[...] = acc[:B] + acc[B:]
        for k in range(NZ):
            kept[k] = GFA[16 * k:16 * k + 16, :]
        for k in ZO:
            send(kept.at[lax.rem(z + k, NZ)], got.at[k - 1], group, dev(0, 0, 0, k))

    def student_product():
        product(lambda t: SE[t] * ITW[...], GAS, GAR, AR)

    def teacher_product():
        product(lambda t: E[t, :B] * CF[ITERS - 1, pl.ds(t, 1), :], GTS, GTR, TR)

    def student_totals():
        arrived(TZR, TZ)
        total = TZS[...]
        for k in range(NZ - 1):
            total = total + TZR[k]
        TS[0] = SCALE / total
        ITW[...] = across(TS[0])
        for k in XO:
            for p in (1, 0):
                send(TS.at[0], TS.at[2 * k + p], T1, dev(k, flip * p, 0, 0))
        send(TS.at[0], TS.at[1], T1, dev(0, flip, 0, 0))

    def hand_totals():
        arrived(TS.at[pl.ds(1, NB - 1)], T1)
        send(TS.at[pl.ds(0, NB)], TS.at[pl.ds(NB, NB)], T2, mate)

    def line_totals():
        arrived(TS.at[pl.ds(NB, NB)], T2)
        for j in range(2 * NB):
            ITB[j] = across(TS[j])

    def to_sides(p):
        send(F.at[p], F.at[2 + p], GL + p, dev(1, 0, 0, 0))
        send(F.at[p], F.at[6 + p], GR + p, dev(3, 0, 0, 0))

    def relay(p):
        arrived(F.at[2 + p], GL + p)
        arrived(F.at[6 + p], GR + p)
        send(F.at[2 + p, pl.ds(0, B)], F.at[4 + p, pl.ds(0, B)], GF + p, dev(1, 0, 0, 0))
        send(F.at[6 + p, pl.ds(B, B)], F.at[4 + p, pl.ds(B, B)], GF + p, dev(3, 0, 0, 0))

    def to_pair():
        send(F.at[0], F.at[1], GY, dev(0, flip, 0, 0))

    def second_row():
        arrived(F.at[1], GY)
        to_sides(1)
        relay(0)

    def hand(part):
        lo, count = PARTS[part]
        send(F.at[pl.ds(lo, count)], F.at[pl.ds(NB + lo, count)], GH + part, mate)

    def handed(part):
        lo, count = PARTS[part]
        arrived(F.at[pl.ds(NB + lo, count)], GH + part)
        blocks(NB + lo, NB + lo + count)

    def idle(point):
        pl.semaphore_signal(phase.at[point], inc=1, device_id=mate, device_id_type=MESH)

    def when_idle(point):
        pl.semaphore_wait(phase.at[point], 1)

    own = (x * 2 + lax.rem(y, 2)) * NC + c

    def line_block(j, carry):
        tb = F[j, :B, :].astype(jnp.bfloat16)
        sw = F[j, B:, :]
        SBT[j] = sw.T.astype(jnp.bfloat16)
        ETB[j] = jnp.exp(dot(tb, WU[own]) * INV_T)
        ESB[j] = jnp.exp(dot(sw.astype(jnp.bfloat16), WU[own]) * INV_S)
        return carry

    def blocks(lo, hi):
        lax.fori_loop(lo, hi, line_block, 0)

    last = ITERS - 1

    def weigh_blocks():
        def step(j, carry):
            for q in range(KB // 128):
                part = pl.ds(128 * q, 128)
                ESB[j, :, part] = ESB[j, :, part] * ITB[j]
                ETB[j, :, part] = ETB[j, :, part] * CF[last, pl.ds(own * (KB // 128) + q, 1), :]
            return carry

        lax.fori_loop(0, 2 * NB, step, 0, unroll=2)

    @pl.when(c == 0)
    def _():
        send(CS, CR, UP, mate)
        send(F.at[0], F.at[NB], G0, mate)
        student()
        when_idle(0)
        to_sides(0)
        student_totals()
        when_idle(1)
        to_pair()
        arrived(F.at[NB], G0)
        blocks(NB, NB + 1)
        blocks(0, 1)
        hand_totals()
        when_idle(2)
        second_row()
        student_product()
        hand(0)
        blocks(1, 3)
        line_totals()
        arrived(F.at[4], GF)
        blocks(4, 5)
        when_idle(3)
        relay(1)
        hand(1)
        blocks(3, 4)
        blocks(6, 8)
        arrived(F.at[5], GF + 1)
        hand(2)
        blocks(5, 6)
        handed(0)
        arrived(CF.at[last], DN)
        teacher_product()
        handed(1)
        handed(2)
        weigh_blocks()
        arrived(RB, RM)

    @pl.when(c == 1)
    def _():
        def mate_exp(j, carry):
            e = jnp.exp(dot(F[NB, :B, :].astype(jnp.bfloat16), WU[j]) * INV_T)
            E[2 * j, B:] = e[:, :128]
            E[2 * j + 1, B:] = e[:, 128:]
            return carry

        for i in range(ITERS):
            if i == 0:
                send(F.at[0], F.at[NB], G0, mate)
                arrived(CR, UP)
                XS[0] = CS[...] + CR[...]
            for k in XO:
                send(XS.at[i], XR.at[i, k - 1], XX + i, dev(k, 0, 0, 0))
            if i == 0:
                arrived(F.at[NB], G0)
                lax.fori_loop(0, CH, mate_exp, 0, unroll=4)
            elif i == 1:
                blocks(0, 1)
                blocks(NB, NB + 1)
                hand_totals()
            else:
                hand(0)
                blocks(1, 3)
            arrived(XR.at[i], XX + i)
            YS[i] = (XS[i] + XR[i, 0]) + (XR[i, 1] + XR[i, 2])
            for k in YO:
                send(YS.at[i], YR.at[i, k - 1], YY + i, dev(0, k, 0, 0))
            if i == 0:
                idle(0)
                to_sides(0)
                student()
            elif i == 1:
                idle(2)
                second_row()
                student_product()
            else:
                idle(3)
                relay(1)
                arrived(F.at[4], GF)
                hand(1)
            arrived(YR.at[i], YY + i)
            total = YS[i]
            for k in range(NY - 1):
                total = total + YR[i, k]
            CF[i] = 1.0 / total
            if i == last:
                send(CF.at[last], CF.at[last], DN, mate)

            def step(t, acc):
                return acc + E[t] * CF[i, pl.ds(t, 1), :]

            acc = lax.fori_loop(0, TL, step, jnp.zeros((2 * B, 128), jnp.float32), unroll=8)
            ZS[i, 0:1, :] = jnp.sum(acc[:B].T, 0, keepdims=True)
            ZS[i, 1:2, :] = jnp.sum(acc[B:].T, 0, keepdims=True)
            if i < last:
                for k in ZO:
                    send(ZS.at[i], ZRV.at[i, k - 1], ZZ + i, dev(0, 0, 0, k))
                if i == 0:
                    idle(1)
                    to_pair()
                    student_totals()
                else:
                    line_totals()
                arrived(ZRV.at[i], ZZ + i)
                total = ZS[i]
                for k in range(NZ - 1):
                    total = total + ZRV[i, k]
                inv = 1.0 / total
                RW[:B] = across(inv[0:1])
                RW[B:] = across(inv[1:2])

                def scaled(t, carry):
                    e = E[t] * RW[...]
                    XS[i + 1, pl.ds(t, 1), :] = jnp.sum(e[:B] + e[B:], 0, keepdims=True)
                    return carry

                lax.fori_loop(0, TL, scaled, 0, unroll=8)
            else:
                far = lambda k: -(min(k // (2 * NZ), NX - k // (2 * NZ)) + k // NZ % 2 + min(k % NZ, NZ - k % NZ))
                for k in sorted(range(1, NB * NZ), key=far):
                    to = dev(k // (2 * NZ), flip * (k // NZ % 2), 0, k % NZ)
                    send(ZS.at[i], ZL.at[k], ZZ + i, to)
                ZL[0] = ZS[i]
                arrived(F.at[5], GF + 1)
                hand(2)
                teacher_product()
                blocks(3, NB)
                handed(0)
                handed(1)
                handed(2)
                weigh_blocks()
                arrived(ZL.at[pl.ds(1, NB * NZ - 1)], ZZ + i)
                for j in range(NB):
                    total = ZL[j * NZ]
                    for dz in range(1, NZ):
                        total = total + ZL[j * NZ + dz]
                    inv = 1.0 / total
                    RB[j] = inv[0:1]
                    RB[NB + j] = inv[1:2]
                    RBM[j] = inv[1:2]
                    RBM[NB + j] = inv[0:1]
                send(RBM, RB, RM, mate)

    def line_grad(j, carry):
        rb = across(RB[j] * SCALE)
        for q in range(KB // 128):
            part = pl.ds(128 * q, 128)
            g = ESB[j, :, part] - ETB[j, :, part] * rb
            GB[j, :, 128 * q:128 * q + 128] = g.astype(jnp.bfloat16)
        return carry

    lax.fori_loop(0, 2 * NB, line_grad, 0, unroll=True)
    acc = jnp.zeros((D, KB), jnp.float32)
    for p in range(NB):
        lhs = jnp.concatenate([SBT[2 * p], SBT[2 * p + 1]], 1)
        acc = acc + dot(lhs, jnp.concatenate([GB[2 * p], GB[2 * p + 1]], 0))
    GPS[...] = acc.reshape(D // 4, 4, KB)

    for dy in YO + (0,):
        def scatter(i, carry):
            to = dev(i // NC, dy, lax.rem(i, NC), 0)
            send(GPS.at[to[0]], GPR.at[i // NC * (NY * NC) + dy * NC + lax.rem(i, NC)], GP, to)
            return carry

        lax.fori_loop(0 if dy else 1, NX * NC, scatter, 0)

    RW[:B] = across(RB[0] * SCALE)
    mine = pl.ds(pl.multiple_of(z * 16, 16), 16)
    u, inv = unit_rows(s_ref[mine, :])
    u = u.astype(jnp.float32)
    arrived(GAR, AR)
    arrived(GTR, TR)
    total, teach = GAS[z], GTS[z]
    for k in range(NZ - 1):
        total = total + GAR[k]
        teach = teach + GTR[k]
    total = total - teach * RW[mine, 0:1]
    GFO[0] = (total - u * jnp.sum(u * total, 1, keepdims=True)) * inv
    for k in ZO:
        send(GFO.at[0], GFO.at[k], ZA, dev(0, 0, 0, k))
    gf_out[mine, :] = GFO[0]
    arrived(GFO.at[pl.ds(1, NZ - 1)], ZA)
    for k in range(1, NZ):
        at = lax.rem(z + NZ - k, NZ) * 16
        gf_out[pl.ds(pl.multiple_of(at, 16), 16), :] = GFO[k]

    arrived(GPR.at[pl.ds(1, NX * NY * NC - 1)], GP)
    GPR[0] = GPS[dp]
    for dx in range(NX):
        for dc in range(NC):
            for p in range(2):
                total = GPR[(dx * NY + p) * NC + dc]
                for dy in range(p + 2, NY, 2):
                    total = total + GPR[(dx * NY + dy) * NC + dc]
                at = (lax.rem(x + NX - dx, NX) * 2 + lax.rem(y + p, 2)) * NC + lax.rem(c + dc, NC)
                gp_out[:, pl.ds(pl.multiple_of(at * KB, KB), KB)] = total

    @pl.when(c == 0)
    def _():
        sent(CS, UP)

    @pl.when(c == 1)
    def _():
        for i in range(ITERS):
            sent(XR.at[i], XX + i)
            sent(YR.at[i], YY + i)
            if i < last:
                sent(ZRV.at[i], ZZ + i)
        sent(ZL.at[pl.ds(1, NB * NZ - 1)], ZZ + last)
        sent(CF.at[last], DN)
        sent(RBM, RM)

    sent(TZR, TZ)
    sent(F.at[0], G0)
    sent(F.at[0], GY)
    for p in range(2):
        sent(F.at[p], GL + p)
        sent(F.at[p], GR + p)
        sent(F.at[4 + p], GF + p)
    for part, (lo, count) in enumerate(PARTS):
        sent(F.at[pl.ds(lo, count)], GH + part)
    sent(TS.at[pl.ds(1, NB - 1)], T1)
    sent(TS.at[pl.ds(0, NB)], T2)
    sent(GPR.at[pl.ds(1, NX * NY * NC - 1)], GP)
    sent(GAR, AR)
    sent(GTR, TR)
    sent(GFO.at[pl.ds(1, NZ - 1)], ZA)


def place(features, protos, features_out, protos_out, features_held, protos_held, sem):
    into = [
        pltpu.make_async_copy(features, features_held, sem.at[0]),
        pltpu.make_async_copy(protos, protos_held, sem.at[1]),
    ]
    out = [
        pltpu.make_async_copy(features_held, features_out, sem.at[2]),
        pltpu.make_async_copy(protos_held, protos_out, sem.at[3]),
    ]
    for copy in into:
        copy.start()
    for k in (1, 0):
        into[k].wait()
        out[k].start()
    for copy in out:
        copy.wait()


def shards(teacher, student, protos):
    f32, bf16 = jnp.float32, jnp.bfloat16
    vm = pltpu.VMEM
    scratch = [
        vm((B, D), bf16),
        vm((B, D), bf16),
        vm((D, K), bf16),
        vm((CH, D, 256), bf16),
        vm((TL, 2 * B, 128), f32),
        vm((TL, B, 128), f32),
        vm((2 * NB, 2 * B, D), f32),
        vm((2 * NB, B, KB), f32),
        vm((2 * NB, B, KB), f32),
        vm((2 * NB, D, B), bf16),
        vm((2 * NB, B, KB), bf16),
        vm((64, 4, KB), f32),
        vm((64, 4, KB), f32),
        vm((NZ, 16, D), f32),
        vm((NZ - 1, 16, D), f32),
        vm((NZ, 16, D), f32),
        vm((NZ - 1, 16, D), f32),
        vm((NZ, 16, D), f32),
        vm((B, D), f32),
        vm((TL, 128), f32),
        vm((TL, 128), f32),
        vm((ITERS, TL, 128), f32),
        vm((ITERS, NX - 1, TL, 128), f32),
        vm((ITERS, TL, 128), f32),
        vm((ITERS, NY - 1, TL, 128), f32),
        vm((ITERS, TL, 128), f32),
        vm((ITERS, 2, 128), f32),
        vm((ITERS - 1, NZ - 1, 2, 128), f32),
        vm((NB * NZ, 2, 128), f32),
        vm((1, 128), f32),
        vm((NZ - 1, 1, 128), f32),
        vm((2 * NB, 1, 128), f32),
        vm((2 * NB, 1, 128), f32),
        vm((2 * NB, 1, 128), f32),
        vm((2 * NB, B, 128), f32),
        vm((2 * B, 128), f32),
        vm((B, 128), f32),
        pltpu.SemaphoreType.DMA((2 + LOADS,)),
        pltpu.SemaphoreType.DMA((GROUPS,)),
        pltpu.SemaphoreType.DMA((GROUPS,)),
        pltpu.SemaphoreType.REGULAR((4,)),
    ]
    whole = pl.BlockSpec(memory_space=pltpu.VMEM)
    anywhere = pl.BlockSpec(memory_space=pl.ANY)
    grads = pl.pallas_call(
        body,
        out_shape=(jax.ShapeDtypeStruct((B, D), f32), jax.ShapeDtypeStruct((4, K), f32)),
        in_specs=[anywhere] * 3,
        out_specs=(whole, whole),
        scratch_shapes=scratch,
        compiler_params=pltpu.CompilerParams(
            collective_id=0, has_side_effects=True, vmem_limit_bytes=60 * 2**20
        ),
    )(teacher, student, protos)
    return pl.pallas_call(
        place,
        out_shape=tuple(jax.ShapeDtypeStruct(g.shape, g.dtype) for g in grads),
        in_specs=[anywhere] * 2,
        out_specs=(anywhere,) * 2,
        scratch_shapes=[vm((B, D), f32), vm((4, K), f32), pltpu.SemaphoreType.DMA((4,))],
        compiler_params=pltpu.CompilerParams(vmem_limit_bytes=60 * 2**20),
    )(*grads)


def solution(mesh):
    placed = (P("dp", None), P("dp", None), P(None, "proto"))
    return jax.shard_map(
        shards,
        mesh=mesh,
        in_specs=placed,
        out_specs=(P("dp", None), P("dp", "proto")),
        check_vma=False,
    )
```

```python
import functools

import jax
import jax.numpy as jnp
from jax import lax
from jax.experimental import pallas as pl
from jax.experimental.pallas import tpu as pltpu
from jax.sharding import PartitionSpec as P

EPS = 1e-06
INV_T = 1.0 / 0.07
INV_S = 1.0 / 0.1
ITERS = 3
NX, NY, NC, NZ = 4, 8, 2, 8
B = 128
D = 256
K = 4096
CH = K // 256
TL = K // 128
NB = 2 * NX
KB = K // (NB * NC)
SCALE = 32768 / 64.0 / 0.1
MESH = pl.DeviceIdType.MESH

UP, DN, G0, GY, NO, TZ, T1, T2, RM, GP, AR, TR, ZA = range(13)
XX, YY, ZZ = (13, 16, 19)
GL, GR, GF, GH = (22, 24, 26, 28)
GROUPS = 31
PARTS = ((1, 2), (3, 2), (5, 3))
XO = (2, 1, 3)
YO = ZO = (4, 3, 5, 2, 6, 1, 7)
LOADS = 2


def dot(a, b):
    return jnp.dot(a, b, preferred_element_type=jnp.float32)


def unit_rows(raw):
    wide = raw.astype(jnp.float32)
    inv = lax.rsqrt(jnp.sum(wide * wide, 1, keepdims=True) + EPS)
    return (wide * inv).astype(jnp.bfloat16), inv


def across(row):
    return jnp.broadcast_to(row, (128, 128)).T


def body(
    t_hbm, s_hbm, w_hbm, gf_out, gp_out,
    t_ref, s_ref, w_ref, WU, E, SE, F, ETB, ESB, SBT, GB, GPS, GPR, GAS, GAR, GTS, GTR, GFO, GFA,
    CS, CR, XS, XR, YS, YR, CF, ZS, ZRV, ZL, TZS, TZR, TS, RB, RBM, ITB, RW, ITW, lsem, ssem, rsem, phase,
):
    dp = lax.axis_index("dp")
    z = lax.axis_index("proto")
    c = lax.rem(dp, 2)
    y = lax.rem(dp // 2, NY)
    x = dp // (2 * NY)

    def dev(dx, dy, dc, dz):
        return (
            (lax.rem(x + dx, NX) * NY + lax.rem(y + dy, NY)) * NC + lax.rem(c + dc, NC),
            lax.rem(z + dz, NZ),
        )

    mate = dev(0, 0, 1, 0)
    flip = NY + 1 - 2 * lax.rem(y, 2)

    def send(src, dst, group, to):
        pltpu.make_async_remote_copy(
            src, dst, ssem.at[group], rsem.at[group], device_id=to, device_id_type=MESH
        ).start()

    def arrived(ref, group):
        pltpu.make_async_remote_copy(
            ref, ref, ssem.at[group], rsem.at[group], device_id=mate, device_id_type=MESH
        ).wait_recv()

    def sent(ref, group):
        pltpu.make_async_remote_copy(
            ref, ref, ssem.at[group], rsem.at[group], device_id=mate, device_id_type=MESH
        ).wait_send()

    offsets = [(0, k, 0, 0) for k in YO] + [(0, 0, 0, k) for k in ZO] + [(k, 0, 0, 0) for k in XO]
    offsets = sorted(offsets, key=lambda o: -(min(o[0], NX - o[0]) + min(o[1], NY - o[1]) + min(o[3], NZ - o[3])))
    peers = [dev(k, flip, 0, 0) for k in XO] + [dev(*o) for o in offsets] + [mate]
    barrier = pltpu.get_barrier_semaphore()
    for to in peers:
        pl.semaphore_signal(barrier, inc=1, device_id=to, device_id_type=MESH)

    loads = [pltpu.make_async_copy(t_hbm, t_ref, lsem.at[0])]
    for piece in range(LOADS):
        cols = pl.ds(piece * (K // LOADS), K // LOADS)
        loads.append(pltpu.make_async_copy(w_hbm.at[:, cols], w_ref.at[:, cols], lsem.at[1 + piece]))
    loads.append(pltpu.make_async_copy(s_hbm, s_ref, lsem.at[1 + LOADS]))
    for load in loads:
        load.start()

    loads[0].wait()
    t_unit, _ = unit_rows(t_ref[...])
    F[0, :B, :] = t_unit.astype(jnp.float32)

    def first(j, carry):
        w = w_ref[:, pl.ds(pl.multiple_of(j * 256, 256), 256)].astype(jnp.float32)
        w = (w * lax.rsqrt(jnp.sum(w * w, 0, keepdims=True) + EPS)).astype(jnp.bfloat16)
        WU[j] = w
        e = jnp.exp(dot(t_unit, w) * INV_T)
        E[2 * j, :B] = e[:, :128]
        E[2 * j + 1, :B] = e[:, 128:]
        CS[pl.ds(2 * j, 1), :] = jnp.sum(e[:, :128], 0, keepdims=True)
        CS[pl.ds(2 * j + 1, 1), :] = jnp.sum(e[:, 128:], 0, keepdims=True)
        return carry

    per = CH // LOADS
    for piece in range(LOADS):
        loads[1 + piece].wait()
        lax.fori_loop(piece * per, piece * per + per, first, 0, unroll=True)
    loads[1 + LOADS].wait()
    s_unit, _ = unit_rows(s_ref[...])
    F[0, B:, :] = s_unit.astype(jnp.float32)
    pl.semaphore_wait(barrier, len(peers))

    def student():
        def step(j, acc):
            e = jnp.exp(dot(F[0, B:, :].astype(jnp.bfloat16), WU[j]) * INV_S)
            SE[2 * j] = e[:, :128]
            SE[2 * j + 1] = e[:, 128:]
            return acc + e[:, :128] + e[:, 128:]

        acc = lax.fori_loop(0, CH, step, jnp.zeros((B, 128), jnp.float32), unroll=4)
        TZS[...] = jnp.sum(acc.T, 0, keepdims=True)
        for k in ZO:
            send(TZS, TZR.at[k - 1], TZ, dev(0, 0, 0, k))

    def product(tile, kept, got, group):
        def step(j, acc):
            g = jnp.concatenate([tile(2 * j), tile(2 * j + 1)], 1)
            high = g.astype(jnp.bfloat16)
            low = (g - high.astype(jnp.float32)).astype(jnp.bfloat16)
            return acc + lax.dot_general(
                jnp.concatenate([high, low], 0), WU[j], (((1,), (1,)), ((), ())), preferred_element_type=jnp.float32
            )

        acc = lax.fori_loop(0, CH, step, jnp.zeros((2 * B, D), jnp.float32), unroll=4)
        GFA[...] = acc[:B] + acc[B:]
        for k in range(NZ):
            kept[k] = GFA[16 * k:16 * k + 16, :]
        for k in ZO:
            send(kept.at[lax.rem(z + k, NZ)], got.at[k - 1], group, dev(0, 0, 0, k))

    def student_product():
        product(lambda t: SE[t] * ITW[...], GAS, GAR, AR)

    def teacher_product():
        product(lambda t: E[t, :B] * CF[ITERS - 1, pl.ds(t, 1), :], GTS, GTR, TR)

    def student_totals():
        arrived(TZR, TZ)
        total = TZS[...]
        for k in range(NZ - 1):
            total = total + TZR[k]
        TS[0] = SCALE / total
        ITW[...] = across(TS[0])
        for k in XO:
            for p in (1, 0):
                send(TS.at[0], TS.at[2 * k + p], T1, dev(k, flip * p, 0, 0))
        send(TS.at[0], TS.at[1], T1, dev(0, flip, 0, 0))

    def hand_totals():
        arrived(TS.at[pl.ds(1, NB - 1)], T1)
        send(TS.at[pl.ds(0, NB)], TS.at[pl.ds(NB, NB)], T2, mate)

    def line_totals():
        arrived(TS.at[pl.ds(NB, NB)], T2)
        for j in range(2 * NB):
            ITB[j] = across(TS[j])

    def to_sides(p):
        send(F.at[p], F.at[2 + p], GL + p, dev(1, 0, 0, 0))
        send(F.at[p], F.at[6 + p], GR + p, dev(3, 0, 0, 0))

    def relay(p):
        arrived(F.at[2 + p], GL + p)
        arrived(F.at[6 + p], GR + p)
        send(F.at[2 + p, pl.ds(0, B)], F.at[4 + p, pl.ds(0, B)], GF + p, dev(1, 0, 0, 0))
        send(F.at[6 + p, pl.ds(B, B)], F.at[4 + p, pl.ds(B, B)], GF + p, dev(3, 0, 0, 0))

    def to_pair():
        send(F.at[0], F.at[1], GY, dev(0, flip, 0, 0))

    def second_row():
        arrived(F.at[1], GY)
        to_sides(1)
        relay(0)

    def hand(part):
        lo, count = PARTS[part]
        send(F.at[pl.ds(lo, count)], F.at[pl.ds(NB + lo, count)], GH + part, mate)

    def handed(part):
        lo, count = PARTS[part]
        arrived(F.at[pl.ds(NB + lo, count)], GH + part)
        blocks(NB + lo, NB + lo + count)

    def idle(point):
        pl.semaphore_signal(phase.at[point], inc=1, device_id=mate, device_id_type=MESH)

    def when_idle(point):
        pl.semaphore_wait(phase.at[point], 1)

    own = (x * 2 + lax.rem(y, 2)) * NC + c

    def line_block(j, carry):
        tb = F[j, :B, :].astype(jnp.bfloat16)
        sw = F[j, B:, :]
        SBT[j] = sw.T.astype(jnp.bfloat16)
        ETB[j] = jnp.exp(dot(tb, WU[own]) * INV_T)
        ESB[j] = jnp.exp(dot(sw.astype(jnp.bfloat16), WU[own]) * INV_S)
        return carry

    def blocks(lo, hi):
        lax.fori_loop(lo, hi, line_block, 0)

    last = ITERS - 1

    @pl.when(c == 0)
    def _():
        send(CS, CR, UP, mate)
        send(F.at[0], F.at[NB], G0, mate)
        student()
        when_idle(0)
        to_sides(0)
        student_totals()
        when_idle(1)
        to_pair()
        arrived(F.at[NB], G0)
        blocks(NB, NB + 1)
        blocks(0, 1)
        hand_totals()
        when_idle(2)
        second_row()
        student_product()
        hand(0)
        blocks(1, 3)
        line_totals()
        arrived(F.at[4], GF)
        blocks(4, 5)
        when_idle(3)
        relay(1)
        hand(1)
        blocks(3, 4)
        blocks(6, 8)
        arrived(F.at[5], GF + 1)
        hand(2)
        blocks(5, 6)
        handed(0)
        arrived(CF.at[last], DN)
        teacher_product()
        handed(1)
        handed(2)
        arrived(RB, RM)

    @pl.when(c == 1)
    def _():
        def mate_exp(j, carry):
            e = jnp.exp(dot(F[NB, :B, :].astype(jnp.bfloat16), WU[j]) * INV_T)
            E[2 * j, B:] = e[:, :128]
            E[2 * j + 1, B:] = e[:, 128:]
            return carry

        for i in range(ITERS):
            if i == 0:
                send(F.at[0], F.at[NB], G0, mate)
                arrived(CR, UP)
                XS[0] = CS[...] + CR[...]
            for k in XO:
                send(XS.at[i], XR.at[i, k - 1], XX + i, dev(k, 0, 0, 0))
            if i == 0:
                arrived(F.at[NB], G0)
                lax.fori_loop(0, CH, mate_exp, 0, unroll=4)
            elif i == 1:
                blocks(0, 1)
                blocks(NB, NB + 1)
                hand_totals()
            else:
                hand(0)
                blocks(1, 3)
            arrived(XR.at[i], XX + i)
            YS[i] = (XS[i] + XR[i, 0]) + (XR[i, 1] + XR[i, 2])
            for k in YO:
                send(YS.at[i], YR.at[i, k - 1], YY + i, dev(0, k, 0, 0))
            if i == 0:
                idle(0)
                to_sides(0)
                student()
            elif i == 1:
                idle(2)
                second_row()
                student_product()
            else:
                idle(3)
                relay(1)
                arrived(F.at[4], GF)
                hand(1)
            arrived(YR.at[i], YY + i)
            total = YS[i]
            for k in range(NY - 1):
                total = total + YR[i, k]
            CF[i] = 1.0 / total
            if i == last:
                send(CF.at[last], CF.at[last], DN, mate)

            def step(t, acc):
                return acc + E[t] * CF[i, pl.ds(t, 1), :]

            acc = lax.fori_loop(0, TL, step, jnp.zeros((2 * B, 128), jnp.float32), unroll=8)
            ZS[i, 0:1, :] = jnp.sum(acc[:B].T, 0, keepdims=True)
            ZS[i, 1:2, :] = jnp.sum(acc[B:].T, 0, keepdims=True)
            if i < last:
                for k in ZO:
                    send(ZS.at[i], ZRV.at[i, k - 1], ZZ + i, dev(0, 0, 0, k))
                if i == 0:
                    idle(1)
                    to_pair()
                    student_totals()
                else:
                    line_totals()
                arrived(ZRV.at[i], ZZ + i)
                total = ZS[i]
                for k in range(NZ - 1):
                    total = total + ZRV[i, k]
                inv = 1.0 / total
                RW[:B] = across(inv[0:1])
                RW[B:] = across(inv[1:2])

                def scaled(t, carry):
                    e = E[t] * RW[...]
                    XS[i + 1, pl.ds(t, 1), :] = jnp.sum(e[:B] + e[B:], 0, keepdims=True)
                    return carry

                lax.fori_loop(0, TL, scaled, 0, unroll=8)
            else:
                far = lambda k: -(min(k // (2 * NZ), NX - k // (2 * NZ)) + k // NZ % 2 + min(k % NZ, NZ - k % NZ))
                for k in sorted(range(1, NB * NZ), key=far):
                    to = dev(k // (2 * NZ), flip * (k // NZ % 2), 0, k % NZ)
                    send(ZS.at[i], ZL.at[k], ZZ + i, to)
                ZL[0] = ZS[i]
                arrived(F.at[5], GF + 1)
                hand(2)
                teacher_product()
                blocks(3, NB)
                handed(0)
                handed(1)
                handed(2)
                arrived(ZL.at[pl.ds(1, NB * NZ - 1)], ZZ + i)
                for j in range(NB):
                    total = ZL[j * NZ]
                    for dz in range(1, NZ):
                        total = total + ZL[j * NZ + dz]
                    inv = 1.0 / total
                    RB[j] = inv[0:1]
                    RB[NB + j] = inv[1:2]
                    RBM[j] = inv[1:2]
                    RBM[NB + j] = inv[0:1]
                send(RBM, RB, RM, mate)

    def line_grad(j, carry):
        rb = across(RB[j] * SCALE)
        for q in range(KB // 128):
            part = pl.ds(128 * q, 128)
            col = CF[last, pl.ds(own * (KB // 128) + q, 1), :]
            g = ESB[j, :, part] * ITB[j] - (ETB[j, :, part] * col) * rb
            GB[j, :, 128 * q:128 * q + 128] = g.astype(jnp.bfloat16)
        return carry

    lax.fori_loop(0, 2 * NB, line_grad, 0, unroll=True)
    acc = jnp.zeros((D, KB), jnp.float32)
    for p in range(NB):
        lhs = jnp.concatenate([SBT[2 * p], SBT[2 * p + 1]], 1)
        acc = acc + dot(lhs, jnp.concatenate([GB[2 * p], GB[2 * p + 1]], 0))
    GPS[...] = acc.reshape(D // 4, 4, KB)

    for dy in YO + (0,):
        def scatter(i, carry):
            to = dev(i // NC, dy, lax.rem(i, NC), 0)
            send(GPS.at[to[0]], GPR.at[i // NC * (NY * NC) + dy * NC + lax.rem(i, NC)], GP, to)
            return carry

        lax.fori_loop(0 if dy else 1, NX * NC, scatter, 0)

    RW[:B] = across(RB[0] * SCALE)
    mine = pl.ds(pl.multiple_of(z * 16, 16), 16)
    u, inv = unit_rows(s_ref[mine, :])
    u = u.astype(jnp.float32)
    arrived(GAR, AR)
    arrived(GTR, TR)
    total, teach = GAS[z], GTS[z]
    for k in range(NZ - 1):
        total = total + GAR[k]
        teach = teach + GTR[k]
    total = total - teach * RW[mine, 0:1]
    GFO[0] = (total - u * jnp.sum(u * total, 1, keepdims=True)) * inv
    for k in ZO:
        send(GFO.at[0], GFO.at[k], ZA, dev(0, 0, 0, k))
    gf_out[mine, :] = GFO[0]
    arrived(GFO.at[pl.ds(1, NZ - 1)], ZA)
    for k in range(1, NZ):
        at = lax.rem(z + NZ - k, NZ) * 16
        gf_out[pl.ds(pl.multiple_of(at, 16), 16), :] = GFO[k]

    arrived(GPR.at[pl.ds(1, NX * NY * NC - 1)], GP)
    GPR[0] = GPS[dp]
    for dx in range(NX):
        for dc in range(NC):
            for p in range(2):
                total = GPR[(dx * NY + p) * NC + dc]
                for dy in range(p + 2, NY, 2):
                    total = total + GPR[(dx * NY + dy) * NC + dc]
                at = (lax.rem(x + NX - dx, NX) * 2 + lax.rem(y + p, 2)) * NC + lax.rem(c + dc, NC)
                gp_out[:, pl.ds(pl.multiple_of(at * KB, KB), KB)] = total

    @pl.when(c == 0)
    def _():
        sent(CS, UP)

    @pl.when(c == 1)
    def _():
        for i in range(ITERS):
            sent(XR.at[i], XX + i)
            sent(YR.at[i], YY + i)
            if i < last:
                sent(ZRV.at[i], ZZ + i)
        sent(ZL.at[pl.ds(1, NB * NZ - 1)], ZZ + last)
        sent(CF.at[last], DN)
        sent(RBM, RM)

    sent(TZR, TZ)
    sent(F.at[0], G0)
    sent(F.at[0], GY)
    for p in range(2):
        sent(F.at[p], GL + p)
        sent(F.at[p], GR + p)
        sent(F.at[4 + p], GF + p)
    for part, (lo, count) in enumerate(PARTS):
        sent(F.at[pl.ds(lo, count)], GH + part)
    sent(TS.at[pl.ds(1, NB - 1)], T1)
    sent(TS.at[pl.ds(0, NB)], T2)
    sent(GPR.at[pl.ds(1, NX * NY * NC - 1)], GP)
    sent(GAR, AR)
    sent(GTR, TR)
    sent(GFO.at[pl.ds(1, NZ - 1)], ZA)


def place(features, protos, features_out, protos_out):
    features_out[...] = features[...]
    protos_out[...] = protos[...]


def shards(teacher, student, protos):
    f32, bf16 = jnp.float32, jnp.bfloat16
    vm = pltpu.VMEM
    scratch = [
        vm((B, D), bf16),
        vm((B, D), bf16),
        vm((D, K), bf16),
        vm((CH, D, 256), bf16),
        vm((TL, 2 * B, 128), f32),
        vm((TL, B, 128), f32),
        vm((2 * NB, 2 * B, D), f32),
        vm((2 * NB, B, KB), f32),
        vm((2 * NB, B, KB), f32),
        vm((2 * NB, D, B), bf16),
        vm((2 * NB, B, KB), bf16),
        vm((64, 4, KB), f32),
        vm((64, 4, KB), f32),
        vm((NZ, 16, D), f32),
        vm((NZ - 1, 16, D), f32),
        vm((NZ, 16, D), f32),
        vm((NZ - 1, 16, D), f32),
        vm((NZ, 16, D), f32),
        vm((B, D), f32),
        vm((TL, 128), f32),
        vm((TL, 128), f32),
        vm((ITERS, TL, 128), f32),
        vm((ITERS, NX - 1, TL, 128), f32),
        vm((ITERS, TL, 128), f32),
        vm((ITERS, NY - 1, TL, 128), f32),
        vm((ITERS, TL, 128), f32),
        vm((ITERS, 2, 128), f32),
        vm((ITERS - 1, NZ - 1, 2, 128), f32),
        vm((NB * NZ, 2, 128), f32),
        vm((1, 128), f32),
        vm((NZ - 1, 1, 128), f32),
        vm((2 * NB, 1, 128), f32),
        vm((2 * NB, 1, 128), f32),
        vm((2 * NB, 1, 128), f32),
        vm((2 * NB, B, 128), f32),
        vm((2 * B, 128), f32),
        vm((B, 128), f32),
        pltpu.SemaphoreType.DMA((2 + LOADS,)),
        pltpu.SemaphoreType.DMA((GROUPS,)),
        pltpu.SemaphoreType.DMA((GROUPS,)),
        pltpu.SemaphoreType.REGULAR((4,)),
    ]
    whole = pl.BlockSpec(memory_space=pltpu.VMEM)
    anywhere = pl.BlockSpec(memory_space=pl.ANY)
    grads = pl.pallas_call(
        body,
        out_shape=(jax.ShapeDtypeStruct((B, D), f32), jax.ShapeDtypeStruct((4, K), f32)),
        in_specs=[anywhere] * 3,
        out_specs=(whole, whole),
        scratch_shapes=scratch,
        compiler_params=pltpu.CompilerParams(
            collective_id=0, has_side_effects=True, vmem_limit_bytes=60 * 2**20
        ),
    )(teacher, student, protos)
    return pl.pallas_call(
        place,
        out_shape=tuple(jax.ShapeDtypeStruct(g.shape, g.dtype) for g in grads),
        in_specs=[whole] * 2,
        out_specs=(whole,) * 2,
        compiler_params=pltpu.CompilerParams(vmem_limit_bytes=60 * 2**20),
    )(*grads)


def solution(mesh):
    placed = (P("dp", None), P("dp", None), P(None, "proto"))
    return jax.shard_map(
        shards,
        mesh=mesh,
        in_specs=placed,
        out_specs=(P("dp", None), P("dp", "proto")),
        check_vma=False,
    )
```
